32 devices in a mesh: dp: 4 (over x, core), seq: 8 (over z, y).
Axes of the slice: x: 2, y: 2, z: 4, core: 2. Of those that a mesh axis runs over, the one named last changes fastest.
Arguments:
- tokens: bfloat16 [4, 2048, 1024], P('dp', 'seq'), may hold values from -6 to 6
- target: bfloat16 [4, 2048, 1024], P('dp', 'seq'), may hold values from -6 to 6
- valid: int32 [4, 2048], P('dp', 'seq'), may hold values from 0 to 1
- in_weight: bfloat16 [1024, 4608], P('seq'), may hold values from -0.1875 to 0.1875
- small_weight: bfloat16 [1024, 12], P('seq'), may hold values from -0.1875 to 0.1875
- out_weight: bfloat16 [1024, 1536], P('seq'), may hold values from -0.15625 to 0.15625
- ffn_in: bfloat16 [1024, 5632], P('seq'), may hold values from -0.1875 to 0.1875
- ffn_out: bfloat16 [1024, 2816], P('seq'), may hold values from -0.109375 to 0.109375
- gain_first: float32 [1024], replicated, may hold values from 0.5 to 1.5
- gain_second: float32 [1024], replicated, may hold values from 0.5 to 1.5
- gain_out: float32 [256], replicated, may hold values from 0.5 to 1.5
- conv_weight: float32 [4, 3072], replicated, may hold values from -2.5 to 2.5
- decay_log: float32 [6], replicated, may hold values from -10 to -2.5
- decay_bias: float32 [6], replicated, may hold values from -1 to 1
Outputs:
- block_out: bfloat16 [4, 2048, 1024], P('dp', 'seq')
- loss_value: float32 [], replicated
- grad_tokens: float32 [4, 2048, 1024], P('dp', 'seq')
- grad_in_weight: float32 [1024, 4608], P('seq')
- grad_small_weight: float32 [1024, 12], P('seq')
- grad_out_weight: float32 [1024, 1536], P('seq')
- grad_ffn_in: float32 [1024, 5632], P('seq')
- grad_ffn_out: float32 [1024, 2816], P('seq')
- grad_gain_first: float32 [1024], replicated
- grad_gain_second: float32 [1024], replicated
- grad_gain_out: float32 [256], replicated
- grad_conv_weight: float32 [4, 3072], replicated
- grad_decay_log: float32 [6], replicated
- grad_decay_bias: float32 [6], replicated
The draws below stay inside these ranges and needn't reach their ends.
All inputs are finite; a program needn't handle non-finite values.
Results may differ from the reference program's by a relative error of at most 0.019.
The reference program's roundings to bfloat16 on the way (of `normed`, `mixed_in`, `branch`, `second` and `active`) count: a program that leaves them out, or rounds other values in their place, can miss the bound.
Values may be sent and summed in bfloat16 or wider, within the bound.
A program may use at most 256 MiB of HBM per device.

```python
import jax
import jax.numpy as jnp
from jax import lax

D = 1024
HEADS = 6
DK = 128
DV = 256
FF = 2816
CONV = 4
BLOCK = 64
KEYS = 768
VALUES = 1536
SEQ_LEN = 2048
SEQS = 4
TOKENS = 8192


def draw_valid(key, part):
    key = jax.random.fold_in(key, 3)
    position = lax.broadcasted_iota(jnp.int32, (SEQS, SEQ_LEN), 1)
    sequence = lax.broadcasted_iota(jnp.int32, (SEQS, SEQ_LEN), 0)
    limit = 100 + 500 * sequence // max(SEQS - 1, 1) + 300 * position // SEQ_LEN
    sample = jax.random.randint(key, (SEQS, SEQ_LEN), 0, 1000)
    return (sample < limit).astype(jnp.int32)


def draw_decay_log(key, part):
    key = jax.random.fold_in(key, 5)
    return jax.random.uniform(key, (HEADS,), jnp.float32, -10.0, -2.5)


def shard_levels(own_key, shape, cuts, least, top_value):
    def one(dim, parts):
        steps = jax.random.uniform(jax.random.fold_in(jax.random.fold_in(own_key, 6), dim), (parts,), jnp.float32, least / len(cuts), top_value / len(cuts))
        return jnp.repeat(jnp.exp(steps), shape[dim] // parts).reshape((-1,) + (1,) * (len(shape) - dim - 1))

    gain = one(*cuts[0])
    for cut in cuts[1:]:
        gain = gain * one(*cut)
    return gain


def noise(stream_key, extent, deviation, reach, shards=(), kind=jnp.bfloat16):
    factor_of = shard_levels(stream_key, extent, shards, -0.22, 0.18) if shards else 1.0
    drawn = jax.random.normal(stream_key, extent, jnp.float32) * deviation * factor_of
    return jnp.minimum(jnp.maximum(drawn, -reach), reach).astype(kind)


def setup_inputs(seed: int = 0) -> dict:
    key_list = jax.random.split(jax.random.key(seed), 15)
    tokens = noise(key_list[0], (SEQS, SEQ_LEN, D), 1.0, 6.0, ((0, 4), (1, 8)))
    target = noise(key_list[1], (SEQS, SEQ_LEN, D), 1.0, 6.0, ((0, 4), (1, 8)))
    valid = draw_valid(jax.random.fold_in(key_list[14], 71), 0)
    in_weight = noise(key_list[3], (D, 2 * KEYS + 2 * VALUES), D ** -0.5, 0.1875, ((0, 8),))
    small_weight = noise(key_list[4], (D, 2 * HEADS), D ** -0.5, 0.1875, ((0, 8),))
    out_weight = noise(key_list[5], (D, VALUES), VALUES ** -0.5, 0.15625, ((0, 8),))
    ffn_in = noise(key_list[6], (D, 2 * FF), D ** -0.5, 0.1875, ((0, 8),))
    ffn_out = noise(key_list[7], (D, FF), FF ** -0.5, 0.109375, ((0, 8),))
    gain_first = jnp.clip(1.0 + 0.1 * jax.random.normal(key_list[8], (D,), jnp.float32), 0.5, 1.5)
    gain_second = jnp.clip(1.0 + 0.1 * jax.random.normal(key_list[9], (D,), jnp.float32), 0.5, 1.5)
    gain_out = jnp.clip(1.0 + 0.1 * jax.random.normal(key_list[10], (DV,), jnp.float32), 0.5, 1.5)
    conv_weight = noise(key_list[11], (CONV, 2 * KEYS + VALUES), 0.5, 2.5, (), jnp.float32)
    decay_log = draw_decay_log(jax.random.fold_in(key_list[14], 71), 0)
    decay_bias = jnp.clip(jax.random.uniform(key_list[13], (HEADS,), jnp.float32, -1.0, 1.0), -1.0, 1.0)
    return dict(tokens=tokens, target=target, valid=valid, in_weight=in_weight, small_weight=small_weight, out_weight=out_weight, ffn_in=ffn_in, ffn_out=ffn_out, gain_first=gain_first, gain_second=gain_second, gain_out=gain_out, conv_weight=conv_weight, decay_log=decay_log, decay_bias=decay_bias)


precise = lax.Precision.HIGHEST
epsilon = 1e-06

@jax.custom_vjp
def low(v):
    return lax.optimization_barrier(v.astype(jnp.bfloat16)).astype(jnp.float32)

@jax.custom_vjp
def low_back(v):
    return v

def low_keep(v):
    return (low(v), None)

def low_pass(kept, grad):
    return (grad,)

def back_keep(v):
    return (v, None)

def back_low(kept, grad):
    return (low(grad),)
low.defvjp(low_keep, low_pass)
low_back.defvjp(back_keep, back_low)

def rms_scale(field_in, gain_vec):
    return field_in * lax.rsqrt(lax.optimization_barrier(jnp.mean(field_in * field_in, axis=-1, keepdims=True)) + epsilon) * gain_vec

def unit_rows(field_in):
    return field_in * lax.rsqrt(lax.optimization_barrier(jnp.sum(field_in * field_in, axis=-1, keepdims=True)) + epsilon)

def block_frame(key_rows, strength, forget):
    block_size = forget.shape[1]
    cumulative = jnp.cumsum(forget, axis=1)
    row_ids = lax.broadcasted_iota(jnp.int32, (block_size, block_size), 0)
    col_ids = lax.broadcasted_iota(jnp.int32, (block_size, block_size), 1)
    lower_mask = (row_ids >= col_ids).astype(jnp.float32)
    strict = (row_ids > col_ids).astype(jnp.float32)
    decays = jnp.exp((cumulative[:, :, None] - cumulative[:, None, :]) * lower_mask) * lower_mask
    keys_dot = jnp.einsum('hid,hjd->hij', key_rows, key_rows, precision=precise)
    system = jnp.eye(block_size, dtype=keys_dot.dtype) + strength[:, :, None] * keys_dot * decays * strict
    return (cumulative, decays, system)

def block_step(memory, pieces):
    queries, key_rows, values, strength, forget = pieces
    cumulative, decays, system = block_frame(key_rows, strength, forget)
    growth = jnp.exp(cumulative)
    projected = jnp.einsum('hcd,hdv->hcv', key_rows, memory, precision=precise)
    wanted = strength[:, :, None] * (values - growth[:, :, None] * projected)
    update = jax.scipy.linalg.solve_triangular(system, wanted, lower=True, unit_diagonal=True)
    scores = jnp.einsum('hid,hjd->hij', queries, key_rows, precision=precise) * decays
    read_out = jnp.einsum('hcd,hdv->hcv', queries, memory, precision=precise)
    output = growth[:, :, None] * read_out + jnp.einsum('hij,hjv->hiv', scores, update, precision=precise)
    final_log = cumulative[:, -1]
    weights = jnp.exp(final_log[:, None] - cumulative)
    new_memory = jnp.exp(final_log)[:, None, None] * memory + jnp.einsum('hcd,hcv->hdv', key_rows * weights[:, :, None], update, precision=precise)
    return (new_memory, output)

def to_blocks(field_in):
    blocks = field_in.shape[0] // BLOCK
    return jnp.swapaxes(field_in.reshape((blocks, BLOCK) + field_in.shape[1:]), 1, 2)

def run_blocks(entering, queries, key_rows, values, strength, forget):
    length = queries.shape[0]
    pieces = (to_blocks(queries), to_blocks(key_rows), to_blocks(values), to_blocks(strength), to_blocks(forget))
    leaving, outputs = lax.scan(jax.checkpoint(block_step), entering, pieces)
    return (jnp.swapaxes(outputs, 1, 2).reshape(length, HEADS, DV), leaving)

def prepare(padded, little, conv_weight, decay_log, decay_bias):
    length = padded.shape[0] - (CONV - 1)
    convolved = conv_weight[0] * padded[0:length]
    for offset in range(1, CONV):
        convolved = convolved + conv_weight[offset] * padded[offset:offset + length]
    active = jax.nn.silu(convolved)
    queries = unit_rows(active[:, :KEYS].reshape(length, HEADS, DK)) * DK ** (-0.5)
    key_rows = unit_rows(active[:, KEYS:2 * KEYS].reshape(length, HEADS, DK))
    values = active[:, 2 * KEYS:].reshape(length, HEADS, DV)
    strength = jax.nn.sigmoid(little[:, :HEADS])
    forget = -jnp.exp(decay_log) * jax.nn.softplus(little[:, HEADS:] + decay_bias)
    return (queries, key_rows, values, strength, forget)

def gated_norm(mixed_out, gate_pre, gain_out):
    length = mixed_out.shape[0]
    return (rms_scale(mixed_out, gain_out) * jax.nn.silu(gate_pre.reshape(length, HEADS, DV))).reshape(length, VALUES)

def swiglu(gate_up):
    return jax.nn.silu(gate_up[:, :FF]) * gate_up[:, FF:]

def per_sequence(params, inputs, wanted, mask_row):
    in_weight, small_weight, out_weight, ffn_in, ffn_out, gain_first, gain_second, gain_out, conv_weight, decay_log, decay_bias = params
    length = inputs.shape[0]
    normed = low(rms_scale(inputs, gain_first))
    project = low_back(jnp.dot(normed, in_weight, precision=precise))
    little = low_back(jnp.dot(normed, small_weight, precision=precise))
    mixed_in = low(project[:, :2 * KEYS + VALUES])
    gate_pre = project[:, 2 * KEYS + VALUES:]
    padded = jnp.concatenate([jnp.zeros((CONV - 1, 2 * KEYS + VALUES), mixed_in.dtype), mixed_in], axis=0)
    queries, key_rows, values, strength, forget = prepare(padded, little, conv_weight, decay_log, decay_bias)
    entering = jnp.zeros((HEADS, DK, DV), mixed_in.dtype)
    mixed_out, leaving = run_blocks(entering, queries, key_rows, values, strength, forget)
    branch = low(gated_norm(mixed_out, gate_pre, gain_out))
    attended = low_back(jnp.dot(branch, out_weight.T, precision=precise))
    hidden = inputs + attended
    second = low(rms_scale(hidden, gain_second))
    gate_up = low_back(jnp.dot(second, ffn_in, precision=precise))
    active = low(swiglu(gate_up))
    feed_out = low_back(jnp.dot(active, ffn_out.T, precision=precise))
    summed = hidden + feed_out
    errors = summed - wanted
    partial_value = jnp.sum(mask_row * lax.optimization_barrier(jnp.mean(errors * errors, axis=-1)))
    return (summed, partial_value)

def reference(tokens, target, valid, in_weight, small_weight, out_weight, ffn_in, ffn_out, gain_first, gain_second, gain_out, conv_weight, decay_log, decay_bias):
    floats = (in_weight.astype(jnp.float32), small_weight.astype(jnp.float32), out_weight.astype(jnp.float32), ffn_in.astype(jnp.float32), ffn_out.astype(jnp.float32), gain_first, gain_second, gain_out, conv_weight, decay_log, decay_bias)
    inputs = tokens.astype(jnp.float32)
    wanted = target.astype(jnp.float32)
    mask_rows = valid.astype(jnp.float32)
    valid_count = jnp.maximum(jnp.sum(mask_rows), 1.0)

    def forward(params, inputs_all):

        def single(triple):
            return jax.checkpoint(per_sequence)(params, triple[0], triple[1], triple[2])
        summed, partials = lax.map(single, (inputs_all, wanted, mask_rows))
        return (summed, jnp.sum(partials) / valid_count)
    (summed, loss_value), pullback = jax.vjp(forward, floats, inputs)
    gradients, grad_tokens = pullback((jnp.zeros_like(summed), jnp.ones_like(loss_value) * (TOKENS * D / 2)))
    return (summed.astype(jnp.bfloat16), loss_value, grad_tokens, gradients[0], gradients[1], gradients[2], gradients[3], gradients[4], gradients[5], gradients[6], gradients[7], gradients[8], gradients[9], gradients[10])
```

```python
import functools

import jax
import jax.numpy as jnp
from jax import lax
from jax.experimental import pallas as pl
from jax.experimental.pallas import tpu as pltpu
from jax.sharding import PartitionSpec as P

HEADS = 6
DK = 128
DV = 256
FF = 2816
CONV = 4
BLOCK = 64
KEYS = 768
VALUES = 1536


precise = lax.Precision.HIGHEST
epsilon = 1e-06


def shifted(value, axis, steps):
    count = lax.axis_size(axis)
    leading, last = (max(0, -steps), min(count, count - steps))
    return lax.ppermute(value, axis, [(source, source + steps) for source in range(leading, last)])


def rms_scale(field_in, gain_vec):
    return (
        field_in
        * lax.rsqrt(jnp.mean(field_in * field_in, axis=-1, keepdims=True) + epsilon)
        * gain_vec
    )


def unit_rows(field_in):
    return field_in * lax.rsqrt(jnp.sum(field_in * field_in, axis=-1, keepdims=True) + epsilon)


def prepare(padded, little, conv_weight, decay_log, decay_bias):
    length = padded.shape[0] - (CONV - 1)
    convolved = conv_weight[0] * padded[0:length]
    for offset in range(1, CONV):
        convolved = convolved + conv_weight[offset] * padded[offset : offset + length]
    active = jax.nn.silu(convolved)
    queries = unit_rows(active[:, :KEYS].reshape(length, HEADS, DK)) * DK ** (-0.5)
    key_rows = unit_rows(active[:, KEYS : 2 * KEYS].reshape(length, HEADS, DK))
    values = active[:, 2 * KEYS :].reshape(length, HEADS, DV)
    strength = jax.nn.sigmoid(little[:, :HEADS])
    forget = -jnp.exp(decay_log) * jax.nn.softplus(little[:, HEADS:] + decay_bias)
    return (queries, key_rows, values, strength, forget)


def gated_norm(mixed_out, gate_pre, gain_out):
    length = mixed_out.shape[0]
    return (
        rms_scale(mixed_out, gain_out) * jax.nn.silu(gate_pre.reshape(length, HEADS, DV))
    ).reshape(length, VALUES)


def swiglu(gate_up):
    return jax.nn.silu(gate_up[:, :FF]) * gate_up[:, FF:]


MESH = pl.DeviceIdType.MESH
NN = (((1,), (0,)), ((), ()))
NT = (((1,), (1,)), ((), ()))
TN = (((0,), (0,)), ((), ()))


def exact(left, right, dims=NN):
    return lax.dot_general(
        left, right, dims, precision=precise, preferred_element_type=jnp.float32
    )


def iotas(rows, columns):
    return (
        lax.broadcasted_iota(jnp.int32, (rows, columns), 0),
        lax.broadcasted_iota(jnp.int32, (rows, columns), 1),
    )


def lower_inverse(system):
    size = system.shape[0]
    row, col = iotas(size, size)
    inverse = (row == col).astype(jnp.float32) - jnp.where(row // 2 == col // 2, system, 0.0)
    width = 2
    while width < size:
        joined = (row // (2 * width) == col // (2 * width)) & (row // width != col // width)
        inverse = inverse - exact(inverse, exact(jnp.where(joined, system, 0.0), inverse))
        width *= 2
    return inverse


def decay_table(gcol, grow):
    size = gcol.shape[0]
    row, col = iotas(size, size)
    keep = row >= col
    return jnp.where(keep, jnp.exp(jnp.where(keep, gcol - grow, 0.0)), 0.0)


def local_kernel(q_ref, k_ref, v_ref, cols_ref, rows_ref, t_ref, u_ref, w_ref, m_ref, b_ref, o_ref, e_ref):
    queries, keys, values = q_ref[0], k_ref[0], v_ref[0]
    cols = cols_ref[0, 0]
    gcol, beta = cols[:, 0:1], cols[:, 1:2]
    grow = rows_ref[0, 0][0:1, :]
    size = keys.shape[0]
    half = size // 2
    decays = decay_table(gcol, grow)
    row, col = iotas(size, size)
    system = jnp.where(row > col, beta * exact(keys, keys, NT) * decays, 0.0)
    first = lower_inverse(system[:half, :half])
    second = lower_inverse(system[half:, half:])
    corner = -exact(second, exact(system[half:, :half], first))
    t_ref[0, 0, :half, :half] = first
    t_ref[0, 0, :half, half:] = jnp.zeros((half, half), jnp.float32)
    t_ref[0, 0, half:, :half] = corner
    t_ref[0, 0, half:, half:] = second
    solve = t_ref[0, 0]
    growth = jnp.exp(gcol)
    last = gcol[size - 1 :, :]
    weights = jnp.exp(last - gcol)
    update = exact(solve, beta * values)
    back = exact(solve, (beta * growth) * keys)
    scores = exact(queries, keys, NT) * decays
    weighted = keys * weights
    drow, dcol = iotas(DK, DK)
    u_ref[0, 0] = update
    w_ref[0, 0] = back
    m_ref[0, 0] = jnp.where(drow == dcol, jnp.exp(last), 0.0) - exact(weighted, back, TN)
    b_ref[0, 0] = exact(weighted, update, TN)
    o_ref[0, 0] = exact(scores, update)
    e_ref[0, 0] = growth * queries - exact(scores, back)


def per_unit(*shape):
    return pl.BlockSpec((1, 1) + shape, lambda j, h: (j, h) + (0,) * len(shape))


def per_head(length, width):
    return pl.BlockSpec((1, length, width), lambda j, h: (j, 0, h))


def delta_local(queries, keys, values, cols, rows):
    seqs, length = queries.shape[:2]
    heads = cols.shape[1]

    def out(*shape):
        return jax.ShapeDtypeStruct((seqs, heads) + shape, jnp.float32)

    return pl.pallas_call(
        local_kernel,
        grid=(seqs, heads),
        in_specs=[
            per_head(length, DK),
            per_head(length, DK),
            per_head(length, DV),
            per_unit(length, 8),
            per_unit(8, length),
        ],
        out_specs=[
            per_unit(length, length),
            per_unit(length, DV),
            per_unit(length, DK),
            per_unit(DK, DK),
            per_unit(DK, DV),
            per_unit(length, DV),
            per_unit(length, DK),
        ],
        out_shape=[
            out(length, length),
            out(length, DV),
            out(length, DK),
            out(DK, DK),
            out(DK, DV),
            out(length, DV),
            out(length, DK),
        ],
        compiler_params=pltpu.CompilerParams(vmem_limit_bytes=48 * 2**20),
        name="delta_local",
    )(queries, keys, values, cols, rows)


def grads_kernel(
    q_ref, k_ref, v_ref, cols_ref, rows_ref, t_ref, u_ref, w_ref, s_ref, do_ref, ds_ref,
    dq_ref, dk_ref, dv_ref, dcols_ref, drows_ref,
):
    queries, keys, values = q_ref[0], k_ref[0], v_ref[0]
    cols = cols_ref[0, 0]
    gcol, beta = cols[:, 0:1], cols[:, 1:2]
    grow = rows_ref[0, 0][0:1, :]
    size = keys.shape[0]
    decays = decay_table(gcol, grow)
    row, col = iotas(size, size)
    strict = row > col
    memory, after = s_ref[0, 0], ds_ref[0, 0]
    grad_out = do_ref[0]
    growth = jnp.exp(gcol)
    last = gcol[size - 1 :, :]
    weights = jnp.exp(last - gcol)
    update = u_ref[0, 0] - exact(w_ref[0, 0], memory)
    scores = exact(queries, keys, NT) * decays
    keys_dot = jnp.where(strict, exact(keys, keys, NT) * decays, 0.0)
    grad_update = exact(scores, grad_out, TN) + exact(keys * weights, after)
    grad_wanted = exact(t_ref[0, 0], grad_update, TN)
    grad_system = -exact(grad_wanted, update, NT)
    grad_scores = exact(grad_out, update, NT)
    through = keys_dot * grad_system
    total = grad_scores * scores + beta * through
    query_part = growth * exact(grad_out, memory, NT)
    key_read = growth * exact(grad_wanted, memory, NT)
    key_part = beta * key_read
    end_part = weights * exact(update, after, NT)
    grad_dot = grad_scores * decays
    grad_keys_dot = jnp.where(strict, grad_system * decays, 0.0) * beta
    dq_ref[0] = query_part + exact(grad_dot, keys)
    dk_ref[0] = (
        end_part - key_part + exact(grad_dot, queries, TN)
        + exact(grad_keys_dot, keys) + exact(grad_keys_dot, keys, TN)
    )
    dv_ref[0] = beta * grad_wanted
    key_line = jnp.sum(keys * key_part, axis=1, keepdims=True)
    end_line = jnp.sum(keys * end_part, axis=1, keepdims=True)
    grad_beta = (
        jnp.sum(grad_wanted * values, axis=1, keepdims=True)
        - jnp.sum(keys * key_read, axis=1, keepdims=True)
        + jnp.sum(through, axis=1, keepdims=True)
    )
    grad_log = (
        jnp.sum(queries * query_part, axis=1, keepdims=True)
        - key_line
        - end_line
        + jnp.sum(total, axis=1, keepdims=True)
    )
    grad_last = jnp.sum(end_line) + jnp.sum(jnp.exp(last) * jnp.sum(memory * after, axis=1, keepdims=True))
    line = lax.broadcasted_iota(jnp.int32, (size, 1), 0)
    grad_log = grad_log + jnp.where(line == size - 1, grad_last, 0.0)
    lane = lax.broadcasted_iota(jnp.int32, (size, 8), 1)
    dcols_ref[0, 0] = jnp.where(lane == 0, grad_log, jnp.where(lane == 1, grad_beta, 0.0))
    drows_ref[0, 0] = jnp.broadcast_to(jnp.sum(total, axis=0, keepdims=True), (8, size))


def delta_grads(queries, keys, values, cols, rows, solve, update, back, entering, grad_out, after):
    seqs, length = queries.shape[:2]
    heads = cols.shape[1]
    return pl.pallas_call(
        grads_kernel,
        grid=(seqs, heads),
        in_specs=[
            per_head(length, DK),
            per_head(length, DK),
            per_head(length, DV),
            per_unit(length, 8),
            per_unit(8, length),
            per_unit(length, length),
            per_unit(length, DV),
            per_unit(length, DK),
            per_unit(DK, DV),
            per_head(length, DV),
            per_unit(DK, DV),
        ],
        out_specs=[
            per_head(length, DK),
            per_head(length, DK),
            per_head(length, DV),
            per_unit(length, 8),
            per_unit(8, length),
        ],
        out_shape=[
            jax.ShapeDtypeStruct(queries.shape, jnp.float32),
            jax.ShapeDtypeStruct(keys.shape, jnp.float32),
            jax.ShapeDtypeStruct(values.shape, jnp.float32),
            jax.ShapeDtypeStruct(cols.shape, jnp.float32),
            jax.ShapeDtypeStruct(rows.shape, jnp.float32),
        ],
        compiler_params=pltpu.CompilerParams(vmem_limit_bytes=48 * 2**20),
        name="delta_grads",
    )(queries, keys, values, cols, rows, solve, update, back, entering, grad_out, after)


def relay_kernel(count, ahead, m_ref, b_ref, s_ref, sending, arriving, send_sem, recv_sem):
    place, group = lax.axis_index("seq"), lax.axis_index("dp")
    units = m_ref.shape[0]
    if ahead:
        is_first, is_last = place == 0, place == count - 1
        before, beyond = lax.rem(place + count - 1, count), lax.rem(place + 1, count)
    else:
        is_first, is_last = place == count - 1, place == 0
        before, beyond = lax.rem(place + 1, count), lax.rem(place + count - 1, count)
    barrier = pltpu.get_barrier_semaphore()

    @pl.when(jnp.logical_not(is_first))
    def _():
        pl.semaphore_signal(barrier, inc=1, device_id=(group, before), device_id_type=MESH)

    @pl.when(jnp.logical_not(is_last))
    def _():
        pl.semaphore_wait(barrier, 1)

    def copy_of(unit):
        return pltpu.make_async_remote_copy(
            src_ref=sending.at[unit],
            dst_ref=arriving.at[unit],
            send_sem=send_sem.at[unit],
            recv_sem=recv_sem.at[unit],
            device_id=(group, beyond),
            device_id_type=MESH,
        )

    for unit in range(units):

        @pl.when(is_first)
        def _():
            s_ref[unit] = jnp.zeros_like(s_ref[unit])

        @pl.when(jnp.logical_not(is_first))
        def _():
            copy_of(unit).wait_recv()
            s_ref[unit] = arriving[unit].astype(jnp.float32)

        @pl.when(jnp.logical_not(is_last))
        def _():
            step = exact(m_ref[unit], s_ref[unit], NN if ahead else TN) + b_ref[unit]
            sending[unit] = step.astype(jnp.bfloat16)
            copy_of(unit).start()

    @pl.when(jnp.logical_not(is_last))
    def _():
        for unit in range(units):
            copy_of(unit).wait_send()


def relay(mapping, offset, ahead):
    count = lax.axis_size("seq")
    seqs, heads = mapping.shape[:2]
    units = seqs * heads
    whole = pl.BlockSpec(memory_space=pltpu.VMEM)
    found = pl.pallas_call(
        functools.partial(relay_kernel, count, ahead),
        out_shape=jax.ShapeDtypeStruct((units, DK, DV), jnp.float32),
        in_specs=[whole, whole],
        out_specs=whole,
        scratch_shapes=[
            pltpu.VMEM((units, DK, DV), jnp.bfloat16),
            pltpu.VMEM((units, DK, DV), jnp.bfloat16),
            pltpu.SemaphoreType.DMA((units,)),
            pltpu.SemaphoreType.DMA((units,)),
        ],
        compiler_params=pltpu.CompilerParams(
            collective_id=1 if ahead else 2, has_side_effects=True, vmem_limit_bytes=48 * 2**20
        ),
        name="relay_ahead" if ahead else "relay_back",
    )(mapping.reshape(units, DK, DK), offset.reshape(units, DK, DV))
    return found.reshape(seqs, heads, DK, DV)


def on_device(
    tokens,
    target,
    valid,
    in_weight,
    small_weight,
    out_weight,
    ffn_in,
    ffn_out,
    gain_first,
    gain_second,
    gain_out,
    conv_weight,
    decay_log,
    decay_bias,
):
    inputs = tokens[0].astype(jnp.float32)
    length = inputs.shape[0]
    w_in, w_small = (
        lax.all_gather(in_weight, "seq", axis=0, tiled=True),
        lax.all_gather(small_weight, "seq", axis=0, tiled=True),
    )
    normed_f, first_pull = jax.vjp(rms_scale, inputs, gain_first)
    normed = normed_f.astype(jnp.bfloat16)
    project = jnp.dot(normed, w_in, preferred_element_type=jnp.float32)
    little = jnp.dot(normed, w_small, preferred_element_type=jnp.float32)
    mixed_in = project[:, : 2 * KEYS + VALUES].astype(jnp.bfloat16)
    gate_pre = project[:, 2 * KEYS + VALUES :]
    rim_rows = shifted(mixed_in[length - (CONV - 1) :], "seq", 1)
    padded = jnp.concatenate([rim_rows, mixed_in], axis=0).astype(jnp.float32)
    prepared, local_pull = jax.vjp(prepare, padded, little, conv_weight, decay_log, decay_bias)
    queries, key_rows, values, strength, forget = prepared
    cumulative = jnp.cumsum(forget, axis=0).T
    strength_t = strength.T
    cols = jnp.stack([cumulative, strength_t] + [jnp.zeros_like(cumulative)] * 6, axis=-1)[None]
    rows = jnp.stack([cumulative] * 8, axis=1)[None]
    flat_q, flat_k = queries.reshape(1, length, KEYS), key_rows.reshape(1, length, KEYS)
    flat_v = values.reshape(1, length, VALUES)
    solve, update, back, mapping, offset, own_out, reach = delta_local(
        flat_q, flat_k, flat_v, cols, rows
    )
    entering = relay(mapping, offset, True)
    mixed_out = jnp.transpose(
        own_out[0] + jnp.einsum("htk,hkv->htv", reach[0], entering[0], precision=precise),
        (1, 0, 2),
    )
    branch_f, gated_pull = jax.vjp(gated_norm, mixed_out, gate_pre, gain_out)
    branch = branch_f.astype(jnp.bfloat16)
    w_out, w_up, w_down = (
        lax.all_gather(out_weight, "seq", axis=0, tiled=True),
        lax.all_gather(ffn_in, "seq", axis=0, tiled=True),
        lax.all_gather(ffn_out, "seq", axis=0, tiled=True),
    )
    attended = jnp.einsum("tv,dv->td", branch, w_out, preferred_element_type=jnp.float32)
    hidden = inputs + attended
    second_f, second_pull = jax.vjp(rms_scale, hidden, gain_second)
    second = second_f.astype(jnp.bfloat16)
    gate_up = jnp.dot(second, w_up, preferred_element_type=jnp.float32)
    active_f, swiglu_pull = jax.vjp(swiglu, gate_up)
    active = active_f.astype(jnp.bfloat16)
    feed_out = jnp.einsum("tf,df->td", active, w_down, preferred_element_type=jnp.float32)
    summed = hidden + feed_out
    mask_row = valid[0].astype(jnp.float32)
    errors = summed - target[0].astype(jnp.float32)
    totals = lax.psum(
        (jnp.sum(mask_row * jnp.mean(errors * errors, axis=-1)), jnp.sum(mask_row)), ("dp", "seq")
    )
    valid_count = jnp.maximum(totals[1], 1.0)
    loss_value = totals[0] / valid_count
    all_tokens = length * lax.axis_size("dp") * lax.axis_size("seq")
    grad_summed = all_tokens / valid_count * mask_row[:, None] * errors
    grad_feed = grad_summed.astype(jnp.bfloat16)
    grad_active = jnp.dot(grad_feed, w_down, preferred_element_type=jnp.float32)
    grad_ffn_out = jnp.einsum("td,tf->df", grad_feed, active, preferred_element_type=jnp.float32)
    grad_gate_up = swiglu_pull(grad_active)[0].astype(jnp.bfloat16)
    grad_ffn_in = jnp.einsum("td,tf->df", second, grad_gate_up, preferred_element_type=jnp.float32)
    grad_second = jnp.einsum("tf,df->td", grad_gate_up, w_up, preferred_element_type=jnp.float32)
    hidden_part, grad_gain_second = second_pull(grad_second)
    grad_hidden = grad_summed + hidden_part
    grad_attn = grad_hidden.astype(jnp.bfloat16)
    grad_out_weight = jnp.einsum("td,tv->dv", grad_attn, branch, preferred_element_type=jnp.float32)
    grad_branch = jnp.dot(grad_attn, w_out, preferred_element_type=jnp.float32)
    grad_mixed, grad_gate_pre, grad_gain_out = gated_pull(grad_branch)
    returning = jnp.einsum("htk,thv->hkv", reach[0], grad_mixed, precision=precise)[None]
    after = relay(mapping, returning, False)
    grad_q, grad_k, grad_v, grad_cols, grad_rows = delta_grads(
        flat_q, flat_k, flat_v, cols, rows, solve, update, back, entering,
        grad_mixed.reshape(1, length, VALUES), after,
    )
    grad_log = grad_cols[0, :, :, 0] - grad_rows[0, :, 0, :]
    grad_forget = lax.cumsum(grad_log, axis=1, reverse=True).T
    grad_prepared = (
        grad_q.reshape(length, HEADS, DK),
        grad_k.reshape(length, HEADS, DK),
        grad_v.reshape(length, HEADS, DV),
        grad_cols[0, :, :, 1].T,
        grad_forget,
    )
    grad_padded, grad_little, grad_conv, grad_decay_log, grad_decay_bias = local_pull(grad_prepared)
    rim_grad = shifted(grad_padded[: CONV - 1].astype(jnp.bfloat16), "seq", -1).astype(jnp.float32)
    grad_mixed_in = grad_padded[CONV - 1 :] + jnp.concatenate(
        [jnp.zeros((length - (CONV - 1), grad_padded.shape[1]), jnp.float32), rim_grad], axis=0
    )
    grad_project = jnp.concatenate([grad_mixed_in, grad_gate_pre], axis=1).astype(jnp.bfloat16)
    grad_little_b = grad_little.astype(jnp.bfloat16)
    grad_in_weight = jnp.einsum(
        "td,tp->dp", normed, grad_project, preferred_element_type=jnp.float32
    )
    grad_small_weight = jnp.einsum(
        "td,ts->ds", normed, grad_little_b, preferred_element_type=jnp.float32
    )
    grad_normed = jnp.einsum(
        "tp,dp->td", grad_project, w_in, preferred_element_type=jnp.float32
    ) + jnp.einsum("ts,ds->td", grad_little_b, w_small, preferred_element_type=jnp.float32)
    input_part, grad_gain_first = first_pull(grad_normed)
    grad_tokens = grad_hidden + input_part
    stored = (
        lax.psum_scatter(
            grad_in_weight.astype(jnp.bfloat16), "seq", scatter_dimension=0, tiled=True
        ).astype(jnp.float32),
        lax.psum_scatter(
            grad_small_weight.astype(jnp.bfloat16), "seq", scatter_dimension=0, tiled=True
        ).astype(jnp.float32),
        lax.psum_scatter(
            grad_out_weight.astype(jnp.bfloat16), "seq", scatter_dimension=0, tiled=True
        ).astype(jnp.float32),
        lax.psum_scatter(
            grad_ffn_in.astype(jnp.bfloat16), "seq", scatter_dimension=0, tiled=True
        ).astype(jnp.float32),
        lax.psum_scatter(
            grad_ffn_out.astype(jnp.bfloat16), "seq", scatter_dimension=0, tiled=True
        ).astype(jnp.float32),
    )
    stored = (
        lax.psum(stored[0].astype(jnp.bfloat16), "dp").astype(jnp.float32),
        lax.psum(stored[1].astype(jnp.bfloat16), "dp").astype(jnp.float32),
        lax.psum(stored[2].astype(jnp.bfloat16), "dp").astype(jnp.float32),
        lax.psum(stored[3].astype(jnp.bfloat16), "dp").astype(jnp.float32),
        lax.psum(stored[4].astype(jnp.bfloat16), "dp").astype(jnp.float32),
    )
    smalls = lax.psum(
        (
            grad_gain_first,
            grad_gain_second,
            grad_gain_out,
            grad_conv,
            grad_decay_log,
            grad_decay_bias,
        ),
        ("dp", "seq"),
    )
    return (
        summed.astype(jnp.bfloat16)[None],
        loss_value,
        grad_tokens[None],
        stored[0],
        stored[1],
        stored[2],
        stored[3],
        stored[4],
        smalls[0],
        smalls[1],
        smalls[2],
        smalls[3],
        smalls[4],
        smalls[5],
    )


def solution(mesh):
    placed = (
        P("dp", "seq", None),
        P("dp", "seq", None),
        P("dp", "seq"),
        P("seq", None),
        P("seq", None),
        P("seq", None),
        P("seq", None),
        P("seq", None),
        P(),
        P(),
        P(),
        P(),
        P(),
        P(),
    )
    return jax.shard_map(
        on_device,
        mesh=mesh,
        in_specs=placed,
        out_specs=(
            P("dp", "seq", None),
            P(),
            P("dp", "seq", None),
            P("seq", None),
            P("seq", None),
            P("seq", None),
            P("seq", None),
            P("seq", None),
            P(),
            P(),
            P(),
            P(),
            P(),
            P(),
        ),
        check_vma=False,
    )
```

```python
import functools

import jax
import jax.numpy as jnp
from jax import lax
from jax.experimental import pallas as pl
from jax.experimental.pallas import tpu as pltpu
from jax.sharding import PartitionSpec as P

HEADS = 6
DK = 128
DV = 256
FF = 2816
CONV = 4
BLOCK = 64
KEYS = 768
VALUES = 1536


precise = lax.Precision.HIGHEST
epsilon = 1e-06


def rms_scale(field_in, gain_vec):
    return (
        field_in
        * lax.rsqrt(jnp.mean(field_in * field_in, axis=-1, keepdims=True) + epsilon)
        * gain_vec
    )


def unit_rows(field_in):
    return field_in * lax.rsqrt(jnp.sum(field_in * field_in, axis=-1, keepdims=True) + epsilon)


MESH = pl.DeviceIdType.MESH
NN = (((1,), (0,)), ((), ()))
NT = (((1,), (1,)), ((), ()))
TN = (((0,), (0,)), ((), ()))


def exact(left, right, dims=NN):
    return lax.dot_general(
        left, right, dims, precision=precise, preferred_element_type=jnp.float32
    )


def iotas(rows, columns):
    return (
        lax.broadcasted_iota(jnp.int32, (rows, columns), 0),
        lax.broadcasted_iota(jnp.int32, (rows, columns), 1),
    )


def lower_inverse(system):
    size = system.shape[0]
    row, col = iotas(size, size)
    inverse = (row == col).astype(jnp.float32) - jnp.where(row // 2 == col // 2, system, 0.0)
    width = 2
    while width < size:
        joined = (row // (2 * width) == col // (2 * width)) & (row // width != col // width)
        inverse = inverse - exact(inverse, exact(jnp.where(joined, system, 0.0), inverse))
        width *= 2
    return inverse


def decay_table(gcol, grow):
    size = gcol.shape[0]
    row, col = iotas(size, size)
    keep = row >= col
    return jnp.where(keep, jnp.exp(jnp.where(keep, gcol - grow, 0.0)), 0.0)


def local_kernel(q_ref, k_ref, v_ref, cols_ref, rows_ref, t_ref, u_ref, w_ref, m_ref, b_ref, o_ref, e_ref):
    queries, keys, values = q_ref[0], k_ref[0], v_ref[0]
    cols = cols_ref[0, 0]
    gcol, beta = cols[:, 0:1], cols[:, 1:2]
    grow = rows_ref[0, 0][0:1, :]
    size = keys.shape[0]
    half = size // 2
    decays = decay_table(gcol, grow)
    row, col = iotas(size, size)
    system = jnp.where(row > col, beta * exact(keys, keys, NT) * decays, 0.0)
    first = lower_inverse(system[:half, :half])
    second = lower_inverse(system[half:, half:])
    corner = -exact(second, exact(system[half:, :half], first))
    t_ref[0, 0, :half, :half] = first
    t_ref[0, 0, :half, half:] = jnp.zeros((half, half), jnp.float32)
    t_ref[0, 0, half:, :half] = corner
    t_ref[0, 0, half:, half:] = second
    solve = t_ref[0, 0]
    growth = jnp.exp(gcol)
    last = gcol[size - 1 :, :]
    weights = jnp.exp(last - gcol)
    update = exact(solve, beta * values)
    back = exact(solve, (beta * growth) * keys)
    scores = exact(queries, keys, NT) * decays
    weighted = keys * weights
    drow, dcol = iotas(DK, DK)
    u_ref[0, 0] = update
    w_ref[0, 0] = back
    m_ref[0, 0] = jnp.where(drow == dcol, jnp.exp(last), 0.0) - exact(weighted, back, TN)
    b_ref[0, 0] = exact(weighted, update, TN)
    o_ref[0, 0] = exact(scores, update)
    e_ref[0, 0] = growth * queries - exact(scores, back)


def per_unit(*shape):
    return pl.BlockSpec((1, 1) + shape, lambda j, h: (j, h) + (0,) * len(shape))


def per_head(length, width):
    return pl.BlockSpec((1, length, width), lambda j, h: (j, 0, h))


def delta_local(queries, keys, values, cols, rows):
    seqs, length = queries.shape[:2]
    heads = cols.shape[1]

    def out(*shape):
        return jax.ShapeDtypeStruct((seqs, heads) + shape, jnp.float32)

    return pl.pallas_call(
        local_kernel,
        grid=(seqs, heads),
        in_specs=[
            per_head(length, DK),
            per_head(length, DK),
            per_head(length, DV),
            per_unit(length, 8),
            per_unit(8, length),
        ],
        out_specs=[
            per_unit(length, length),
            per_unit(length, DV),
            per_unit(length, DK),
            per_unit(DK, DK),
            per_unit(DK, DV),
            per_unit(length, DV),
            per_unit(length, DK),
        ],
        out_shape=[
            out(length, length),
            out(length, DV),
            out(length, DK),
            out(DK, DK),
            out(DK, DV),
            out(length, DV),
            out(length, DK),
        ],
        compiler_params=pltpu.CompilerParams(vmem_limit_bytes=48 * 2**20),
        name="delta_local",
    )(queries, keys, values, cols, rows)


def grads_kernel(
    q_ref, k_ref, v_ref, cols_ref, rows_ref, t_ref, u_ref, w_ref, s_ref, do_ref, ds_ref,
    dq_ref, dk_ref, dv_ref, dcols_ref, drows_ref,
):
    queries, keys, values = q_ref[0], k_ref[0], v_ref[0]
    cols = cols_ref[0, 0]
    gcol, beta = cols[:, 0:1], cols[:, 1:2]
    grow = rows_ref[0, 0][0:1, :]
    size = keys.shape[0]
    decays = decay_table(gcol, grow)
    row, col = iotas(size, size)
    strict = row > col
    memory, after = s_ref[0, 0], ds_ref[0, 0]
    grad_out = do_ref[0]
    growth = jnp.exp(gcol)
    last = gcol[size - 1 :, :]
    weights = jnp.exp(last - gcol)
    update = u_ref[0, 0] - exact(w_ref[0, 0], memory)
    scores = exact(queries, keys, NT) * decays
    keys_dot = jnp.where(strict, exact(keys, keys, NT) * decays, 0.0)
    grad_update = exact(scores, grad_out, TN) + exact(keys * weights, after)
    grad_wanted = exact(t_ref[0, 0], grad_update, TN)
    grad_system = -exact(grad_wanted, update, NT)
    grad_scores = exact(grad_out, update, NT)
    through = keys_dot * grad_system
    total = grad_scores * scores + beta * through
    query_part = growth * exact(grad_out, memory, NT)
    key_read = growth * exact(grad_wanted, memory, NT)
    key_part = beta * key_read
    end_part = weights * exact(update, after, NT)
    grad_dot = grad_scores * decays
    grad_keys_dot = jnp.where(strict, grad_system * decays, 0.0) * beta
    dq_ref[0] = query_part + exact(grad_dot, keys)
    dk_ref[0] = (
        end_part - key_part + exact(grad_dot, queries, TN)
        + exact(grad_keys_dot, keys) + exact(grad_keys_dot, keys, TN)
    )
    dv_ref[0] = beta * grad_wanted
    key_line = jnp.sum(keys * key_part, axis=1, keepdims=True)
    end_line = jnp.sum(keys * end_part, axis=1, keepdims=True)
    grad_beta = (
        jnp.sum(grad_wanted * values, axis=1, keepdims=True)
        - jnp.sum(keys * key_read, axis=1, keepdims=True)
        + jnp.sum(through, axis=1, keepdims=True)
    )
    grad_log = (
        jnp.sum(queries * query_part, axis=1, keepdims=True)
        - key_line
        - end_line
        + jnp.sum(total, axis=1, keepdims=True)
    )
    grad_last = jnp.sum(end_line) + jnp.sum(jnp.exp(last) * jnp.sum(memory * after, axis=1, keepdims=True))
    line = lax.broadcasted_iota(jnp.int32, (size, 1), 0)
    grad_log = grad_log + jnp.where(line == size - 1, grad_last, 0.0)
    lane = lax.broadcasted_iota(jnp.int32, (size, 8), 1)
    dcols_ref[0, 0] = jnp.where(lane == 0, grad_log, jnp.where(lane == 1, grad_beta, 0.0))
    drows_ref[0, 0] = jnp.broadcast_to(jnp.sum(total, axis=0, keepdims=True), (8, size))


def delta_grads(queries, keys, values, cols, rows, solve, update, back, entering, grad_out, after):
    seqs, length = queries.shape[:2]
    heads = cols.shape[1]
    return pl.pallas_call(
        grads_kernel,
        grid=(seqs, heads),
        in_specs=[
            per_head(length, DK),
            per_head(length, DK),
            per_head(length, DV),
            per_unit(length, 8),
            per_unit(8, length),
            per_unit(length, length),
            per_unit(length, DV),
            per_unit(length, DK),
            per_unit(DK, DV),
            per_head(length, DV),
            per_unit(DK, DV),
        ],
        out_specs=[
            per_head(length, DK),
            per_head(length, DK),
            per_head(length, DV),
            per_unit(length, 8),
            per_unit(8, length),
        ],
        out_shape=[
            jax.ShapeDtypeStruct(queries.shape, jnp.float32),
            jax.ShapeDtypeStruct(keys.shape, jnp.float32),
            jax.ShapeDtypeStruct(values.shape, jnp.float32),
            jax.ShapeDtypeStruct(cols.shape, jnp.float32),
            jax.ShapeDtypeStruct(rows.shape, jnp.float32),
        ],
        compiler_params=pltpu.CompilerParams(vmem_limit_bytes=48 * 2**20),
        name="delta_grads",
    )(queries, keys, values, cols, rows, solve, update, back, entering, grad_out, after)


def relay_kernel(count, ahead, m_ref, b_ref, s_ref, sending, arriving, send_sem, recv_sem):
    place, group = lax.axis_index("seq"), lax.axis_index("dp")
    units = m_ref.shape[0]
    if ahead:
        is_first, is_last = place == 0, place == count - 1
        before, beyond = lax.rem(place + count - 1, count), lax.rem(place + 1, count)
    else:
        is_first, is_last = place == count - 1, place == 0
        before, beyond = lax.rem(place + 1, count), lax.rem(place + count - 1, count)
    barrier = pltpu.get_barrier_semaphore()

    @pl.when(jnp.logical_not(is_first))
    def _():
        pl.semaphore_signal(barrier, inc=1, device_id=(group, before), device_id_type=MESH)

    @pl.when(jnp.logical_not(is_last))
    def _():
        pl.semaphore_wait(barrier, 1)

    def copy_of(unit):
        return pltpu.make_async_remote_copy(
            src_ref=sending.at[unit],
            dst_ref=arriving.at[unit],
            send_sem=send_sem.at[unit],
            recv_sem=recv_sem.at[unit],
            device_id=(group, beyond),
            device_id_type=MESH,
        )

    for unit in range(units):

        @pl.when(is_first)
        def _():
            s_ref[unit] = jnp.zeros_like(s_ref[unit])

        @pl.when(jnp.logical_not(is_first))
        def _():
            copy_of(unit).wait_recv()
            s_ref[unit] = arriving[unit].astype(jnp.float32)

        @pl.when(jnp.logical_not(is_last))
        def _():
            step = exact(m_ref[unit], s_ref[unit], NN if ahead else TN) + b_ref[unit]
            sending[unit] = step.astype(jnp.bfloat16)
            copy_of(unit).start()

    @pl.when(jnp.logical_not(is_last))
    def _():
        for unit in range(units):
            copy_of(unit).wait_send()


def relay(mapping, offset, ahead):
    count = lax.axis_size("seq")
    seqs, heads = mapping.shape[:2]
    units = seqs * heads
    whole = pl.BlockSpec(memory_space=pltpu.VMEM)
    found = pl.pallas_call(
        functools.partial(relay_kernel, count, ahead),
        out_shape=jax.ShapeDtypeStruct((units, DK, DV), jnp.float32),
        in_specs=[whole, whole],
        out_specs=whole,
        scratch_shapes=[
            pltpu.VMEM((units, DK, DV), jnp.bfloat16),
            pltpu.VMEM((units, DK, DV), jnp.bfloat16),
            pltpu.SemaphoreType.DMA((units,)),
            pltpu.SemaphoreType.DMA((units,)),
        ],
        compiler_params=pltpu.CompilerParams(
            collective_id=1 if ahead else 2, has_side_effects=True, vmem_limit_bytes=48 * 2**20
        ),
        name="relay_ahead" if ahead else "relay_back",
    )(mapping.reshape(units, DK, DK), offset.reshape(units, DK, DV))
    return found.reshape(seqs, heads, DK, DV)


def tile_start(start):
    return pl.multiple_of(start, 128)


class Place:
    def __init__(self, groups, count):
        self.groups, self.count, self.half = groups, count, count // 2
        self.group, self.place = lax.axis_index("dp"), lax.axis_index("seq")
        self.pair, self.side = self.place // 2, self.place % 2
        self.plane = (self.group // 2) % 2
        self.group_swap = self.group + 1 - 2 * (self.group % 2)
        self.across = self.group + 2 - 4 * self.plane
        self.beside = self.place + 1 - 2 * self.side

    def shard(self, pair, side):
        return 2 * pair + side

    def ahead(self, step):
        return lax.rem(self.pair + step, self.half)

    def behind(self, step):
        return lax.rem(self.pair + self.half - step, self.half)

    def partners(self):
        along = [(self.group, self.shard(self.ahead(step), self.side)) for step in range(1, self.half)]
        return along + [(self.group, self.beside), (self.across, self.place)]


def greet(signalled, awaited):
    barrier = pltpu.get_barrier_semaphore()
    for device in signalled:
        pl.semaphore_signal(barrier, inc=1, device_id=device, device_id_type=MESH)
    pl.semaphore_wait(barrier, awaited)


def remote(source, target, sends, receives, index, device):
    return pltpu.make_async_remote_copy(
        src_ref=source,
        dst_ref=target,
        send_sem=sends.at[index],
        recv_sem=receives.at[index],
        device_id=device,
        device_id_type=MESH,
    )


class Gather:
    def __init__(self, at, source, target, share, sends, receives, local):
        self.at, self.source, self.target = at, source, target
        self.sends, self.receives, self.local = sends, receives, local
        width = source.shape[1]
        self.own = pl.ds(tile_start(at.plane * share), width - share)
        self.lent = pl.ds(tile_start(at.plane * (width - share)), share)
        self.borrowed = pl.ds(tile_start((1 - at.plane) * (width - share)), share)
        self.started = []

    def copy(self, index, shard, columns, device, from_source=False):
        there = self.target.at[shard, :, columns]
        here = self.source.at[:, columns] if from_source else there
        return remote(here, there, self.sends, self.receives, index, device)

    def along(self, step):
        at = self.at
        device = (at.group, at.shard(at.ahead(step), at.side))
        return self.copy(step - 1, at.place, self.own, device, True)

    def beside(self, step):
        at = self.at
        shard = at.shard(at.behind(step), at.side)
        return self.copy(at.half - 1 + step, shard, self.own, (at.group, at.beside), step == 0)

    def across(self, step, side):
        at = self.at
        shard = at.shard(at.behind(step), at.side if side == 0 else 1 - at.side)
        return self.copy(2 * at.half - 1 + 2 * step + side - 1, shard, self.lent, (at.across, at.place))

    def keep(self):
        return pltpu.make_async_copy(self.source, self.target.at[self.at.place], self.local)

    def launch(self, copy):
        copy.start()
        self.started.append(copy)

    def begin(self):
        self.keep().start()
        for step in range(1, self.at.half):
            self.launch(self.along(step))
        self.launch(self.beside(0))

    def arrived(self, index, shard, columns):
        self.copy(index, shard, columns, (self.at.group, self.at.place)).wait_recv()

    def pass_along(self, step):
        at = self.at
        self.arrived(step - 1, at.shard(at.behind(step), at.side), self.own)
        self.launch(self.beside(step))
        self.launch(self.across(step, 0))

    def pass_beside(self, step):
        at = self.at
        self.arrived(at.half - 1 + step, at.shard(at.behind(step), 1 - at.side), self.own)
        self.launch(self.across(step, 1))

    def finish(self):
        at = self.at
        for step in range(at.half):
            for side in range(2):
                if step or side:
                    shard = at.shard(at.behind(step), at.side if side == 0 else 1 - at.side)
                    self.arrived(2 * at.half - 1 + 2 * step + side - 1, shard, self.borrowed)
        for copy in self.started:
            copy.wait_send()
        self.keep().wait()

    def stages(self):
        half = self.at.half
        first = [functools.partial(self.pass_along, step) for step in range(1, half)]
        second = [functools.partial(self.pass_beside, step) for step in range(half)]
        return first, second


def copies_of_gather(count):
    return 2 * count - 2


def lagged(plans):
    depth = max(len(plan) for plan in plans)
    turns = []
    for turn in range(len(plans) + depth - 1):
        steps = []
        for index, plan in enumerate(plans):
            if 0 <= turn - index < len(plan):
                steps = plan[turn - index] + steps
        turns.append(steps)
    return turns


class Reduce:
    def __init__(self, at, given, total, other, share, buffers, sems):
        self.at, self.given, self.total, self.other, self.share = at, given, total, other, share
        self.acc, self.from_across, self.from_beside, self.from_along, self.part, self.from_plane, self.far = buffers
        self.sends, self.receives, self.local = sems
        width = total.shape[1]
        self.wide = width - share
        self.own = pl.ds(tile_start(at.plane * share), self.wide)
        self.lent = pl.ds(tile_start((1 - at.plane) * self.wide), share)
        self.inner = pl.ds(tile_start(at.plane * (width - 2 * share)), share)
        self.theirs = pl.ds(tile_start((1 - at.plane) * share), self.wide)
        self.started = []

    def launch(self, copy):
        copy.start()
        self.started.append(copy)

    def across(self, shard, index):
        at = self.at
        return remote(
            self.given.at[shard, :, self.lent], self.from_across.at[shard],
            self.sends, self.receives, index, (at.across, at.place),
        )

    def beside(self, pair):
        at = self.at
        return remote(
            self.acc.at[at.shard(pair, 1 - at.side)], self.from_beside.at[pair],
            self.sends, self.receives, at.count + pair, (at.group, at.beside),
        )

    def along(self, step):
        at = self.at
        shard = at.shard(at.ahead(step), at.side)
        return remote(
            self.acc.at[shard], self.from_along.at[step - 1],
            self.sends, self.receives, at.count + at.half + step - 1, (at.group, shard),
        )

    def plane(self):
        at = self.at
        return remote(
            self.part, self.from_plane, self.sends, self.receives,
            at.count + 2 * at.half - 1, (at.across, at.place),
        )

    def further(self, index, distance):
        at = self.at
        group = at.group + distance - 2 * distance * ((at.group // distance) % 2)
        return remote(
            self.total, self.far.at[index], self.sends, self.receives,
            at.count + 2 * at.half + 1 + index, (group, at.place),
        )

    def core(self):
        at = self.at
        return remote(
            self.total, self.other, self.sends, self.receives,
            at.count + 2 * at.half, (at.group_swap, at.place),
        )

    def load(self, shard, index):
        return pltpu.make_async_copy(self.given.at[shard, :, self.own], self.acc.at[shard], self.local.at[index])

    def order(self, side):
        at = self.at
        return [(pair, at.shard(pair, at.side if side else 1 - at.side)) for pair in range(at.half)]

    def begin(self):
        for side in range(2):
            for pair, shard in self.order(side):
                self.load(shard, 2 * pair + side).start()
                self.launch(self.across(shard, 2 * pair + side))

    def add_across(self, side):
        for pair, shard in self.order(side):
            self.load(shard, 2 * pair + side).wait()
            self.across(shard, 2 * pair + side).wait_recv()
            mine = self.acc[shard, :, self.inner].astype(jnp.float32)
            got = self.from_across[shard].astype(jnp.float32)
            self.acc[shard, :, self.inner] = (mine + got).astype(jnp.bfloat16)
            if side == 0:
                self.launch(self.beside(pair))

    def add_beside(self):
        at = self.at
        for step in range(1, at.half + 1):
            pair = at.ahead(step)
            shard = at.shard(pair, at.side)
            self.beside(pair).wait_recv()
            mine = self.acc[shard].astype(jnp.float32)
            self.acc[shard] = (mine + self.from_beside[pair].astype(jnp.float32)).astype(jnp.bfloat16)
            if step < at.half:
                self.launch(self.along(step))

    def add_along(self):
        at = self.at
        value = self.acc[at.place].astype(jnp.float32)
        for step in range(1, at.half):
            self.along(step).wait_recv()
            value = value + self.from_along[step - 1].astype(jnp.float32)
        self.part[...] = value.astype(jnp.bfloat16)
        self.launch(self.plane())

    def add_plane(self):
        self.plane().wait_recv()
        self.total[...] = jnp.zeros_like(self.total)
        self.total[:, self.own] = self.part[...]
        mine = self.total[:, self.theirs].astype(jnp.float32)
        got = self.from_plane[...].astype(jnp.float32)
        self.total[:, self.theirs] = (mine + got).astype(jnp.bfloat16)
        distance = 4
        while distance < self.at.groups:
            copy = self.further(distance.bit_length() - 3, distance)
            copy.start()
            copy.wait()
            got = self.far[distance.bit_length() - 3].astype(jnp.float32)
            self.total[...] = (self.total[...].astype(jnp.float32) + got).astype(jnp.bfloat16)
            distance *= 2
        self.launch(self.core())

    def finish(self):
        self.core().wait_recv()
        for copy in self.started:
            copy.wait_send()

    def stages(self):
        return [
            [functools.partial(self.add_across, 0)],
            [functools.partial(self.add_across, 1), self.add_beside],
            [self.add_along],
            [self.add_plane],
        ]
ANY = pl.BlockSpec(memory_space=pl.ANY)
ROOM = pl.BlockSpec(memory_space=pltpu.VMEM)
PAD = 16


def neighbours(at, step):
    place = lax.rem(at.place + at.count + step, at.count)
    return (at.group, place), (at.group_swap, place)


def gather_first_kernel(groups, count, share, *refs):
    source, tokens, target, mask = refs[:4]
    gathered, tokens_other, target_other, mask_other, rim = refs[4:9]
    sends, receives, local, swap_send, swap_recv = refs[9:]
    at = Place(groups, count)
    core = (at.group_swap, at.place)
    greet(at.partners() + [core] + list(neighbours(at, -1)), count // 2 + 4)
    swaps = [
        remote(here, there, swap_send, swap_recv, index, core)
        for index, (here, there) in enumerate(
            ((tokens, tokens_other), (target, target_other), (mask, mask_other))
        )
    ]
    length = tokens.shape[0]
    tail = tokens.at[pl.ds(length - PAD, PAD)]
    own_next, swap_next = neighbours(at, 1)
    rims = [
        remote(tail, rim.at[0], swap_send, swap_recv, 3, own_next),
        remote(tail, rim.at[1], swap_send, swap_recv, 4, swap_next),
    ]
    plan = Gather(at, source, gathered, share, sends, receives, local.at[0])

    @pl.when(at.place < count - 1)
    def _():
        for copy in rims:
            copy.start()

    plan.begin()
    for copy in swaps:
        copy.start()
    for stage in plan.stages():
        for step in stage:
            step()
    plan.finish()
    for copy in swaps:
        copy.wait()

    @pl.when(at.place == 0)
    def _():
        rim[...] = jnp.zeros_like(rim)

    @pl.when(at.place > 0)
    def _():
        for copy in rims:
            copy.wait_recv()

    @pl.when(at.place < count - 1)
    def _():
        for copy in rims:
            copy.wait_send()


def gather_first(source, tokens, target, mask, share):
    groups, count = lax.axis_size("dp"), lax.axis_size("seq")
    rows, width = source.shape
    return pl.pallas_call(
        functools.partial(gather_first_kernel, groups, count, share),
        out_shape=[
            jax.ShapeDtypeStruct((count, rows, width), source.dtype),
            jax.ShapeDtypeStruct(tokens.shape, tokens.dtype),
            jax.ShapeDtypeStruct(target.shape, target.dtype),
            jax.ShapeDtypeStruct(mask.shape, mask.dtype),
            jax.ShapeDtypeStruct((2, PAD, tokens.shape[1]), tokens.dtype),
        ],
        in_specs=[ANY] * 4,
        out_specs=[ANY] * 4 + [ROOM],
        scratch_shapes=[
            pltpu.SemaphoreType.DMA((copies_of_gather(count),)),
            pltpu.SemaphoreType.DMA((copies_of_gather(count),)),
            pltpu.SemaphoreType.DMA((1,)),
            pltpu.SemaphoreType.DMA((5,)),
            pltpu.SemaphoreType.DMA((5,)),
        ],
        compiler_params=pltpu.CompilerParams(collective_id=3, has_side_effects=True),
        name="gather_first",
    )(source, tokens, target, mask)


def gather_rest_kernel(groups, count, shares, *refs):
    number = len(shares)
    sources, targets = refs[:number], refs[number : 2 * number]
    sends, receives, local = refs[2 * number :]
    at = Place(groups, count)
    greet(at.partners(), count // 2 + 1)
    plans = [
        Gather(at, sources[i], targets[i], shares[i], sends.at[i], receives.at[i], local.at[i])
        for i in range(number)
    ]
    for plan in plans:
        plan.begin()
    for turn in lagged([plan.stages() for plan in plans]):
        for step in turn:
            step()
    for plan in plans:
        plan.finish()


def gather_rest(sources, shares):
    groups, count = lax.axis_size("dp"), lax.axis_size("seq")
    number = len(sources)
    return pl.pallas_call(
        functools.partial(gather_rest_kernel, groups, count, shares),
        out_shape=[jax.ShapeDtypeStruct((count,) + v.shape, v.dtype) for v in sources],
        in_specs=[ANY] * number,
        out_specs=[ANY] * number,
        scratch_shapes=[
            pltpu.SemaphoreType.DMA((number, copies_of_gather(count))),
            pltpu.SemaphoreType.DMA((number, copies_of_gather(count))),
            pltpu.SemaphoreType.DMA((number,)),
        ],
        compiler_params=pltpu.CompilerParams(collective_id=4, has_side_effects=True),
        name="gather_rest",
    )(*sources)


def reduce_buffers(groups, count, rows, width, share):
    wide, half = width - share, count // 2
    steps = max(1, (groups // 4).bit_length() - 1)
    kind = jnp.bfloat16
    return [
        pltpu.VMEM((count, rows, wide), kind),
        pltpu.VMEM((count, rows, share), kind),
        pltpu.VMEM((half, rows, wide), kind),
        pltpu.VMEM((half - 1, rows, wide), kind),
        pltpu.VMEM((rows, wide), kind),
        pltpu.VMEM((rows, wide), kind),
        pltpu.VMEM((steps, rows, width), kind),
    ]


def copies_of_reduce(groups, count):
    return 2 * count + 1 + max(1, (groups // 4).bit_length() - 1)


def further_groups(at):
    found, distance = [], 4
    while distance < at.groups:
        found.append((at.group + distance - 2 * distance * ((at.group // distance) % 2), at.place))
        distance *= 2
    return found


def reduce_plans(at, givens, totals, others, shares, scratch):
    number = len(shares)
    sends, receives, local = scratch[7 * number : 7 * number + 3]
    return [
        Reduce(
            at, givens[i], totals[i], others[i], shares[i], scratch[7 * i : 7 * i + 7],
            (sends.at[i], receives.at[i], local.at[i]),
        )
        for i in range(number)
    ]


def reduce_scratch(groups, count, rows, widths, shares):
    scratch = []
    for width, share in zip(widths, shares):
        scratch += reduce_buffers(groups, count, rows, width, share)
    number, copies = len(widths), copies_of_reduce(groups, count)
    return scratch + [
        pltpu.SemaphoreType.DMA((number, copies)),
        pltpu.SemaphoreType.DMA((number, copies)),
        pltpu.SemaphoreType.DMA((number, count)),
    ]


def reduce_rest_kernel(groups, count, shares, *refs):
    number = len(shares)
    givens, totals, others = refs[:number], refs[number : 2 * number], refs[2 * number : 3 * number]
    at = Place(groups, count)
    further = further_groups(at)
    partners = at.partners() + [(at.group_swap, at.place)] + further
    greet(partners, count // 2 + 2 + len(further))
    plans = reduce_plans(at, givens, totals, others, shares, refs[3 * number :])
    for plan in plans:
        plan.begin()
    for turn in lagged([plan.stages() for plan in plans]):
        for step in turn:
            step()
    for plan in plans:
        plan.finish()


def reduce_rest(givens, shares):
    groups, count = lax.axis_size("dp"), lax.axis_size("seq")
    number = len(givens)
    rows = givens[0].shape[1]
    widths = [v.shape[2] for v in givens]
    results = [jax.ShapeDtypeStruct((rows, width), jnp.bfloat16) for width in widths]
    return pl.pallas_call(
        functools.partial(reduce_rest_kernel, groups, count, shares),
        out_shape=results * 2,
        in_specs=[ANY] * number,
        out_specs=[ROOM] * (2 * number),
        scratch_shapes=reduce_scratch(groups, count, rows, widths, shares),
        compiler_params=pltpu.CompilerParams(
            collective_id=5, has_side_effects=True, vmem_limit_bytes=56 * 2**20
        ),
        name="reduce_rest",
    )(*givens)


def reduce_first_kernel(groups, count, share, *refs):
    given, swap, rims, small = refs[:4]
    total, other, swap_got, rim_got, small_sum = refs[4:9]
    scratch = refs[9:]
    small_got, small_hold, swap_send, swap_recv, small_send, small_recv = scratch[10:]
    at = Place(groups, count)
    further = further_groups(at)
    core = (at.group_swap, at.place)
    stages = []
    distance = 1
    while distance < groups:
        stages.append((at.group + distance - 2 * distance * ((at.group // distance) % 2), at.place))
        distance *= 2
    distance = 1
    while distance < count:
        stages.append((at.group, at.place + distance - 2 * distance * ((at.place // distance) % 2)))
        distance *= 2
    partners = at.partners() + [core] + further + stages + list(neighbours(at, 1))
    greet(partners, count // 2 + 4 + len(further) + len(stages))
    own_back, swap_back = neighbours(at, -1)
    swapped = remote(swap, swap_got, swap_send, swap_recv, 0, core)
    rim_copies = [
        remote(rims.at[0], rim_got.at[0], swap_send, swap_recv, 1, own_back),
        remote(rims.at[1], rim_got.at[1], swap_send, swap_recv, 2, swap_back),
    ]
    plan = reduce_plans(at, [given], [total], [other], [share], scratch)[0]
    plan.begin()
    swapped.start()

    @pl.when(at.place > 0)
    def _():
        for copy in rim_copies:
            copy.start()

    small_hold[0] = small[...]

    def add_small(index):
        copy = remote(
            small_hold.at[index], small_got.at[index], small_send, small_recv, index, stages[index]
        )
        copy.start()
        copy.wait()
        small_hold[index + 1] = small_hold[index] + small_got[index]

    steps = [step for stage in plan.stages() for step in stage]
    for index in range(max(len(steps), len(stages))):
        if index < len(steps):
            steps[index]()
        if index < len(stages):
            add_small(index)
    small_sum[...] = small_hold[len(stages)]
    swapped.wait()

    @pl.when(at.place == count - 1)
    def _():
        rim_got[...] = jnp.zeros_like(rim_got)

    @pl.when(at.place < count - 1)
    def _():
        for copy in rim_copies:
            copy.wait_recv()

    @pl.when(at.place > 0)
    def _():
        for copy in rim_copies:
            copy.wait_send()

    plan.finish()


def reduce_first(given, swap, rims, small, share):
    groups, count = lax.axis_size("dp"), lax.axis_size("seq")
    unused, rows, width = given.shape
    rounds = (groups.bit_length() - 1) + (count.bit_length() - 1)
    result = jax.ShapeDtypeStruct((rows, width), jnp.bfloat16)
    return pl.pallas_call(
        functools.partial(reduce_first_kernel, groups, count, share),
        out_shape=[
            result,
            result,
            jax.ShapeDtypeStruct(swap.shape, swap.dtype),
            jax.ShapeDtypeStruct(rims.shape, rims.dtype),
            jax.ShapeDtypeStruct(small.shape, small.dtype),
        ],
        in_specs=[ANY, ROOM, ROOM, ROOM],
        out_specs=[ROOM] * 5,
        scratch_shapes=reduce_scratch(groups, count, rows, [width], [share])
        + [
            pltpu.VMEM((rounds,) + small.shape, jnp.float32),
            pltpu.VMEM((rounds + 1,) + small.shape, jnp.float32),
            pltpu.SemaphoreType.DMA((3,)),
            pltpu.SemaphoreType.DMA((3,)),
            pltpu.SemaphoreType.DMA((rounds,)),
            pltpu.SemaphoreType.DMA((rounds,)),
        ],
        compiler_params=pltpu.CompilerParams(
            collective_id=6, has_side_effects=True, vmem_limit_bytes=56 * 2**20
        ),
        name="reduce_first",
    )(given, swap, rims, small)


def third(width, weight):
    return 128 * max(1, round(width * weight / 128))


def prepare(padded, little, conv_weight, decay_log, decay_bias):
    seqs, length = padded.shape[0], padded.shape[1] - (CONV - 1)
    convolved = conv_weight[0] * padded[:, 0:length]
    for offset in range(1, CONV):
        convolved = convolved + conv_weight[offset] * padded[:, offset : offset + length]
    active = jax.nn.silu(convolved)
    heads = decay_log.shape[0]
    keys = heads * DK
    queries = unit_rows(active[..., :keys].reshape(seqs, length, heads, DK)) * DK ** (-0.5)
    key_rows = unit_rows(active[..., keys : 2 * keys].reshape(seqs, length, heads, DK))
    strength = jax.nn.sigmoid(little[..., :heads])
    forget = -jnp.exp(decay_log) * jax.nn.softplus(little[..., heads:] + decay_bias)
    return (
        queries.reshape(seqs, length, keys),
        key_rows.reshape(seqs, length, keys),
        active[..., 2 * keys :],
        strength,
        forget,
    )


def gated_norm(mixed_out, gate_pre, gain_out):
    rows, width = mixed_out.shape
    split = mixed_out.reshape(rows, width // DV, DV)
    gate = jax.nn.silu(gate_pre.reshape(split.shape))
    return (rms_scale(split, gain_out) * gate).reshape(rows, width)


def swiglu(gate_up):
    hidden_units = gate_up.shape[1] // 2
    return jax.nn.silu(gate_up[:, :hidden_units]) * gate_up[:, hidden_units:]


def norm_parts(field_in):
    scale = lax.rsqrt(jnp.mean(field_in * field_in, axis=-1, keepdims=True) + epsilon)
    return scale, field_in * scale


def norm_back(scale, unit, gain_vec, grad):
    scaled = grad * gain_vec
    return scale * (scaled - unit * jnp.mean(scaled * unit, axis=-1, keepdims=True))


def dense(left, right, dims):
    return lax.dot_general(left, right, (dims, ((), ())), preferred_element_type=jnp.float32)


def on_device(
    tokens,
    target,
    valid,
    in_weight,
    small_weight,
    out_weight,
    ffn_in,
    ffn_out,
    gain_first,
    gain_second,
    gain_out,
    conv_weight,
    decay_log,
    decay_bias,
):
    count = lax.axis_size("seq")
    groups = lax.axis_size("dp")
    core = lax.axis_index("dp") % 2
    rows = in_weight.shape[0]
    length, model = tokens.shape[1], tokens.shape[2]
    both = 2 * length
    heads = HEADS // 2
    keys, vals = KEYS // 2, VALUES // 2

    def mine(array, start, width):
        return lax.dynamic_slice_in_dim(array, start + core * width, width, array.ndim - 1)

    def qkv_half(array):
        parts = [mine(array, 0, keys), mine(array, KEYS, keys), mine(array, 2 * KEYS, vals)]
        return jnp.concatenate(parts, axis=1)

    small_half = [mine(small_weight, 0, heads), mine(small_weight, HEADS, heads)]
    spare = jnp.zeros((rows, 128 - 2 * heads), jnp.bfloat16)
    part_first = jnp.concatenate([qkv_half(in_weight)] + small_half + [spare], axis=1)
    part_gate = mine(in_weight, 2 * KEYS + VALUES, vals)
    part_out = mine(out_weight, 0, vals)
    part_up = jnp.concatenate([mine(ffn_in, 0, FF // 2), mine(ffn_in, FF, FF // 2)], axis=1)
    part_down = mine(ffn_out, 0, FF // 2)
    first_width = part_first.shape[1]

    mask_own = valid[0].astype(jnp.float32)
    mask_rows = jnp.broadcast_to(mask_own[None, :], (8, length))
    w_first, tokens_other, target_other, mask_other, rim = gather_first(
        part_first, tokens[0], target[0], mask_rows, third(first_width, 0.33)
    )
    rests = [part_gate, part_out, part_up, part_down]
    w_gate, w_out, w_up, w_down = gather_rest(rests, [third(v.shape[1], 0.33) for v in rests])
    w_first, w_gate, w_out, w_up, w_down = (
        v.reshape(model, v.shape[2]) for v in (w_first, w_gate, w_out, w_up, w_down)
    )

    inputs = jnp.concatenate(
        [tokens[0], tokens_other, rim.reshape(2 * PAD, model)], axis=0
    ).astype(jnp.float32)
    first_scale, first_unit = norm_parts(inputs)
    normed = (first_unit * gain_first).astype(jnp.bfloat16)
    project = dense(normed, w_first, ((1,), (0,)))
    gate_pre = dense(normed[:both], w_gate, ((1,), (0,)))
    mixed_width = 2 * keys + vals
    mixed_in = project[:, :mixed_width].astype(jnp.bfloat16).astype(jnp.float32)
    little = project[:both, mixed_width : mixed_width + 2 * heads].reshape(2, length, 2 * heads)
    padded = jnp.concatenate(
        [
            mixed_in[both:].reshape(2, PAD, mixed_width)[:, PAD - (CONV - 1) :],
            mixed_in[:both].reshape(2, length, mixed_width),
        ],
        axis=1,
    )
    own_conv = qkv_half(conv_weight)
    own_log, own_bias = mine(decay_log, 0, heads), mine(decay_bias, 0, heads)
    prepared, local_pull = jax.vjp(prepare, padded, little, own_conv, own_log, own_bias)
    queries, key_rows, values, strength, forget = prepared
    cumulative = jnp.swapaxes(jnp.cumsum(forget, axis=1), 1, 2)
    strength_t = jnp.swapaxes(strength, 1, 2)
    cols = jnp.stack([cumulative, strength_t] + [jnp.zeros_like(cumulative)] * 6, axis=-1)
    table = jnp.stack([cumulative] * 8, axis=2)
    solve, update, back, mapping, offset, own_out, reach = delta_local(
        queries, key_rows, values, cols, table
    )
    entering = relay(mapping, offset, True)
    mixed_out = jnp.swapaxes(
        own_out + jnp.einsum("jhtk,jhkv->jhtv", reach, entering, precision=precise), 1, 2
    ).reshape(both, vals)
    branch_f, gated_pull = jax.vjp(gated_norm, mixed_out, gate_pre, gain_out)
    branch = branch_f.astype(jnp.bfloat16)

    def core_sum(part):
        pairs = [(group, group ^ 1) for group in range(groups)]
        got = lax.ppermute(part.astype(jnp.bfloat16), "dp", pairs)
        return part + jnp.concatenate([got[length:], got[:length]], axis=0).astype(jnp.float32)

    hidden = inputs[:both] + core_sum(dense(branch, w_out, ((1,), (1,))))
    second_scale, second_unit = norm_parts(hidden)
    second = (second_unit * gain_second).astype(jnp.bfloat16)
    gate_up = dense(second, w_up, ((1,), (0,)))
    active_f, swiglu_pull = jax.vjp(swiglu, gate_up)
    active = active_f.astype(jnp.bfloat16)
    summed = hidden + core_sum(dense(active, w_down, ((1,), (1,))))
    mask = jnp.concatenate([mask_own, mask_other[0]])
    errors = summed - jnp.concatenate([target[0], target_other]).astype(jnp.float32)
    own_errors = errors[:length]
    loss_part = jnp.sum(mask_own * jnp.mean(own_errors * own_errors, axis=-1))

    grad_summed = mask[:, None] * errors
    grad_feed = grad_summed.astype(jnp.bfloat16)
    grad_active = dense(grad_feed, w_down, ((1,), (0,)))
    grad_down = dense(grad_feed, active, ((0,), (0,))).astype(jnp.bfloat16)
    grad_gate_up = swiglu_pull(grad_active)[0].astype(jnp.bfloat16)
    grad_up = dense(second, grad_gate_up, ((0,), (0,))).astype(jnp.bfloat16)
    grad_second = core_sum(dense(grad_gate_up, w_up, ((1,), (1,))))
    grad_gain_second = jnp.sum((grad_second * second_unit)[:length], axis=0)
    grad_hidden = grad_summed + norm_back(second_scale, second_unit, gain_second, grad_second)
    grad_attn = grad_hidden.astype(jnp.bfloat16)
    grad_out = dense(grad_attn, branch, ((0,), (0,))).astype(jnp.bfloat16)
    grad_branch = dense(grad_attn, w_out, ((1,), (0,)))
    grad_mixed, grad_gate_pre, grad_gain_out = gated_pull(grad_branch)
    grad_gate_pre = grad_gate_pre.astype(jnp.bfloat16)
    grad_gate = dense(normed[:both], grad_gate_pre, ((0,), (0,))).astype(jnp.bfloat16)

    grad_rests = [grad_down, grad_up, grad_out, grad_gate]
    reduced = reduce_rest(
        [v.reshape(count, rows, v.shape[1]) for v in grad_rests],
        [third(v.shape[1], 0.28) for v in grad_rests],
    )

    split_mixed = grad_mixed.reshape(2, length, heads, DV)
    returning = jnp.einsum("jhtk,jthv->jhkv", reach, split_mixed, precision=precise)
    after = relay(mapping, returning, False)
    grad_q, grad_k, grad_v, grad_cols, grad_rows = delta_grads(
        queries, key_rows, values, cols, table, solve, update, back, entering,
        grad_mixed.reshape(2, length, vals), after,
    )
    grad_log = grad_cols[..., 0] - grad_rows[:, :, 0, :]
    grad_forget = jnp.swapaxes(lax.cumsum(grad_log, axis=2, reverse=True), 1, 2)
    grad_prepared = (grad_q, grad_k, grad_v, jnp.swapaxes(grad_cols[..., 1], 1, 2), grad_forget)
    grad_padded, grad_little, grad_conv, grad_decay_log, grad_decay_bias = local_pull(grad_prepared)
    grad_little = jnp.concatenate(
        [grad_little.reshape(both, 2 * heads), jnp.zeros((2 * PAD, 2 * heads), jnp.float32)], axis=0
    )
    rim_part = jnp.concatenate(
        [
            jnp.zeros((2, PAD - (CONV - 1), mixed_width), jnp.float32),
            grad_padded[:, : CONV - 1],
        ],
        axis=1,
    )
    grad_first = jnp.concatenate(
        [
            jnp.concatenate(
                [
                    grad_padded[:, CONV - 1 :].reshape(both, mixed_width),
                    rim_part.reshape(2 * PAD, mixed_width),
                ],
                axis=0,
            ),
            grad_little,
            jnp.zeros((both + 2 * PAD, 128 - 2 * heads), jnp.float32),
        ],
        axis=1,
    ).astype(jnp.bfloat16)
    grad_w_first = dense(normed, grad_first, ((0,), (0,))).astype(jnp.bfloat16)
    normed_part = dense(grad_first, w_first, ((1,), (1,)))
    normed_part = jnp.concatenate(
        [normed_part[:both] + dense(grad_gate_pre, w_gate, ((1,), (1,))), normed_part[both:]], axis=0
    )
    grad_gain_first = jnp.sum(normed_part * first_unit, axis=0)

    def place_half(array, start, width, values_):
        at = array.ndim - 1
        return lax.dynamic_update_slice_in_dim(array, values_, start + core * width, at)

    all_conv = jnp.zeros(conv_weight.shape, jnp.float32)
    all_conv = place_half(all_conv, 0, keys, grad_conv[:, :keys])
    all_conv = place_half(all_conv, KEYS, keys, grad_conv[:, keys : 2 * keys])
    all_conv = place_half(all_conv, 2 * KEYS, vals, grad_conv[:, 2 * keys :])
    no_heads = jnp.zeros((HEADS,), jnp.float32)
    smalls = [
        grad_gain_first,
        grad_gain_second,
        grad_gain_out,
        all_conv.reshape(-1),
        place_half(no_heads, 0, heads, grad_decay_log),
        place_half(no_heads, 0, heads, grad_decay_bias),
        loss_part[None],
        jnp.sum(mask_own)[None],
    ]
    sizes = [v.shape[0] for v in smalls]
    extra = -sum(sizes) % 1024
    packed = jnp.concatenate(smalls + [jnp.zeros((extra,), jnp.float32)]).reshape(-1, 128)
    total_first, other_first, swap_got, rim_got, small_sum = reduce_first(
        grad_w_first.reshape(count, rows, first_width),
        normed_part[length:both].astype(jnp.bfloat16),
        normed_part[both:].reshape(2, PAD, model).astype(jnp.bfloat16),
        packed,
        third(first_width, 0.28),
    )
    small_flat = small_sum.reshape(-1)
    found, start = [], 0
    for size in sizes:
        found.append(small_flat[start : start + size])
        start += size
    valid_count = jnp.maximum(found[7][0], 1.0)
    loss_value = found[6][0] / valid_count
    factor = length * groups * count / valid_count

    rim_rows = jnp.sum(rim_got.astype(jnp.float32), axis=0)
    grad_normed = normed_part[:length] + swap_got.astype(jnp.float32)
    grad_normed = jnp.concatenate(
        [grad_normed[: length - PAD], grad_normed[length - PAD :] + rim_rows], axis=0
    )
    grad_tokens = grad_hidden[:length] + norm_back(
        first_scale[:length], first_unit[:length], gain_first, grad_normed
    )

    def join(own, other, start, width):
        own_part, other_part = own[:, start : start + width], other[:, start : start + width]
        low = jnp.where(core == 0, own_part, other_part)
        high = jnp.where(core == 0, other_part, own_part)
        return [low, high]

    def joined(parts):
        return jnp.concatenate(parts, axis=1).astype(jnp.float32) * factor

    pair_first = (total_first, other_first)
    pair_down, pair_up, pair_out, pair_gate = ((reduced[i], reduced[4 + i]) for i in range(4))
    result_in = joined(
        join(*pair_first, 0, keys)
        + join(*pair_first, keys, keys)
        + join(*pair_first, 2 * keys, vals)
        + join(*pair_gate, 0, vals)
    )
    result_small = joined(
        join(*pair_first, mixed_width, heads) + join(*pair_first, mixed_width + heads, heads)
    )
    result_out = joined(join(*pair_out, 0, vals))
    result_up = joined(join(*pair_up, 0, FF // 2) + join(*pair_up, FF // 2, FF // 2))
    result_down = joined(join(*pair_down, 0, FF // 2))
    return (
        summed[:length].astype(jnp.bfloat16)[None],
        loss_value,
        (grad_tokens * factor)[None],
        result_in,
        result_small,
        result_out,
        result_up,
        result_down,
        found[0] * factor,
        found[1] * factor,
        found[2] * factor,
        found[3].reshape(conv_weight.shape) * factor,
        found[4] * factor,
        found[5] * factor,
    )


def solution(mesh):
    placed = (
        P("dp", "seq", None),
        P("dp", "seq", None),
        P("dp", "seq"),
        P("seq", None),
        P("seq", None),
        P("seq", None),
        P("seq", None),
        P("seq", None),
        P(),
        P(),
        P(),
        P(),
        P(),
        P(),
    )
    return jax.shard_map(
        on_device,
        mesh=mesh,
        in_specs=placed,
        out_specs=(
            P("dp", "seq", None),
            P(),
            P("dp", "seq", None),
            P("seq", None),
            P("seq", None),
            P("seq", None),
            P("seq", None),
            P("seq", None),
            P(),
            P(),
            P(),
            P(),
            P(),
            P(),
        ),
        check_vma=False,
    )
```

```python
import functools

import jax
import jax.numpy as jnp
from jax import lax
from jax.experimental import pallas as pl
from jax.experimental.pallas import tpu as pltpu
from jax.sharding import PartitionSpec as P

HEADS = 6
DK = 128
DV = 256
FF = 2816
CONV = 4
BLOCK = 64
KEYS = 768
VALUES = 1536


precise = lax.Precision.HIGHEST
epsilon = 1e-06


MESH = pl.DeviceIdType.MESH
NN = (((1,), (0,)), ((), ()))
NT = (((1,), (1,)), ((), ()))
TN = (((0,), (0,)), ((), ()))


def exact(left, right, dims=NN):
    return lax.dot_general(
        left, right, dims, precision=precise, preferred_element_type=jnp.float32
    )


def near(left, right, dims=NN):
    return lax.dot_general(
        left.astype(jnp.bfloat16),
        right.astype(jnp.bfloat16),
        dims,
        preferred_element_type=jnp.float32,
    )


def close(left, right, dims=NN):
    left_top, right_top = left.astype(jnp.bfloat16), right.astype(jnp.bfloat16)
    left_rest = (left - left_top.astype(jnp.float32)).astype(jnp.bfloat16)
    right_rest = (right - right_top.astype(jnp.float32)).astype(jnp.bfloat16)
    return (
        near(left_rest, right_top, dims) + near(left_top, right_rest, dims)
    ) + near(left_top, right_top, dims)


def iotas(rows, columns):
    return (
        lax.broadcasted_iota(jnp.int32, (rows, columns), 0),
        lax.broadcasted_iota(jnp.int32, (rows, columns), 1),
    )


def decay_table(gcol, grow):
    size = gcol.shape[0]
    row, col = iotas(size, size)
    keep = row >= col
    return jnp.where(keep, jnp.exp(jnp.where(keep, gcol - grow, 0.0)), 0.0)


def tile_start(start):
    return pl.multiple_of(start, 128)


class Place:
    def __init__(self, groups, count):
        self.groups, self.count, self.half = groups, count, count // 2
        self.group, self.place = lax.axis_index("dp"), lax.axis_index("seq")
        self.pair, self.side = self.place // 2, self.place % 2
        self.plane = (self.group // 2) % 2
        self.group_swap = self.group + 1 - 2 * (self.group % 2)
        self.across = self.group + 2 - 4 * self.plane
        self.beside = self.place + 1 - 2 * self.side

    def shard(self, pair, side):
        return 2 * pair + side

    def ahead(self, step):
        return lax.rem(self.pair + step, self.half)

    def behind(self, step):
        return lax.rem(self.pair + self.half - step, self.half)

    def partners(self):
        along = [(self.group, self.shard(self.ahead(step), self.side)) for step in range(1, self.half)]
        return along + [(self.group, self.beside), (self.across, self.place)]


def greet(signalled, awaited):
    barrier = pltpu.get_barrier_semaphore()
    for device in signalled:
        pl.semaphore_signal(barrier, inc=1, device_id=device, device_id_type=MESH)
    pl.semaphore_wait(barrier, awaited)


def remote(source, target, sends, receives, index, device):
    return pltpu.make_async_remote_copy(
        src_ref=source,
        dst_ref=target,
        send_sem=sends.at[index],
        recv_sem=receives.at[index],
        device_id=device,
        device_id_type=MESH,
    )


class Gather:
    def __init__(self, at, source, target, lines, share, sends, receives, local):
        self.at, self.source, self.target, self.lines = at, source, target, lines
        self.sends, self.receives, self.local = sends, receives, local
        width = source.shape[1]
        self.own = pl.ds(tile_start(at.plane * share), width - share)
        self.lent = pl.ds(tile_start(at.plane * (width - share)), share)
        self.borrowed = pl.ds(tile_start((1 - at.plane) * (width - share)), share)
        self.started = {}

    def copy(self, index, shard, columns, device, from_source=False):
        there = self.target.at[shard, self.lines, columns]
        here = self.source.at[self.lines, columns] if from_source else there
        return remote(here, there, self.sends, self.receives, index, device)

    def along(self, step):
        at = self.at
        device = (at.group, at.shard(at.ahead(step), at.side))
        return self.copy(step - 1, at.place, self.own, device, True)

    def beside(self, step):
        at = self.at
        shard = at.shard(at.behind(step), at.side)
        return self.copy(at.half - 1 + step, shard, self.own, (at.group, at.beside), step == 0)

    def across(self, step, side):
        at = self.at
        shard = at.shard(at.behind(step), at.side if side == 0 else 1 - at.side)
        return self.copy(2 * at.half - 1 + 2 * step + side - 1, shard, self.lent, (at.across, at.place))

    def keep(self):
        return pltpu.make_async_copy(
            self.source.at[self.lines], self.target.at[self.at.place, self.lines], self.local
        )

    def launch(self, make, *where):
        make(*where).start()
        self.started[make.__name__, where] = make

    def begin(self):
        self.keep().start()
        for step in range(1, self.at.half):
            self.launch(self.along, step)
        self.launch(self.beside, 0)

    def arrived(self, index, shard, columns):
        self.copy(index, shard, columns, (self.at.group, self.at.place)).wait_recv()

    def pass_along(self, step):
        at = self.at
        self.arrived(step - 1, at.shard(at.behind(step), at.side), self.own)
        self.launch(self.beside, step)
        self.launch(self.across, step, 0)

    def pass_beside(self, step):
        at = self.at
        self.arrived(at.half - 1 + step, at.shard(at.behind(step), 1 - at.side), self.own)
        self.launch(self.across, step, 1)

    def finish(self):
        at = self.at
        for step in range(at.half):
            for side in range(2):
                if step or side:
                    shard = at.shard(at.behind(step), at.side if side == 0 else 1 - at.side)
                    self.arrived(2 * at.half - 1 + 2 * step + side - 1, shard, self.borrowed)
        for (unused, where), make in self.started.items():
            make(*where).wait_send()
        self.keep().wait()

    def stages(self):
        half = self.at.half
        first = [functools.partial(self.pass_along, step) for step in range(1, half)]
        second = [functools.partial(self.pass_beside, step) for step in range(half)]
        return first, second


def copies_of_gather(count):
    return 2 * count - 2


def lagged(plans):
    depth = max(len(plan) for plan in plans)
    turns = []
    for turn in range(len(plans) + depth - 1):
        steps = []
        for index, plan in enumerate(plans):
            if 0 <= turn - index < len(plan):
                steps = plan[turn - index] + steps
        turns.append(steps)
    return turns


class Reduce:
    def __init__(self, at, given, total, other, lines, share, buffers, sems):
        self.at, self.given, self.total, self.other = at, given, total, other
        self.lines, self.share = lines, share
        self.acc, self.from_across, self.from_beside, self.from_along, self.part, self.from_plane, self.far = buffers
        self.sends, self.receives, self.local = sems
        width = total.shape[1]
        self.wide = width - share
        self.own = pl.ds(tile_start(at.plane * share), self.wide)
        self.lent = pl.ds(tile_start((1 - at.plane) * self.wide), share)
        self.inner = pl.ds(tile_start(at.plane * (width - 2 * share)), share)
        self.theirs = pl.ds(tile_start((1 - at.plane) * share), self.wide)
        self.started = {}

    def launch(self, make, *where):
        make(*where).start()
        self.started[make.__name__, where] = make

    def side(self, mine):
        return self.at.side if mine else 1 - self.at.side

    def across(self, mine):
        at = self.at
        return remote(
            self.given.at[:, self.side(mine), self.lines, self.lent], self.from_across.at[mine],
            self.sends, self.receives, mine, (at.across, at.place),
        )

    def load(self, mine):
        return pltpu.make_async_copy(
            self.given.at[:, self.side(mine), self.lines, self.own], self.acc.at[mine],
            self.local.at[mine],
        )

    def beside(self):
        at = self.at
        return remote(
            self.acc.at[0], self.from_beside, self.sends, self.receives, 2, (at.group, at.beside)
        )

    def along(self, step):
        at = self.at
        pair = at.ahead(step)
        return remote(
            self.acc.at[1, pair], self.from_along.at[step - 1],
            self.sends, self.receives, 4 + step, (at.group, at.shard(pair, at.side)),
        )

    def plane(self):
        at = self.at
        return remote(
            self.part, self.from_plane, self.sends, self.receives, 3, (at.across, at.place)
        )

    def core(self):
        at = self.at
        return remote(
            self.total.at[self.lines], self.other.at[self.lines], self.sends, self.receives,
            4, (at.group_swap, at.place),
        )

    def further(self, index, distance):
        at = self.at
        group = at.group + distance - 2 * distance * ((at.group // distance) % 2)
        return remote(
            self.total.at[self.lines], self.far.at[index], self.sends, self.receives,
            4 + at.half + index, (group, at.place),
        )

    def begin(self):
        for mine in range(2):
            self.load(mine).start()
            self.launch(self.across, mine)

    def add_across(self, mine):
        self.load(mine).wait()
        self.across(mine).wait_recv()
        held = self.acc[mine, :, :, self.inner].astype(jnp.float32)
        got = self.from_across[mine].astype(jnp.float32)
        self.acc[mine, :, :, self.inner] = (held + got).astype(jnp.bfloat16)
        if not mine:
            self.launch(self.beside)

    def add_beside(self):
        self.beside().wait_recv()
        for step in range(1, self.at.half + 1):
            pair = self.at.ahead(step)
            held = self.acc[1, pair].astype(jnp.float32)
            got = self.from_beside[pair].astype(jnp.float32)
            self.acc[1, pair] = (held + got).astype(jnp.bfloat16)
            if step < self.at.half:
                self.launch(self.along, step)

    def add_along(self):
        value = self.acc[1, self.at.pair].astype(jnp.float32)
        for step in range(1, self.at.half):
            self.along(step).wait_recv()
            value = value + self.from_along[step - 1].astype(jnp.float32)
        self.part[...] = value.astype(jnp.bfloat16)
        self.launch(self.plane)

    def add_plane(self):
        self.plane().wait_recv()
        height = self.part.shape[0]
        self.total[self.lines] = jnp.zeros((height, self.total.shape[1]), jnp.bfloat16)
        self.total[self.lines, self.own] = self.part[...]
        held = self.total[self.lines, self.theirs].astype(jnp.float32)
        got = self.from_plane[...].astype(jnp.float32)
        self.total[self.lines, self.theirs] = (held + got).astype(jnp.bfloat16)
        distance = 4
        while distance < self.at.groups:
            index = distance.bit_length() - 3
            copy = self.further(index, distance)
            copy.start()
            copy.wait()
            got = self.far[index].astype(jnp.float32)
            value = self.total[self.lines].astype(jnp.float32) + got
            self.total[self.lines] = value.astype(jnp.bfloat16)
            distance *= 2
        self.launch(self.core)

    def finish(self):
        self.core().wait_recv()
        for (unused, where), make in self.started.items():
            make(*where).wait_send()

    def stages(self):
        return [
            [functools.partial(self.add_across, 0)],
            [functools.partial(self.add_across, 1), self.add_beside],
            [self.add_along],
            [self.add_plane],
        ]


ANY = pl.BlockSpec(memory_space=pl.ANY)
ROOM = pl.BlockSpec(memory_space=pltpu.VMEM)
PAD = 16
CHUNKS, WINDOW = 4, 2
REDUCE_CHUNKS, REDUCE_WINDOW = 4, 2


def neighbours(at, step):
    place = lax.rem(at.place + at.count + step, at.count)
    return (at.group, place), (at.group_swap, place)


def chunks_of(rows):
    return max(1, min(CHUNKS, rows // 16))


def gather_sems(count, rows, number):
    chunks = chunks_of(rows)
    return [
        pltpu.SemaphoreType.DMA((number * chunks, copies_of_gather(count))),
        pltpu.SemaphoreType.DMA((number * chunks, copies_of_gather(count))),
        pltpu.SemaphoreType.DMA((number * chunks,)),
    ]


def gather_plans(at, sources, targets, shares, sends, receives, local):
    rows = sources[0].shape[0]
    chunks = chunks_of(rows)
    lines = rows // chunks
    return [
        Gather(
            at, sources[i], targets[i], pl.ds(part * lines, lines), shares[i],
            sends.at[i * chunks + part], receives.at[i * chunks + part], local.at[i * chunks + part],
        )
        for i in range(len(sources))
        for part in range(chunks)
    ]


def gather_steps(plans):
    steps = [plan.begin for plan in plans[:WINDOW]]
    for index, turn in enumerate(lagged([plan.stages() for plan in plans])):
        steps += turn
        if index + WINDOW < len(plans):
            steps.append(plans[index + WINDOW].begin)
    return steps + [plan.finish for plan in plans]


def reduce_steps(plans):
    steps = [plan.begin for plan in plans[:REDUCE_WINDOW]]
    for index, turn in enumerate(lagged([plan.stages() for plan in plans])):
        steps += turn
        if index + REDUCE_WINDOW < len(plans):
            steps.append(plans[index + REDUCE_WINDOW].begin)
    return steps + [plan.finish for plan in plans]


def gather_first_kernel(groups, count, share, *refs):
    source, tokens, target, mask = refs[:4]
    gathered, tokens_other, target_other, mask_other, rim = refs[4:9]
    sends, receives, local, swap_send, swap_recv = refs[9:]
    at = Place(groups, count)
    core = (at.group_swap, at.place)
    greet(at.partners() + [core] + list(neighbours(at, -1)), count // 2 + 4)
    swaps = [
        remote(here, there, swap_send, swap_recv, index, core)
        for index, (here, there) in enumerate(
            ((tokens, tokens_other), (target, target_other), (mask, mask_other))
        )
    ]
    length = tokens.shape[0]
    tail = tokens.at[pl.ds(length - PAD, PAD)]
    own_next, swap_next = neighbours(at, 1)
    rims = [
        remote(tail, rim.at[0], swap_send, swap_recv, 3, own_next),
        remote(tail, rim.at[1], swap_send, swap_recv, 4, swap_next),
    ]
    plans = gather_plans(at, [source], [gathered], [share], sends, receives, local)

    @pl.when(at.place < count - 1)
    def _():
        for copy in rims:
            copy.start()

    for copy in swaps:
        copy.start()
    for step in gather_steps(plans):
        step()
    for copy in swaps:
        copy.wait()

    @pl.when(at.place == 0)
    def _():
        rim[...] = jnp.zeros_like(rim)

    @pl.when(at.place > 0)
    def _():
        for copy in rims:
            copy.wait_recv()

    @pl.when(at.place < count - 1)
    def _():
        for copy in rims:
            copy.wait_send()


def gather_first(source, tokens, target, mask, share):
    groups, count = lax.axis_size("dp"), lax.axis_size("seq")
    rows, width = source.shape
    return pl.pallas_call(
        functools.partial(gather_first_kernel, groups, count, share),
        out_shape=[
            jax.ShapeDtypeStruct((count, rows, width), source.dtype),
            jax.ShapeDtypeStruct(tokens.shape, tokens.dtype),
            jax.ShapeDtypeStruct(target.shape, target.dtype),
            jax.ShapeDtypeStruct(mask.shape, mask.dtype),
            jax.ShapeDtypeStruct((2, PAD, tokens.shape[1]), tokens.dtype),
        ],
        in_specs=[ANY] * 4,
        out_specs=[ANY] * 4 + [ROOM],
        scratch_shapes=[
            *gather_sems(count, rows, 1),
            pltpu.SemaphoreType.DMA((5,)),
            pltpu.SemaphoreType.DMA((5,)),
        ],
        compiler_params=pltpu.CompilerParams(collective_id=3, has_side_effects=True),
        name="gather_first",
    )(source, tokens, target, mask)


def reduce_buffers(groups, count, rows, width, share):
    wide, half = width - share, count // 2
    steps = max(1, (groups // 4).bit_length() - 1)
    kind = jnp.bfloat16
    return [
        pltpu.VMEM((2, half, rows, wide), kind),
        pltpu.VMEM((2, half, rows, share), kind),
        pltpu.VMEM((half, rows, wide), kind),
        pltpu.VMEM((half - 1, rows, wide), kind),
        pltpu.VMEM((rows, wide), kind),
        pltpu.VMEM((rows, wide), kind),
        pltpu.VMEM((steps, rows, width), kind),
    ]


def copies_of_reduce(groups, count):
    return count // 2 + 4 + max(1, (groups // 4).bit_length() - 1)


def further_groups(at):
    found, distance = [], 4
    while distance < at.groups:
        found.append((at.group + distance - 2 * distance * ((at.group // distance) % 2), at.place))
        distance *= 2
    return found


def reduce_plans(at, givens, totals, others, shares, scratch):
    number, rows = len(shares), givens[0].shape[2]
    chunks = reduce_chunks(rows)
    lines = rows // chunks
    sends, receives, local = scratch[7 * number * chunks : 7 * number * chunks + 3]
    plans = []
    for i in range(number):
        for part in range(chunks):
            spot = i * chunks + part
            plans.append(
                Reduce(
                    at, givens[i], totals[i], others[i], pl.ds(part * lines, lines), shares[i],
                    scratch[7 * spot : 7 * spot + 7],
                    (sends.at[spot], receives.at[spot], local.at[spot]),
                )
            )
    return plans


def reduce_chunks(rows):
    return max(1, min(REDUCE_CHUNKS, rows // 16))


def reduce_scratch(groups, count, rows, widths, shares):
    scratch, chunks = [], reduce_chunks(rows)
    for width, share in zip(widths, shares):
        scratch += reduce_buffers(groups, count, rows // chunks, width, share) * chunks
    number, copies = len(widths) * chunks, copies_of_reduce(groups, count)
    return scratch + [
        pltpu.SemaphoreType.DMA((number, copies)),
        pltpu.SemaphoreType.DMA((number, copies)),
        pltpu.SemaphoreType.DMA((number, 2)),
    ]


class Relay:
    def __init__(self, at, forward, units, sending, arriving, sends, receives):
        self.at, self.units = at, units
        self.sending, self.arriving, self.sends, self.receives = sending, arriving, sends, receives
        last = at.count - 1
        step = 1 if forward else -1
        self.is_first = at.place == (0 if forward else last)
        self.is_last = at.place == (last if forward else 0)
        self.beyond = (at.group, lax.rem(at.place + at.count + step, at.count))
        self.before = (at.group, lax.rem(at.place + at.count - step, at.count))

    def copy(self, unit):
        return remote(
            self.sending.at[unit], self.arriving.at[unit], self.sends, self.receives, unit, self.beyond
        )

    def receive(self, unit, target):
        @pl.when(self.is_first)
        def _():
            target[unit] = jnp.zeros(target.shape[1:], jnp.float32)

        @pl.when(jnp.logical_not(self.is_first))
        def _():
            self.copy(unit).wait_recv()
            target[unit] = self.arriving[unit].astype(jnp.float32)

    def send(self, unit, value):
        @pl.when(jnp.logical_not(self.is_last))
        def _():
            self.sending[unit] = value().astype(jnp.bfloat16)
            self.copy(unit).start()

    def finish(self):
        @pl.when(jnp.logical_not(self.is_last))
        def _():
            for unit in range(self.units):
                self.copy(unit).wait_send()


def relay_scratch(units):
    return [
        pltpu.VMEM((units, DK, DV), jnp.bfloat16),
        pltpu.VMEM((units, DK, DV), jnp.bfloat16),
        pltpu.SemaphoreType.DMA((units,)),
        pltpu.SemaphoreType.DMA((units,)),
    ]


class Agenda:
    def __init__(self, steps):
        self.steps, self.done = steps, 0

    def take(self, upto):
        upto = max(upto, self.done)
        found, self.done = self.steps[self.done : upto], upto
        return found

    def until(self, share):
        for step in self.take(int(len(self.steps) * share)):
            step()

    def pieces(self, number, share):
        found = self.take(int(len(self.steps) * share))
        cuts = [len(found) * i // number for i in range(number + 1)]
        return [found[low:high] for low, high in zip(cuts, cuts[1:])]

    def loop(self, rounds, end, stage):
        pieces = self.pieces(rounds * PAUSES, end)
        taken = []

        def body(index, carry):
            for pause, unused in enumerate(stage(index)):
                taken.append(pause)
                for other in range(rounds):
                    found = pieces[other * PAUSES + pause]
                    if found:
                        pl.when(index == other)(functools.partial(run_steps, found))
            return carry

        lax.fori_loop(0, rounds, body, 0)
        assert len(taken) == PAUSES

    def around(self, count, turn, end, main):
        pieces = self.pieces(count, end)
        for index, found in enumerate(pieces):
            if found:
                pl.when(turn > index)(functools.partial(run_steps, found))
        main()
        for index, found in enumerate(pieces):
            if found:
                pl.when(turn <= index)(functools.partial(run_steps, found))


def run_steps(steps):
    for step in steps:
        step()


PAUSES = 9


def lockstep(stages):
    for unused in zip(*stages):
        yield


def rolled(value, shift):
    shift = shift % value.shape[0]
    return value if shift == 0 else pltpu.roll(value, shift, 0)


def silu_parts(value):
    gate = jax.nn.sigmoid(value)
    return value * gate, gate * (1.0 + value * (1.0 - gate))


class Unit:
    def __init__(self, seq, head, heads, mixed_ref, conv_ref):
        self.seq, self.head = seq, head
        self.mixed_ref, self.conv_ref = mixed_ref, conv_ref
        keys = heads * DK
        self.columns = [
            (self.head * DK, DK),
            (keys + self.head * DK, DK),
            (2 * keys + self.head * DV, DV),
        ]

    def taps(self, part):
        start, width = self.columns[part]
        span = pl.ds(start, width)
        field = self.mixed_ref[self.seq, :, span].astype(jnp.float32)
        weights = self.conv_ref[:, span]
        shifts = [rolled(field, CONV - 1 - tap)[PAD:] for tap in range(CONV)]
        value = weights[0:1] * shifts[0]
        for tap in range(1, CONV):
            value = value + weights[tap : tap + 1] * shifts[tap]
        return shifts, weights, value

    def rows(self, part):
        value = self.taps(part)[2]
        active = value * jax.nn.sigmoid(value)
        if part == 2:
            return active
        unit = active * lax.rsqrt(jnp.sum(active * active, axis=1, keepdims=True) + epsilon)
        return unit * DK ** (-0.5) if part == 0 else unit

    def taps_back(self, part, grad, grad_ref, conv_grad_ref):
        shifts, weights, value = self.taps(part)
        active, slope = silu_parts(value)
        if part < 2:
            scale = lax.rsqrt(jnp.sum(active * active, axis=1, keepdims=True) + epsilon)
            unit = active * scale
            grad = grad * DK ** (-0.5) if part == 0 else grad
            grad = scale * (grad - unit * jnp.sum(grad * unit, axis=1, keepdims=True))
        grad = grad * slope
        start, width = self.columns[part]
        span = pl.ds(start, width)
        row = lax.broadcasted_iota(jnp.int32, (8, width), 0)
        taps = jnp.zeros((8, width), jnp.float32)
        longer = jnp.concatenate([jnp.zeros((PAD, width), jnp.float32), grad], axis=0)
        total = jnp.zeros(longer.shape, jnp.float32)
        for tap in range(CONV):
            taps = taps + jnp.where(row == tap, jnp.sum(grad * shifts[tap], axis=0, keepdims=True), 0.0)
            total = total + weights[tap : tap + 1] * rolled(longer, tap - (CONV - 1))
        grad_ref[self.seq, :, span] = total.astype(jnp.bfloat16)
        conv_grad_ref[:, span] += taps


def head_tables(little_ref, head_ref, g_ref, grow_ref):
    seqs, size = little_ref.shape[0], g_ref.shape[1]
    row, col = iotas(size, size)
    below = (row >= col).astype(jnp.float32)
    above = (row <= col).astype(jnp.float32)
    for seq in range(seqs):
        forget = head_ref[0:1] * jax.nn.softplus(little_ref[seq, PAD:, :] + head_ref[1:2])
        g_ref[seq] = exact(below, forget)
        grow_ref[seq] = exact(forget, above, TN)


def head_columns(seq, head, heads, little_ref, g_ref, grow_ref):
    size = g_ref.shape[1]
    lane = lax.broadcasted_iota(jnp.int32, (size, 128), 1)
    line = lax.broadcasted_iota(jnp.int32, (128, size), 0)

    def column(table, index):
        return jnp.sum(jnp.where(lane == index, table, 0.0), axis=1, keepdims=True)

    beta = column(jax.nn.sigmoid(little_ref[seq, PAD:, :]), head)
    gcol = column(g_ref[seq], heads + head)
    grow = jnp.sum(jnp.where(line == heads + head, grow_ref[seq], 0.0), axis=0, keepdims=True)
    return beta, gcol, grow


def merged(inverses, systems, width):
    size = systems[0].shape[0]
    row, col = iotas(size, size)
    joined = (row // (2 * width) == col // (2 * width)) & (row // width != col // width)
    inner = [close(jnp.where(joined, system, 0.0), inverse) for system, inverse in zip(systems, inverses)]
    return [inverse - close(inverse, value) for inverse, value in zip(inverses, inner)]


def forward_kernel(groups, count, shares, *refs):
    number = len(shares)
    mixed_ref, little_ref, gate_ref, conv_ref, head_ref, gain_ref = refs[:6]
    sources, refs = refs[6 : 6 + number], refs[6 + number :]
    branch_ref, out_ref, t_ref, u_ref, w_ref, m_ref, e_ref, s_ref = refs[:8]
    targets, refs = refs[8 : 8 + number], refs[8 + number :]
    b_ref, g_ref, grow_ref, sending, arriving, relay_send, relay_recv = refs[:7]
    sends, receives, local = refs[7:]
    units = t_ref.shape[0]
    heads = units // 2
    size = t_ref.shape[1]
    half = size // 2
    at = Place(groups, count)
    line = Relay(at, True, units, sending, arriving, relay_send, relay_recv)
    greet(at.partners() + [line.before], count // 2 + 2)
    agenda = Agenda(gather_steps(gather_plans(at, sources, targets, shares, sends, receives, local)))
    for step in agenda.take(WINDOW):
        step()
    head_tables(little_ref, head_ref, g_ref, grow_ref)

    def local_stage(seq, head):
        unit = seq * heads + head
        own = Unit(seq, head, heads, mixed_ref, conv_ref)
        beta, gcol, grow = head_columns(seq, head, heads, little_ref, g_ref, grow_ref)
        decays = decay_table(gcol, grow)
        keys = own.rows(1)
        row, col = iotas(size, size)
        system = jnp.where(row > col, beta * close(keys, keys, NT) * decays, 0.0)
        yield
        systems = [system[:half, :half], system[half:, half:]]
        row, col = iotas(half, half)
        inverses = [
            (row == col).astype(jnp.float32) - jnp.where(row // 2 == col // 2, value, 0.0)
            for value in systems
        ]
        width = 2
        while width < half:
            inverses = merged(inverses, systems, width)
            width *= 2
            yield
        corner = -close(inverses[1], close(system[half:, :half], inverses[0]))
        t_ref[unit, :half, :half] = inverses[0]
        t_ref[unit, :half, half:] = jnp.zeros((half, half), jnp.float32)
        t_ref[unit, half:, :half] = corner
        t_ref[unit, half:, half:] = inverses[1]
        solve = t_ref[unit]
        growth = jnp.exp(gcol)
        last = gcol[size - 1 :, :]
        update = near(solve, beta * own.rows(2))
        back = near(solve, (beta * growth) * keys)
        u_ref[unit] = update
        w_ref[unit] = back
        yield
        weighted = keys * jnp.exp(last - gcol)
        drow, dcol = iotas(DK, DK)
        m_ref[unit] = jnp.where(drow == dcol, jnp.exp(last), 0.0) - near(weighted, back, TN)
        b_ref[unit] = near(weighted, update, TN)
        queries = own.rows(0)
        scores = near(queries, keys, NT) * decays
        out_ref[unit] = near(scores, update)
        e_ref[unit] = growth * queries - near(scores, back)
        yield

    agenda.loop(2, FORWARD_LOCAL, lambda seq: lockstep([local_stage(seq, h) for h in range(heads)]))

    def pass_on():
        for unit in range(units):
            line.receive(unit, s_ref)
            line.send(unit, lambda: close(m_ref[unit], s_ref[unit]) + b_ref[unit])

    agenda.around(count, at.place, FORWARD_RELAY, pass_on)

    def read_stage(seq, head):
        unit = seq * heads + head
        value = out_ref[unit] + near(e_ref[unit], s_ref[unit])
        out_ref[unit] = value
        span = pl.ds(head * DV, DV)
        scale = lax.rsqrt(jnp.mean(value * value, axis=1, keepdims=True) + epsilon)
        gate = gate_ref[seq, PAD:, span]
        branch = value * scale * gain_ref[...] * (gate * jax.nn.sigmoid(gate))
        branch_ref[seq, :, span] = branch.astype(jnp.bfloat16)

    for seq in range(2):
        for head in range(heads):
            read_stage(seq, head)
            agenda.until(
                FORWARD_RELAY + (1.0 - FORWARD_RELAY) * (seq * heads + head + 1) / units * 0.6
            )
    agenda.until(1.0)
    line.finish()


FORWARD_LOCAL, FORWARD_RELAY = 0.5, 0.8
BACK_OPEN, BACK_RELAY, BACK_GRADS = 0.15, 0.45, 0.85


def forward_block(mixed_in, little, gate_pre, conv, head, gain, sources, shares):
    groups, count = lax.axis_size("dp"), lax.axis_size("seq")
    number, rows = len(sources), sources[0].shape[0]
    length = mixed_in.shape[1] - PAD
    heads = conv.shape[1] // (2 * DK + DV)
    units = 2 * heads

    def table(*shape):
        return jax.ShapeDtypeStruct((units,) + shape, jnp.float32)

    return pl.pallas_call(
        functools.partial(forward_kernel, groups, count, shares),
        out_shape=[
            jax.ShapeDtypeStruct((2, length, heads * DV), jnp.bfloat16),
            table(length, DV),
            table(length, length),
            table(length, DV),
            table(length, DK),
            table(DK, DK),
            table(length, DK),
            table(DK, DV),
        ]
        + [jax.ShapeDtypeStruct((count,) + v.shape, v.dtype) for v in sources],
        in_specs=[ROOM] * 6 + [ANY] * number,
        out_specs=[ROOM] * 8 + [ANY] * number,
        scratch_shapes=[
            pltpu.VMEM((units, DK, DV), jnp.float32),
            pltpu.VMEM((2, length, 128), jnp.float32),
            pltpu.VMEM((2, 128, length), jnp.float32),
            *relay_scratch(units),
            *gather_sems(count, rows, number),
        ],
        compiler_params=pltpu.CompilerParams(
            collective_id=4, has_side_effects=True, vmem_limit_bytes=56 * 2**20
        ),
        name="forward_block",
    )(mixed_in, little, gate_pre, conv, head, gain, *sources)


def backward_kernel(groups, count, shares, *refs):
    number = len(shares)
    mixed_ref, little_ref, gate_ref, conv_ref, head_ref, gain_ref = refs[:6]
    out_ref, t_ref, u_ref, w_ref, m_ref, e_ref, s_ref, branch_ref = refs[6:14]
    givens, refs = refs[14 : 14 + number], refs[14 + number :]
    grad_ref, conv_grad, gain_grad, head_grad = refs[:4]
    totals, others = refs[4 : 4 + number], refs[4 + number : 4 + 2 * number]
    refs = refs[4 + 2 * number :]
    do_ref, c_ref, ds_ref, lit_ref, g_ref, grow_ref = refs[:6]
    sending, arriving, relay_send, relay_recv = refs[6:10]
    units = t_ref.shape[0]
    heads = units // 2
    size = t_ref.shape[1]
    mixed_width = mixed_ref.shape[2]
    at = Place(groups, count)
    line = Relay(at, False, units, sending, arriving, relay_send, relay_recv)
    further = further_groups(at)
    partners = at.partners() + [(at.group_swap, at.place)] + further + [line.before]
    greet(partners, count // 2 + 3 + len(further))
    plans = reduce_plans(at, givens, totals, others, shares, refs[10:])
    agenda = Agenda(reduce_steps(plans))
    for step in agenda.take(REDUCE_WINDOW):
        step()
    head_tables(little_ref, head_ref, g_ref, grow_ref)
    grad_ref[:, :PAD, mixed_width:] = jnp.zeros(
        (2, PAD, grad_ref.shape[2] - mixed_width), jnp.bfloat16
    )
    conv_grad[...] = jnp.zeros_like(conv_grad)
    gain_grad[...] = jnp.zeros_like(gain_grad)
    head_grad[...] = jnp.zeros_like(head_grad)
    lit_ref[...] = jnp.zeros_like(lit_ref)

    def gate_stage(seq, head):
        unit = seq * heads + head
        span = pl.ds(head * DV, DV)
        value = out_ref[unit]
        scale = lax.rsqrt(jnp.mean(value * value, axis=1, keepdims=True) + epsilon)
        normal = value * scale
        active, slope = silu_parts(gate_ref[seq, PAD:, span])
        grad = branch_ref[seq, :, span]
        gain = gain_ref[...]
        through = grad * active
        gain_grad[0:1] += jnp.sum(through * normal, axis=0, keepdims=True)
        gate_span = pl.ds(mixed_width + 128 + head * DV, DV)
        grad_ref[seq, PAD:, gate_span] = (grad * normal * gain * slope).astype(jnp.bfloat16)
        scaled = through * gain
        grad_out = scale * (scaled - normal * jnp.mean(scaled * normal, axis=1, keepdims=True))
        do_ref[unit] = grad_out
        c_ref[unit] = near(e_ref[unit], grad_out, TN)

    for seq in range(2):
        for head in range(heads):
            gate_stage(seq, head)
    agenda.until(BACK_OPEN)

    def pass_on():
        for unit in range(units):
            line.receive(unit, ds_ref)
            line.send(unit, lambda: close(m_ref[unit], ds_ref[unit], TN) + c_ref[unit])

    agenda.around(count, count - 1 - at.place, BACK_RELAY, pass_on)

    def grad_stage(seq, head):
        unit = seq * heads + head
        own = Unit(seq, head, heads, mixed_ref, conv_ref)
        beta, gcol, grow = head_columns(seq, head, heads, little_ref, g_ref, grow_ref)
        queries, keys, values = own.rows(0), own.rows(1), own.rows(2)
        decays = decay_table(gcol, grow)
        row, col = iotas(size, size)
        strict = row > col
        memory, after = s_ref[unit], ds_ref[unit]
        grad_out = do_ref[unit]
        growth = jnp.exp(gcol)
        last = gcol[size - 1 :, :]
        weights = jnp.exp(last - gcol)
        update = u_ref[unit] - near(w_ref[unit], memory)
        yield
        scores = near(queries, keys, NT) * decays
        keys_dot = jnp.where(strict, near(keys, keys, NT) * decays, 0.0)
        yield
        grad_update = near(scores, grad_out, TN) + near(keys * weights, after)
        yield
        grad_wanted = near(t_ref[unit], grad_update, TN)
        yield
        grad_system = -near(grad_wanted, update, NT)
        grad_scores = near(grad_out, update, NT)
        through = keys_dot * grad_system
        total = grad_scores * scores + beta * through
        yield
        query_part = growth * near(grad_out, memory, NT)
        key_read = growth * near(grad_wanted, memory, NT)
        key_part = beta * key_read
        end_part = weights * near(update, after, NT)
        yield
        grad_dot = grad_scores * decays
        grad_keys_dot = jnp.where(strict, grad_system * decays, 0.0) * beta
        grad_q = query_part + near(grad_dot, keys)
        grad_k = (
            end_part - key_part + near(grad_dot, queries, TN)
            + near(grad_keys_dot, keys) + near(grad_keys_dot, keys, TN)
        )
        yield
        own.taps_back(0, grad_q, grad_ref, conv_grad)
        own.taps_back(1, grad_k, grad_ref, conv_grad)
        own.taps_back(2, beta * grad_wanted, grad_ref, conv_grad)
        yield
        end_line = jnp.sum(keys * end_part, axis=1, keepdims=True)
        grad_beta = (
            jnp.sum(grad_wanted * values, axis=1, keepdims=True)
            - jnp.sum(keys * key_read, axis=1, keepdims=True)
            + jnp.sum(through, axis=1, keepdims=True)
        )
        grad_log = (
            jnp.sum(queries * query_part, axis=1, keepdims=True)
            - jnp.sum(keys * key_part, axis=1, keepdims=True)
            - end_line
            + jnp.sum(total, axis=1, keepdims=True)
        )
        grad_last = jnp.sum(end_line) + jnp.sum(
            jnp.exp(last) * jnp.sum(memory * after, axis=1, keepdims=True)
        )
        spot = lax.broadcasted_iota(jnp.int32, (size, 1), 0)
        grad_log = grad_log + jnp.where(spot == size - 1, grad_last, 0.0)
        later = (col >= row).astype(jnp.float32)
        lane = lax.broadcasted_iota(jnp.int32, (size, 128), 1)
        less = jnp.broadcast_to(jnp.sum(total, axis=0, keepdims=True), (128, size))
        grad_forget = exact(later, jnp.broadcast_to(grad_log, (size, 128))) - exact(later, less, NT)
        rate, bias = head_ref[0:1], head_ref[1:2]
        little = little_ref[own.seq, PAD:, :]
        on_forget = lane == heads + own.head
        grad_soft = jnp.where(on_forget, grad_forget * rate * jax.nn.sigmoid(little + bias), 0.0)
        forget = rate * jax.nn.softplus(little + bias)
        log_line = jnp.sum(jnp.where(on_forget, grad_forget * forget, 0.0), axis=0, keepdims=True)
        head_grad[0:1] += log_line
        head_grad[1:2] += jnp.sum(grad_soft, axis=0, keepdims=True)
        lit_ref[own.seq] += grad_soft + jnp.where(
            lane == own.head, grad_beta * beta * (1.0 - beta), 0.0
        )
        yield

    agenda.loop(2, BACK_GRADS, lambda seq: lockstep([grad_stage(seq, h) for h in range(heads)]))
    grad_ref[:, PAD:, mixed_width : mixed_width + 128] = lit_ref[...].astype(jnp.bfloat16)
    agenda.until(1.0)
    line.finish()


def backward_block(mixed_in, little, gate_pre, conv, head, gain, kept, grad_branch, givens, shares):
    groups, count = lax.axis_size("dp"), lax.axis_size("seq")
    number, rows = len(givens), givens[0].shape[2]
    length = mixed_in.shape[1] - PAD
    units = kept[0].shape[0]
    widths = [v.shape[3] for v in givens]
    results = [jax.ShapeDtypeStruct((rows, width), jnp.bfloat16) for width in widths]
    total_width = mixed_in.shape[2] + 128 + gate_pre.shape[2]
    return pl.pallas_call(
        functools.partial(backward_kernel, groups, count, shares),
        out_shape=[
            jax.ShapeDtypeStruct((2, length + PAD, total_width), jnp.bfloat16),
            jax.ShapeDtypeStruct(conv.shape, jnp.float32),
            jax.ShapeDtypeStruct((8, DV), jnp.float32),
            jax.ShapeDtypeStruct((8, 128), jnp.float32),
        ]
        + results * 2,
        in_specs=[ROOM] * 14 + [ANY] * number,
        out_specs=[ROOM] * (4 + 2 * number),
        scratch_shapes=[
            pltpu.VMEM((units, length, DV), jnp.float32),
            pltpu.VMEM((units, DK, DV), jnp.float32),
            pltpu.VMEM((units, DK, DV), jnp.float32),
            pltpu.VMEM((2, length, 128), jnp.float32),
            pltpu.VMEM((2, length, 128), jnp.float32),
            pltpu.VMEM((2, 128, length), jnp.float32),
            *relay_scratch(units),
            *reduce_scratch(groups, count, rows, widths, shares),
        ],
        compiler_params=pltpu.CompilerParams(
            collective_id=5, has_side_effects=True, vmem_limit_bytes=60 * 2**20
        ),
        name="backward_block",
    )(mixed_in, little, gate_pre, conv, head, gain, *kept, grad_branch, *givens)


def reduce_first_kernel(groups, count, share, *refs):
    given, swap, rims, small = refs[:4]
    total, other, swap_got, rim_got, small_sum = refs[4:9]
    scratch = refs[9:]
    small_got, small_hold, swap_send, swap_recv, small_send, small_recv = scratch[-6:]
    at = Place(groups, count)
    further = further_groups(at)
    core = (at.group_swap, at.place)
    stages = []
    distance = 1
    while distance < groups:
        stages.append((at.group + distance - 2 * distance * ((at.group // distance) % 2), at.place))
        distance *= 2
    distance = 1
    while distance < count:
        stages.append((at.group, at.place + distance - 2 * distance * ((at.place // distance) % 2)))
        distance *= 2
    partners = at.partners() + [core] + further + stages + list(neighbours(at, 1))
    greet(partners, count // 2 + 4 + len(further) + len(stages))
    own_back, swap_back = neighbours(at, -1)
    swapped = remote(swap, swap_got, swap_send, swap_recv, 0, core)
    rim_copies = [
        remote(rims.at[0], rim_got.at[0], swap_send, swap_recv, 1, own_back),
        remote(rims.at[1], rim_got.at[1], swap_send, swap_recv, 2, swap_back),
    ]
    plans = reduce_plans(at, [given], [total], [other], [share], scratch)
    steps = reduce_steps(plans)
    for step in steps[: min(REDUCE_WINDOW, len(plans))]:
        step()
    steps = steps[min(REDUCE_WINDOW, len(plans)) :]
    swapped.start()

    @pl.when(at.place > 0)
    def _():
        for copy in rim_copies:
            copy.start()

    small_hold[0] = small[...]

    def add_small(index):
        copy = remote(
            small_hold.at[index], small_got.at[index], small_send, small_recv, index, stages[index]
        )
        copy.start()
        copy.wait()
        small_hold[index + 1] = small_hold[index] + small_got[index]

    for index in range(max(len(steps), len(stages))):
        if index < len(steps):
            steps[index]()
        if index < len(stages):
            add_small(index)
    small_sum[...] = small_hold[len(stages)]
    swapped.wait()

    @pl.when(at.place == count - 1)
    def _():
        rim_got[...] = jnp.zeros_like(rim_got)

    @pl.when(at.place < count - 1)
    def _():
        for copy in rim_copies:
            copy.wait_recv()

    @pl.when(at.place > 0)
    def _():
        for copy in rim_copies:
            copy.wait_send()


def reduce_first(given, swap, rims, small, share):
    groups, count = lax.axis_size("dp"), lax.axis_size("seq")
    rows, width = given.shape[2:]
    rounds = (groups.bit_length() - 1) + (count.bit_length() - 1)
    result = jax.ShapeDtypeStruct((rows, width), jnp.bfloat16)
    return pl.pallas_call(
        functools.partial(reduce_first_kernel, groups, count, share),
        out_shape=[
            result,
            result,
            jax.ShapeDtypeStruct(swap.shape, swap.dtype),
            jax.ShapeDtypeStruct(rims.shape, rims.dtype),
            jax.ShapeDtypeStruct(small.shape, small.dtype),
        ],
        in_specs=[ANY, ROOM, ROOM, ROOM],
        out_specs=[ROOM] * 5,
        scratch_shapes=reduce_scratch(groups, count, rows, [width], [share])
        + [
            pltpu.VMEM((rounds,) + small.shape, jnp.float32),
            pltpu.VMEM((rounds + 1,) + small.shape, jnp.float32),
            pltpu.SemaphoreType.DMA((3,)),
            pltpu.SemaphoreType.DMA((3,)),
            pltpu.SemaphoreType.DMA((rounds,)),
            pltpu.SemaphoreType.DMA((rounds,)),
        ],
        compiler_params=pltpu.CompilerParams(
            collective_id=6, has_side_effects=True, vmem_limit_bytes=56 * 2**20
        ),
        name="reduce_first",
    )(given, swap, rims, small)


def third(width, weight):
    return 128 * max(1, round(width * weight / 128))


def norm_parts(field_in):
    scale = lax.rsqrt(jnp.mean(field_in * field_in, axis=-1, keepdims=True) + epsilon)
    return scale, field_in * scale


def norm_back(scale, unit, gain_vec, grad):
    scaled = grad * gain_vec
    return scale * (scaled - unit * jnp.mean(scaled * unit, axis=-1, keepdims=True))


def dense(left, right, dims):
    return lax.dot_general(left, right, (dims, ((), ())), preferred_element_type=jnp.float32)


def swiglu(gate_up):
    hidden_units = gate_up.shape[1] // 2
    return jax.nn.silu(gate_up[:, :hidden_units]) * gate_up[:, hidden_units:]


def on_device(
    tokens,
    target,
    valid,
    in_weight,
    small_weight,
    out_weight,
    ffn_in,
    ffn_out,
    gain_first,
    gain_second,
    gain_out,
    conv_weight,
    decay_log,
    decay_bias,
):
    count = lax.axis_size("seq")
    groups = lax.axis_size("dp")
    core = lax.axis_index("dp") % 2
    rows = in_weight.shape[0]
    length, model = tokens.shape[1], tokens.shape[2]
    both, padded = 2 * length, length + PAD
    heads = HEADS // 2
    keys, vals, inner = KEYS // 2, VALUES // 2, FF // 2
    mixed_width = 2 * keys + vals

    def mine(array, start, width):
        return lax.dynamic_slice_in_dim(array, start + core * width, width, array.ndim - 1)

    def qkv_half(array):
        parts = [mine(array, 0, keys), mine(array, KEYS, keys), mine(array, 2 * KEYS, vals)]
        return jnp.concatenate(parts, axis=1)

    small_half = [mine(small_weight, 0, heads), mine(small_weight, HEADS, heads)]
    spare = jnp.zeros((rows, 128 - 2 * heads), jnp.bfloat16)
    part_gate = mine(in_weight, 2 * KEYS + VALUES, vals)
    part_first = jnp.concatenate([qkv_half(in_weight)] + small_half + [spare, part_gate], axis=1)
    part_out = mine(out_weight, 0, vals)
    part_up = jnp.concatenate([mine(ffn_in, 0, inner), mine(ffn_in, FF, inner)], axis=1)
    part_down = mine(ffn_out, 0, inner)
    first_width = part_first.shape[1]

    mask_own = valid[0].astype(jnp.float32)
    mask_rows = jnp.broadcast_to(mask_own[None, :], (8, length))
    w_first, tokens_other, target_other, mask_other, rim = gather_first(
        part_first, tokens[0], target[0], mask_rows, third(first_width, 0.33)
    )
    w_first = w_first.reshape(model, first_width)

    inputs = jnp.concatenate([rim[0], tokens[0], rim[1], tokens_other], axis=0).astype(jnp.float32)
    first_scale, first_unit = norm_parts(inputs)
    normed = (first_unit * gain_first).astype(jnp.bfloat16)
    project = dense(normed, w_first, ((1,), (0,))).reshape(2, padded, first_width)
    mixed_in = project[..., :mixed_width].astype(jnp.bfloat16)
    little = project[..., mixed_width : mixed_width + 128]
    gate_pre = project[..., mixed_width + 128 :]

    own_conv = jnp.concatenate([qkv_half(conv_weight), jnp.zeros((8 - CONV, mixed_width))], axis=0)
    lanes = ((0, 0), (heads, 128 - 2 * heads))
    head = jnp.concatenate(
        [
            jnp.pad(-jnp.exp(mine(decay_log, 0, heads))[None], lanes),
            jnp.pad(mine(decay_bias, 0, heads)[None], lanes),
            jnp.zeros((6, 128), jnp.float32),
        ],
        axis=0,
    )
    gain_row = gain_out[None]
    rests = [part_out, part_up, part_down]
    branch, *kept, w_out, w_up, w_down = forward_block(
        mixed_in, little, gate_pre, own_conv, head, gain_row,
        rests, [third(v.shape[1], 0.33) for v in rests],
    )
    branch = branch.reshape(both, vals)
    w_out, w_up, w_down = (v.reshape(model, v.shape[2]) for v in (w_out, w_up, w_down))

    def core_sum(part):
        pairs = [(group, group ^ 1) for group in range(groups)]
        got = lax.ppermute(part.astype(jnp.bfloat16), "dp", pairs)
        return part + jnp.concatenate([got[length:], got[:length]], axis=0).astype(jnp.float32)

    positions = jnp.concatenate([tokens[0], tokens_other], axis=0).astype(jnp.float32)
    hidden = positions + core_sum(dense(branch, w_out, ((1,), (1,))))
    second_scale, second_unit = norm_parts(hidden)
    second = (second_unit * gain_second).astype(jnp.bfloat16)
    gate_up = dense(second, w_up, ((1,), (0,)))
    active_f, swiglu_pull = jax.vjp(swiglu, gate_up)
    active = active_f.astype(jnp.bfloat16)
    summed = hidden + core_sum(dense(active, w_down, ((1,), (1,))))
    mask = jnp.concatenate([mask_own, mask_other[0]])
    errors = summed - jnp.concatenate([target[0], target_other]).astype(jnp.float32)
    own_errors = errors[:length]
    loss_part = jnp.sum(mask_own * jnp.mean(own_errors * own_errors, axis=-1))

    grad_summed = mask[:, None] * errors
    grad_feed = grad_summed.astype(jnp.bfloat16)
    grad_active = dense(grad_feed, w_down, ((1,), (0,)))
    grad_down = dense(grad_feed, active, ((0,), (0,))).astype(jnp.bfloat16)
    grad_gate_up = swiglu_pull(grad_active)[0].astype(jnp.bfloat16)
    grad_up = dense(second, grad_gate_up, ((0,), (0,))).astype(jnp.bfloat16)
    grad_second = core_sum(dense(grad_gate_up, w_up, ((1,), (1,))))
    grad_gain_second = jnp.sum((grad_second * second_unit)[:length], axis=0)
    grad_hidden = grad_summed + norm_back(second_scale, second_unit, gain_second, grad_second)
    grad_attn = grad_hidden.astype(jnp.bfloat16)
    grad_out = dense(grad_attn, branch, ((0,), (0,))).astype(jnp.bfloat16)
    grad_branch = dense(grad_attn, w_out, ((1,), (0,))).reshape(2, length, vals)

    grad_rests = [grad_down, grad_up, grad_out]
    grad_first, grad_conv, grad_gain_out, grad_head, *reduced = backward_block(
        mixed_in, little, gate_pre, own_conv, head, gain_row, kept, grad_branch,
        [v.reshape(count // 2, 2, rows, v.shape[1]) for v in grad_rests],
        [third(v.shape[1], 0.28) for v in grad_rests],
    )
    grad_first = grad_first.reshape(2 * padded, first_width)
    grad_w_first = dense(normed, grad_first, ((0,), (0,))).astype(jnp.bfloat16)
    normed_part = dense(grad_first, w_first, ((1,), (1,)))
    grad_gain_first = jnp.sum(normed_part * first_unit, axis=0)
    normed_part = normed_part.reshape(2, padded, model)

    def place_half(array, start, width, values):
        at = array.ndim - 1
        return lax.dynamic_update_slice_in_dim(array, values, start + core * width, at)

    all_conv = jnp.zeros(conv_weight.shape, jnp.float32)
    all_conv = place_half(all_conv, 0, keys, grad_conv[:CONV, :keys])
    all_conv = place_half(all_conv, KEYS, keys, grad_conv[:CONV, keys : 2 * keys])
    all_conv = place_half(all_conv, 2 * KEYS, vals, grad_conv[:CONV, 2 * keys :])
    no_heads = jnp.zeros((HEADS,), jnp.float32)
    smalls = [
        grad_gain_first,
        grad_gain_second,
        grad_gain_out[0],
        all_conv.reshape(-1),
        place_half(no_heads, 0, heads, grad_head[0, heads : 2 * heads]),
        place_half(no_heads, 0, heads, grad_head[1, heads : 2 * heads]),
        loss_part[None],
        jnp.sum(mask_own)[None],
    ]
    sizes = [v.shape[0] for v in smalls]
    extra = -sum(sizes) % 1024
    packed = jnp.concatenate(smalls + [jnp.zeros((extra,), jnp.float32)]).reshape(-1, 128)
    total_first, other_first, swap_got, rim_got, small_sum = reduce_first(
        grad_w_first.reshape(count // 2, 2, rows, first_width),
        normed_part[1, PAD:].astype(jnp.bfloat16),
        normed_part[:, :PAD].astype(jnp.bfloat16),
        packed,
        third(first_width, 0.28),
    )
    small_flat = small_sum.reshape(-1)
    found, start = [], 0
    for size in sizes:
        found.append(small_flat[start : start + size])
        start += size
    valid_count = jnp.maximum(found[7][0], 1.0)
    loss_value = found[6][0] / valid_count
    factor = length * groups * count / valid_count

    rim_rows = jnp.sum(rim_got.astype(jnp.float32), axis=0)
    grad_normed = normed_part[0, PAD:] + swap_got.astype(jnp.float32)
    grad_normed = jnp.concatenate(
        [grad_normed[: length - PAD], grad_normed[length - PAD :] + rim_rows], axis=0
    )
    grad_tokens = grad_hidden[:length] + norm_back(
        first_scale[PAD:padded], first_unit[PAD:padded], gain_first, grad_normed
    )

    def join(own, other, start, width):
        own_part, other_part = own[:, start : start + width], other[:, start : start + width]
        low = jnp.where(core == 0, own_part, other_part)
        high = jnp.where(core == 0, other_part, own_part)
        return [low, high]

    def joined(parts):
        return jnp.concatenate(parts, axis=1).astype(jnp.float32) * factor

    pair_first = (total_first, other_first)
    pair_down, pair_up, pair_out = ((reduced[i], reduced[3 + i]) for i in range(3))
    result_in = joined(
        join(*pair_first, 0, keys)
        + join(*pair_first, keys, keys)
        + join(*pair_first, 2 * keys, vals)
        + join(*pair_first, mixed_width + 128, vals)
    )
    result_small = joined(
        join(*pair_first, mixed_width, heads) + join(*pair_first, mixed_width + heads, heads)
    )
    result_out = joined(join(*pair_out, 0, vals))
    result_up = joined(join(*pair_up, 0, inner) + join(*pair_up, inner, inner))
    result_down = joined(join(*pair_down, 0, inner))
    return (
        summed[:length].astype(jnp.bfloat16)[None],
        loss_value,
        (grad_tokens * factor)[None],
        result_in,
        result_small,
        result_out,
        result_up,
        result_down,
        found[0] * factor,
        found[1] * factor,
        found[2] * factor,
        found[3].reshape(conv_weight.shape) * factor,
        found[4] * factor,
        found[5] * factor,
    )


def solution(mesh):
    placed = (
        P("dp", "seq", None),
        P("dp", "seq", None),
        P("dp", "seq"),
        P("seq", None),
        P("seq", None),
        P("seq", None),
        P("seq", None),
        P("seq", None),
        P(),
        P(),
        P(),
        P(),
        P(),
        P(),
    )
    return jax.shard_map(
        on_device,
        mesh=mesh,
        in_specs=placed,
        out_specs=(
            P("dp", "seq", None),
            P(),
            P("dp", "seq", None),
            P("seq", None),
            P("seq", None),
            P("seq", None),
            P("seq", None),
            P("seq", None),
            P(),
            P(),
            P(),
            P(),
            P(),
            P(),
        ),
        check_vma=False,
    )
```

```python
import functools

import jax
import jax.numpy as jnp
from jax import lax
from jax.experimental import pallas as pl
from jax.experimental.pallas import tpu as pltpu
from jax.sharding import PartitionSpec as P

HEADS = 6
DK = 128
DV = 256
FF = 2816
CONV = 4
BLOCK = 64
KEYS = 768
VALUES = 1536


precise = lax.Precision.HIGHEST
epsilon = 1e-06


MESH = pl.DeviceIdType.MESH
NN = (((1,), (0,)), ((), ()))
NT = (((1,), (1,)), ((), ()))
TN = (((0,), (0,)), ((), ()))


def exact(left, right, dims=NN):
    return lax.dot_general(
        left, right, dims, precision=precise, preferred_element_type=jnp.float32
    )


def near(left, right, dims=NN):
    return lax.dot_general(
        left.astype(jnp.bfloat16),
        right.astype(jnp.bfloat16),
        dims,
        preferred_element_type=jnp.float32,
    )


def close(left, right, dims=NN):
    left_top, right_top = left.astype(jnp.bfloat16), right.astype(jnp.bfloat16)
    left_rest = (left - left_top.astype(jnp.float32)).astype(jnp.bfloat16)
    right_rest = (right - right_top.astype(jnp.float32)).astype(jnp.bfloat16)
    return (
        near(left_rest, right_top, dims) + near(left_top, right_rest, dims)
    ) + near(left_top, right_top, dims)


def iotas(rows, columns):
    return (
        lax.broadcasted_iota(jnp.int32, (rows, columns), 0),
        lax.broadcasted_iota(jnp.int32, (rows, columns), 1),
    )


def decay_table(gcol, grow):
    size = gcol.shape[0]
    row, col = iotas(size, size)
    keep = row >= col
    return jnp.where(keep, jnp.exp(jnp.where(keep, gcol - grow, 0.0)), 0.0)


def tile_start(start):
    return pl.multiple_of(start, 128)


class Place:
    def __init__(self, groups, count):
        self.groups, self.count, self.half = groups, count, count // 2
        self.group, self.place = lax.axis_index("dp"), lax.axis_index("seq")
        self.pair, self.side = self.place // 2, self.place % 2
        self.plane = (self.group // 2) % 2
        self.group_swap = self.group + 1 - 2 * (self.group % 2)
        self.across = self.group + 2 - 4 * self.plane
        self.beside = self.place + 1 - 2 * self.side

    def shard(self, pair, side):
        return 2 * pair + side

    def ahead(self, step):
        return lax.rem(self.pair + step, self.half)

    def behind(self, step):
        return lax.rem(self.pair + self.half - step, self.half)

    def partners(self):
        along = [(self.group, self.shard(self.ahead(step), self.side)) for step in range(1, self.half)]
        return along + [(self.group, self.beside), (self.across, self.place)]


def greet(signalled, awaited):
    barrier = pltpu.get_barrier_semaphore()
    for device in signalled:
        pl.semaphore_signal(barrier, inc=1, device_id=device, device_id_type=MESH)
    pl.semaphore_wait(barrier, awaited)


def remote(source, target, sends, receives, index, device):
    return pltpu.make_async_remote_copy(
        src_ref=source,
        dst_ref=target,
        send_sem=sends.at[index],
        recv_sem=receives.at[index],
        device_id=device,
        device_id_type=MESH,
    )


class Gather:
    def __init__(self, at, source, target, lines, share, sends, receives, local):
        self.at, self.source, self.target, self.lines = at, source, target, lines
        self.sends, self.receives, self.local = sends, receives, local
        width = source.shape[1]
        self.own = pl.ds(tile_start(at.plane * share), width - share)
        self.lent = pl.ds(tile_start(at.plane * (width - share)), share)
        self.borrowed = pl.ds(tile_start((1 - at.plane) * (width - share)), share)
        self.started = {}

    def copy(self, index, shard, columns, device, from_source=False):
        there = self.target.at[shard, self.lines, columns]
        here = self.source.at[self.lines, columns] if from_source else there
        return remote(here, there, self.sends, self.receives, index, device)

    def along(self, step):
        at = self.at
        device = (at.group, at.shard(at.ahead(step), at.side))
        return self.copy(step - 1, at.place, self.own, device, True)

    def beside(self, step):
        at = self.at
        shard = at.shard(at.behind(step), at.side)
        return self.copy(at.half - 1 + step, shard, self.own, (at.group, at.beside), step == 0)

    def across(self, step, side):
        at = self.at
        shard = at.shard(at.behind(step), at.side if side == 0 else 1 - at.side)
        return self.copy(2 * at.half - 1 + 2 * step + side - 1, shard, self.lent, (at.across, at.place))

    def keep(self):
        return pltpu.make_async_copy(
            self.source.at[self.lines], self.target.at[self.at.place, self.lines], self.local
        )

    def launch(self, make, *where):
        make(*where).start()
        self.started[make.__name__, where] = make

    def begin(self):
        self.keep().start()
        for step in range(1, self.at.half):
            self.launch(self.along, step)
        self.launch(self.beside, 0)

    def arrived(self, index, shard, columns):
        self.copy(index, shard, columns, (self.at.group, self.at.place)).wait_recv()

    def pass_along(self, step):
        at = self.at
        self.arrived(step - 1, at.shard(at.behind(step), at.side), self.own)
        self.launch(self.beside, step)
        self.launch(self.across, step, 0)

    def pass_beside(self, step):
        at = self.at
        self.arrived(at.half - 1 + step, at.shard(at.behind(step), 1 - at.side), self.own)
        self.launch(self.across, step, 1)

    def take_across(self):
        at = self.at
        for step in range(at.half):
            for side in range(2):
                if step or side:
                    shard = at.shard(at.behind(step), at.side if side == 0 else 1 - at.side)
                    self.arrived(2 * at.half - 1 + 2 * step + side - 1, shard, self.borrowed)
        self.keep().wait()

    def finish(self):
        for (unused, where), make in self.started.items():
            make(*where).wait_send()

    def stages(self):
        half = self.at.half
        first = [functools.partial(self.pass_along, step) for step in range(1, half)]
        second = [functools.partial(self.pass_beside, step) for step in range(half)]
        return [first, second, [self.take_across]]


def copies_of_gather(count):
    return 2 * count - 2


def lagged(plans, lag):
    depth = max(len(plan) for plan in plans)
    turns = []
    for turn in range(len(plans) + lag * (depth - 1)):
        steps = []
        for index, plan in enumerate(plans):
            stage, rest = divmod(turn - index, lag)
            if rest == 0 and 0 <= stage < len(plan):
                steps = plan[stage] + steps
        turns.append(steps)
    return turns


class Work:
    def __init__(self, given, base, width, share, spots):
        self.given, self.base, self.width, self.share, self.spots = given, base, width, share, spots


class Reduce:
    def __init__(self, at, work, lines, buffers, sems):
        self.at, self.given, self.spots, self.lines = at, work.given, work.spots, lines
        self.acc, self.from_across, self.from_beside, self.from_along = buffers[:4]
        self.part, self.from_plane, self.total, self.other, self.far = buffers[4:]
        self.sends, self.receives, self.local = sems
        width, share = work.width, work.share
        self.wide = width - share
        self.own = pl.ds(tile_start(at.plane * share), self.wide)
        self.given_own = pl.ds(tile_start(work.base + at.plane * share), self.wide)
        self.given_lent = pl.ds(tile_start(work.base + (1 - at.plane) * self.wide), share)
        self.inner = pl.ds(tile_start(at.plane * (width - 2 * share)), share)
        self.theirs = pl.ds(tile_start((1 - at.plane) * share), self.wide)
        self.started = {}

    def launch(self, make, *where):
        make(*where).start()
        self.started[make.__name__, where] = make

    def side(self, mine):
        return self.at.side if mine else 1 - self.at.side

    def across(self, mine):
        at = self.at
        return remote(
            self.given.at[:, self.side(mine), self.lines, self.given_lent], self.from_across.at[mine],
            self.sends, self.receives, mine, (at.across, at.place),
        )

    def load(self, mine):
        return pltpu.make_async_copy(
            self.given.at[:, self.side(mine), self.lines, self.given_own], self.acc.at[mine],
            self.local.at[mine],
        )

    def beside(self):
        at = self.at
        return remote(
            self.acc.at[0], self.from_beside, self.sends, self.receives, 2, (at.group, at.beside)
        )

    def along(self, step):
        at = self.at
        pair = at.ahead(step)
        return remote(
            self.acc.at[1, pair], self.from_along.at[step - 1],
            self.sends, self.receives, 4 + step, (at.group, at.shard(pair, at.side)),
        )

    def plane(self):
        at = self.at
        return remote(
            self.part, self.from_plane, self.sends, self.receives, 3, (at.across, at.place)
        )

    def core(self):
        at = self.at
        return remote(
            self.total, self.other, self.sends, self.receives, 4, (at.group_swap, at.place)
        )

    def further(self, index, distance):
        at = self.at
        group = at.group + distance - 2 * distance * ((at.group // distance) % 2)
        return remote(
            self.total, self.far.at[index], self.sends, self.receives,
            4 + at.half + index, (group, at.place),
        )

    def begin(self):
        for mine in range(2):
            self.load(mine).start()
            self.launch(self.across, mine)

    def add_across(self, mine):
        self.load(mine).wait()
        self.across(mine).wait_recv()
        held = self.acc[mine, :, :, self.inner].astype(jnp.float32)
        got = self.from_across[mine].astype(jnp.float32)
        self.acc[mine, :, :, self.inner] = (held + got).astype(jnp.bfloat16)
        if not mine:
            self.launch(self.beside)

    def add_beside(self):
        self.beside().wait_recv()
        for step in range(1, self.at.half + 1):
            pair = self.at.ahead(step)
            held = self.acc[1, pair].astype(jnp.float32)
            got = self.from_beside[pair].astype(jnp.float32)
            self.acc[1, pair] = (held + got).astype(jnp.bfloat16)
            if step < self.at.half:
                self.launch(self.along, step)

    def add_along(self):
        value = self.acc[1, self.at.pair].astype(jnp.float32)
        for step in range(1, self.at.half):
            self.along(step).wait_recv()
            value = value + self.from_along[step - 1].astype(jnp.float32)
        self.part[...] = value.astype(jnp.bfloat16)
        self.launch(self.plane)

    def add_plane(self):
        self.plane().wait_recv()
        self.total[...] = jnp.zeros_like(self.total)
        self.total[:, self.own] = self.part[...]
        held = self.total[:, self.theirs].astype(jnp.float32)
        got = self.from_plane[...].astype(jnp.float32)
        self.total[:, self.theirs] = (held + got).astype(jnp.bfloat16)
        distance = 4
        while distance < self.at.groups:
            index = distance.bit_length() - 3
            copy = self.further(index, distance)
            copy.start()
            copy.wait()
            got = self.far[index].astype(jnp.float32)
            self.total[...] = (self.total[...].astype(jnp.float32) + got).astype(jnp.bfloat16)
            distance *= 2
        self.launch(self.core)

    def deliver(self):
        self.core().wait_recv()
        core = self.at.group % 2
        for target, start, width, source in self.spots:
            for held, which in ((self.total, core), (self.other, 1 - core)):
                span = pl.ds(tile_start(start + which * width), width)
                target[self.lines, span] = held[:, source : source + width]

    def finish(self):
        for (unused, where), make in self.started.items():
            make(*where).wait_send()

    def stages(self):
        return [
            [functools.partial(self.add_across, 0)],
            [functools.partial(self.add_across, 1), self.add_beside],
            [self.add_along],
            [self.add_plane],
            [self.deliver],
        ]


ANY = pl.BlockSpec(memory_space=pl.ANY)
ROOM = pl.BlockSpec(memory_space=pltpu.VMEM)
PAD = 16
CHUNKS, WINDOW, GATHER_LAG = 4, 2, 1
REDUCE_CHUNKS, REDUCE_WINDOW, REDUCE_LAG = 4, 2, 1


def neighbours(at, step):
    place = lax.rem(at.place + at.count + step, at.count)
    return (at.group, place), (at.group_swap, place)


def chunks_of(rows):
    return max(1, min(CHUNKS, rows // 16))


def gather_sems(count, rows, number):
    chunks = chunks_of(rows)
    return [
        pltpu.SemaphoreType.DMA((number * chunks, copies_of_gather(count))),
        pltpu.SemaphoreType.DMA((number * chunks, copies_of_gather(count))),
        pltpu.SemaphoreType.DMA((number * chunks,)),
    ]


def gather_plans(at, sources, targets, shares, sends, receives, local):
    rows = sources[0].shape[0]
    chunks = chunks_of(rows)
    lines = rows // chunks
    return [
        Gather(
            at, sources[i], targets[i], pl.ds(part * lines, lines), shares[i],
            sends.at[i * chunks + part], receives.at[i * chunks + part], local.at[i * chunks + part],
        )
        for i in range(len(sources))
        for part in range(chunks)
    ]


def gather_steps(plans):
    steps = [plan.begin for plan in plans[:WINDOW]]
    for index, turn in enumerate(lagged([plan.stages() for plan in plans], GATHER_LAG)):
        steps += turn
        if index + WINDOW < len(plans):
            steps.append(plans[index + WINDOW].begin)
    return steps + [plan.finish for plan in plans]


def reduce_steps(plans):
    steps = [plan.begin for plan in plans[:REDUCE_WINDOW]]
    for index, turn in enumerate(lagged([plan.stages() for plan in plans], REDUCE_LAG)):
        steps += turn
        if index + REDUCE_WINDOW < len(plans):
            steps.append(plans[index + REDUCE_WINDOW].begin)
    return steps + [plan.finish for plan in plans]


def reduce_buffers(groups, count, rows, width, share):
    wide, half = width - share, count // 2
    kind = jnp.bfloat16
    far = (max(1, (groups // 4).bit_length() - 1), rows, width) if groups > 4 else (1, 16, 128)
    return [
        pltpu.VMEM((2, half, rows, wide), kind),
        pltpu.VMEM((2, half, rows, share), kind),
        pltpu.VMEM((half, rows, wide), kind),
        pltpu.VMEM((half - 1, rows, wide), kind),
        pltpu.VMEM((rows, wide), kind),
        pltpu.VMEM((rows, wide), kind),
        pltpu.VMEM((rows, width), kind),
        pltpu.VMEM((rows, width), kind),
        pltpu.VMEM(far, kind),
    ]


def copies_of_reduce(groups, count):
    return count // 2 + 4 + max(1, (groups // 4).bit_length() - 1)


def further_groups(at):
    found, distance = [], 4
    while distance < at.groups:
        found.append((at.group + distance - 2 * distance * ((at.group // distance) % 2), at.place))
        distance *= 2
    return found


def reduce_plans(at, works, scratch):
    rows = works[0].given.shape[2]
    chunks = reduce_chunks(rows)
    lines = rows // chunks
    sends, receives, local = scratch[9 * len(works) * chunks : 9 * len(works) * chunks + 3]
    plans = []
    for work in works:
        for part in range(chunks):
            spot = len(plans)
            plans.append(
                Reduce(
                    at, work, pl.ds(part * lines, lines), scratch[9 * spot : 9 * spot + 9],
                    (sends.at[spot], receives.at[spot], local.at[spot]),
                )
            )
    return plans


def reduce_chunks(rows):
    return max(1, min(REDUCE_CHUNKS, rows // 16))


def reduce_scratch(groups, count, rows, widths):
    scratch, chunks = [], reduce_chunks(rows)
    for width in widths:
        scratch += reduce_buffers(groups, count, rows // chunks, width, reduce_share(width)) * chunks
    number, copies = len(widths) * chunks, copies_of_reduce(groups, count)
    return scratch + [
        pltpu.SemaphoreType.DMA((number, copies)),
        pltpu.SemaphoreType.DMA((number, copies)),
        pltpu.SemaphoreType.DMA((number, 2)),
    ]


def reduce_share(width):
    return third(width, 0.28)


class Relay:
    def __init__(self, at, forward, units, sending, arriving, sends, receives):
        self.at, self.units = at, units
        self.sending, self.arriving, self.sends, self.receives = sending, arriving, sends, receives
        last = at.count - 1
        step = 1 if forward else -1
        self.is_first = at.place == (0 if forward else last)
        self.is_last = at.place == (last if forward else 0)
        self.beyond = (at.group, lax.rem(at.place + at.count + step, at.count))
        self.before = (at.group, lax.rem(at.place + at.count - step, at.count))

    def copy(self, unit):
        return remote(
            self.sending.at[unit], self.arriving.at[unit], self.sends, self.receives, unit, self.beyond
        )

    def receive(self, unit, target):
        @pl.when(self.is_first)
        def _():
            target[unit] = jnp.zeros(target.shape[1:], jnp.float32)

        @pl.when(jnp.logical_not(self.is_first))
        def _():
            self.copy(unit).wait_recv()
            target[unit] = self.arriving[unit].astype(jnp.float32)

    def send(self, unit, value):
        @pl.when(jnp.logical_not(self.is_last))
        def _():
            self.sending[unit] = value().astype(jnp.bfloat16)
            self.copy(unit).start()

    def finish(self):
        @pl.when(jnp.logical_not(self.is_last))
        def _():
            for unit in range(self.units):
                self.copy(unit).wait_send()


def relay_scratch(units):
    return [
        pltpu.VMEM((units, DK, DV), jnp.bfloat16),
        pltpu.VMEM((units, DK, DV), jnp.bfloat16),
        pltpu.SemaphoreType.DMA((units,)),
        pltpu.SemaphoreType.DMA((units,)),
    ]


class Agenda:
    def __init__(self, steps):
        self.steps, self.done = steps, 0

    def take(self, upto):
        upto = max(upto, self.done)
        found, self.done = self.steps[self.done : upto], upto
        return found

    def until(self, share):
        for step in self.take(int(len(self.steps) * share)):
            step()

    def pieces(self, number, share):
        found = self.take(int(len(self.steps) * share))
        cuts = [len(found) * i // number for i in range(number + 1)]
        return [found[low:high] for low, high in zip(cuts, cuts[1:])]

    def loop(self, rounds, end, stage):
        pieces = self.pieces(rounds * PAUSES, end)
        taken = []

        def body(index, carry):
            for pause, unused in enumerate(stage(index)):
                taken.append(pause)
                for other in range(rounds):
                    found = pieces[other * PAUSES + pause]
                    if found:
                        pl.when(index == other)(functools.partial(run_steps, found))
            return carry

        lax.fori_loop(0, rounds, body, 0)
        assert len(taken) == PAUSES

    def around(self, rounds, turn, end, stage, main):
        pieces = self.pieces(rounds, end)

        def body(index, carry):
            stage(index)
            for other, found in enumerate(pieces):
                if found:
                    pl.when(index == other)(functools.partial(run_steps, found))
            return carry

        split = jnp.minimum(turn, rounds)
        lax.fori_loop(0, split, body, 0)
        main()
        lax.fori_loop(split, rounds, body, 0)


def run_steps(steps):
    for step in steps:
        step()


PAUSES = 9


def lockstep(stages):
    for unused in zip(*stages):
        yield


def rolled(value, shift):
    shift = shift % value.shape[0]
    return value if shift == 0 else pltpu.roll(value, shift, 0)


def silu_parts(value):
    gate = jax.nn.sigmoid(value)
    return value * gate, gate * (1.0 + value * (1.0 - gate))


def lane_start(start):
    return start if isinstance(start, int) else tile_start(start)


class Unit:
    def __init__(self, seq, head, heads, mixed_ref, conv_ref):
        self.seq, self.head = seq, head
        self.mixed_ref, self.conv_ref = mixed_ref, conv_ref
        keys = heads * DK
        self.columns = [
            (lane_start(self.head * DK), DK),
            (lane_start(keys + self.head * DK), DK),
            (lane_start(2 * keys + self.head * DV), DV),
        ]

    def taps(self, part):
        start, width = self.columns[part]
        span = pl.ds(start, width)
        field = self.mixed_ref[self.seq, :, span].astype(jnp.float32)
        weights = self.conv_ref[:, span]
        shifts = [rolled(field, CONV - 1 - tap)[PAD:] for tap in range(CONV)]
        value = weights[0:1] * shifts[0]
        for tap in range(1, CONV):
            value = value + weights[tap : tap + 1] * shifts[tap]
        return shifts, weights, value

    def rows(self, part):
        value = self.taps(part)[2]
        active = value * jax.nn.sigmoid(value)
        if part == 2:
            return active
        unit = active * lax.rsqrt(jnp.sum(active * active, axis=1, keepdims=True) + epsilon)
        return unit * DK ** (-0.5) if part == 0 else unit

    def taps_back(self, part, grad, grad_ref, conv_grad_ref):
        shifts, weights, value = self.taps(part)
        active, slope = silu_parts(value)
        if part < 2:
            scale = lax.rsqrt(jnp.sum(active * active, axis=1, keepdims=True) + epsilon)
            unit = active * scale
            grad = grad * DK ** (-0.5) if part == 0 else grad
            grad = scale * (grad - unit * jnp.sum(grad * unit, axis=1, keepdims=True))
        grad = grad * slope
        start, width = self.columns[part]
        span = pl.ds(start, width)
        row = lax.broadcasted_iota(jnp.int32, (8, width), 0)
        taps = jnp.zeros((8, width), jnp.float32)
        longer = jnp.concatenate([jnp.zeros((PAD, width), jnp.float32), grad], axis=0)
        total = jnp.zeros(longer.shape, jnp.float32)
        for tap in range(CONV):
            taps = taps + jnp.where(row == tap, jnp.sum(grad * shifts[tap], axis=0, keepdims=True), 0.0)
            total = total + weights[tap : tap + 1] * rolled(longer, tap - (CONV - 1))
        grad_ref[self.seq, :, span] = total.astype(jnp.bfloat16)
        conv_grad_ref[:, span] += taps


def head_tables(little_ref, head_ref, g_ref, grow_ref):
    seqs, size = little_ref.shape[0], g_ref.shape[1]
    row, col = iotas(size, size)
    below = (row >= col).astype(jnp.float32)
    above = (row <= col).astype(jnp.float32)
    for seq in range(seqs):
        forget = head_ref[0:1] * jax.nn.softplus(little_ref[seq, PAD:, :] + head_ref[1:2])
        g_ref[seq] = exact(below, forget)
        grow_ref[seq] = exact(forget, above, TN)


def head_columns(seq, head, heads, little_ref, g_ref, grow_ref):
    size = g_ref.shape[1]
    lane = lax.broadcasted_iota(jnp.int32, (size, 128), 1)
    line = lax.broadcasted_iota(jnp.int32, (128, size), 0)

    def column(table, index):
        return jnp.sum(jnp.where(lane == index, table, 0.0), axis=1, keepdims=True)

    beta = column(jax.nn.sigmoid(little_ref[seq, PAD:, :]), head)
    gcol = column(g_ref[seq], heads + head)
    grow = jnp.sum(jnp.where(line == heads + head, grow_ref[seq], 0.0), axis=0, keepdims=True)
    return beta, gcol, grow


def merged(inverses, systems, width):
    size = systems[0].shape[0]
    row, col = iotas(size, size)
    joined = (row // (2 * width) == col // (2 * width)) & (row // width != col // width)
    inner = [close(jnp.where(joined, system, 0.0), inverse) for system, inverse in zip(systems, inverses)]
    return [inverse - close(inverse, value) for inverse, value in zip(inverses, inner)]


def forward_kernel(groups, count, shares, *refs):
    number = len(shares)
    tokens_ref, target_ref, mask_ref, norm_ref, conv_ref, head_ref, gain_ref = refs[:7]
    sources, refs = refs[7 : 7 + number], refs[7 + number :]
    inputs_ref, target_other, mask_other, mixed_ref, little_ref, gate_ref = refs[:6]
    branch_ref, out_ref, t_ref, u_ref, w_ref, m_ref, e_ref, s_ref = refs[6:14]
    targets, refs = refs[14 : 14 + number], refs[14 + number :]
    normed, b_ref, g_ref, grow_ref, sending, arriving, relay_send, relay_recv = refs[:8]
    swap_send, swap_recv, sends, receives, local = refs[8:]
    units = t_ref.shape[0]
    heads = units // 2
    size = t_ref.shape[1]
    half = size // 2
    at = Place(groups, count)
    line = Relay(at, True, units, sending, arriving, relay_send, relay_recv)
    core = (at.group_swap, at.place)
    greet(at.partners() + [line.before, core] + list(neighbours(at, -1)), count // 2 + 5)
    padded = size + PAD
    swaps = [
        remote(here, there, swap_send, swap_recv, index, core)
        for index, (here, there) in enumerate((
            (tokens_ref, inputs_ref.at[pl.ds(padded + PAD, size)]),
            (target_ref, target_other),
            (mask_ref, mask_other),
        ))
    ]
    tail = tokens_ref.at[pl.ds(size - PAD, PAD)]
    own_next, swap_next = neighbours(at, 1)
    rims = [
        remote(tail, inputs_ref.at[pl.ds(0, PAD)], swap_send, swap_recv, 3, own_next),
        remote(tail, inputs_ref.at[pl.ds(padded, PAD)], swap_send, swap_recv, 4, swap_next),
    ]
    swaps[0].start()

    @pl.when(at.place < count - 1)
    def _():
        for copy in rims:
            copy.start()

    plans = gather_plans(at, sources, targets, shares, sends, receives, local)
    agenda = Agenda(gather_steps(plans))
    run_steps(agenda.take(WINDOW))
    for copy in swaps[1:]:
        copy.start()
    inputs_ref[PAD:padded] = tokens_ref[...]

    @pl.when(at.place == 0)
    def _():
        inputs_ref[:PAD] = jnp.zeros((PAD, inputs_ref.shape[1]), jnp.bfloat16)
        inputs_ref[padded : padded + PAD] = jnp.zeros((PAD, inputs_ref.shape[1]), jnp.bfloat16)

    @pl.when(at.place > 0)
    def _():
        for copy in rims:
            copy.wait_recv()

    swaps[0].wait()
    for seq in range(2):
        value = inputs_ref[seq * padded : (seq + 1) * padded].astype(jnp.float32)
        scale = lax.rsqrt(jnp.mean(value * value, axis=1, keepdims=True) + epsilon)
        normed[seq * padded : (seq + 1) * padded] = (value * scale * norm_ref[...]).astype(jnp.bfloat16)
    first_chunks = len(plans) // number
    run_steps(agenda.take(agenda.steps.index(plans[first_chunks - 1].take_across) + 1))

    weight = targets[0]
    model = normed.shape[1]
    mixed_width = mixed_ref.shape[2]
    cuts = [0, mixed_width // 2, mixed_width, mixed_width + 128, weight.shape[2]]
    for start, end in zip(cuts, cuts[1:]):
        value = dense(normed[...], weight[:, :, start:end].reshape(model, end - start), ((1,), (0,)))
        value = value.reshape(2, padded, end - start)
        if end <= mixed_width:
            mixed_ref[:, :, start:end] = value.astype(jnp.bfloat16)
        elif end == mixed_width + 128:
            little_ref[...] = value
        else:
            gate_ref[...] = value
        agenda.until(agenda.done / len(agenda.steps) + FORWARD_PROJECT / 4)
    head_tables(little_ref, head_ref, g_ref, grow_ref)

    def local_stage(seq, head):
        unit = seq * heads + head
        own = Unit(seq, head, heads, mixed_ref, conv_ref)
        beta, gcol, grow = head_columns(seq, head, heads, little_ref, g_ref, grow_ref)
        decays = decay_table(gcol, grow)
        keys = own.rows(1)
        row, col = iotas(size, size)
        system = jnp.where(row > col, beta * close(keys, keys, NT) * decays, 0.0)
        yield
        systems = [system[:half, :half], system[half:, half:]]
        row, col = iotas(half, half)
        inverses = [
            (row == col).astype(jnp.float32) - jnp.where(row // 2 == col // 2, value, 0.0)
            for value in systems
        ]
        width = 2
        while width < half:
            inverses = merged(inverses, systems, width)
            width *= 2
            yield
        corner = -close(inverses[1], close(system[half:, :half], inverses[0]))
        t_ref[unit, :half, :half] = inverses[0]
        t_ref[unit, :half, half:] = jnp.zeros((half, half), jnp.float32)
        t_ref[unit, half:, :half] = corner
        t_ref[unit, half:, half:] = inverses[1]
        solve = t_ref[unit]
        growth = jnp.exp(gcol)
        last = gcol[size - 1 :, :]
        update = near(solve, beta * own.rows(2))
        back = near(solve, (beta * growth) * keys)
        u_ref[unit] = update
        w_ref[unit] = back
        yield
        weighted = keys * jnp.exp(last - gcol)
        drow, dcol = iotas(DK, DK)
        m_ref[unit] = jnp.where(drow == dcol, jnp.exp(last), 0.0) - near(weighted, back, TN)
        b_ref[unit] = near(weighted, update, TN)
        yield

    agenda.loop(2, FORWARD_LOCAL, lambda seq: lockstep([local_stage(seq, h) for h in range(heads)]))

    def pass_on():
        for unit in range(units):
            line.receive(unit, s_ref)
            line.send(unit, lambda: close(m_ref[unit], s_ref[unit]) + b_ref[unit])

    def score_stage(unit):
        seq, head = unit // heads, unit % heads
        own = Unit(seq, head, heads, mixed_ref, conv_ref)
        unused, gcol, grow = head_columns(seq, head, heads, little_ref, g_ref, grow_ref)
        queries = own.rows(0)
        scores = near(queries, own.rows(1), NT) * decay_table(gcol, grow)
        out_ref[unit] = near(scores, u_ref[unit])
        e_ref[unit] = jnp.exp(gcol) * queries - near(scores, w_ref[unit])

    agenda.around(units, at.place, FORWARD_RELAY, score_stage, pass_on)

    def read_stage(seq, head):
        unit = seq * heads + head
        value = out_ref[unit] + near(e_ref[unit], s_ref[unit])
        out_ref[unit] = value
        span = pl.ds(head * DV, DV)
        scale = lax.rsqrt(jnp.mean(value * value, axis=1, keepdims=True) + epsilon)
        gate = gate_ref[seq, PAD:, span]
        branch = value * scale * gain_ref[...] * (gate * jax.nn.sigmoid(gate))
        branch_ref[seq, :, span] = branch.astype(jnp.bfloat16)

    for seq in range(2):
        for head in range(heads):
            read_stage(seq, head)
            agenda.until(
                FORWARD_RELAY + (FORWARD_READ - FORWARD_RELAY) * (seq * heads + head + 1) / units
            )
    agenda.until(1.0)
    line.finish()
    for copy in swaps[1:]:
        copy.wait()

    @pl.when(at.place < count - 1)
    def _():
        for copy in rims:
            copy.wait_send()


FORWARD_PROJECT, FORWARD_LOCAL, FORWARD_RELAY, FORWARD_READ = 0.04, 0.65, 0.85, 0.92
BACK_OPEN, BACK_RELAY, BACK_GRADS = 0.15, 0.45, 0.85


def forward_block(tokens, target, mask, norm_gain, conv, head, gain, sources, shares):
    groups, count = lax.axis_size("dp"), lax.axis_size("seq")
    number, rows = len(sources), sources[0].shape[0]
    length, model = tokens.shape
    mixed_width = conv.shape[1]
    heads = mixed_width // (2 * DK + DV)
    units = 2 * heads
    padded = length + PAD

    def table(*shape):
        return jax.ShapeDtypeStruct((units,) + shape, jnp.float32)

    return pl.pallas_call(
        functools.partial(forward_kernel, groups, count, shares),
        out_shape=[
            jax.ShapeDtypeStruct((2 * padded, model), tokens.dtype),
            jax.ShapeDtypeStruct(target.shape, target.dtype),
            jax.ShapeDtypeStruct(mask.shape, mask.dtype),
            jax.ShapeDtypeStruct((2, padded, mixed_width), jnp.bfloat16),
            jax.ShapeDtypeStruct((2, padded, 128), jnp.float32),
            jax.ShapeDtypeStruct((2, padded, heads * DV), jnp.float32),
            jax.ShapeDtypeStruct((2, length, heads * DV), jnp.bfloat16),
            table(length, DV),
            table(length, length),
            table(length, DV),
            table(length, DK),
            table(DK, DK),
            table(length, DK),
            table(DK, DV),
        ]
        + [jax.ShapeDtypeStruct((count,) + v.shape, v.dtype) for v in sources],
        in_specs=[ROOM, ANY, ANY] + [ROOM] * 4 + [ANY] * number,
        out_specs=[ROOM, ANY, ANY] + [ROOM] * 11 + [ROOM] + [ANY] * (number - 1),
        scratch_shapes=[
            pltpu.VMEM((2 * padded, model), jnp.bfloat16),
            pltpu.VMEM((units, DK, DV), jnp.float32),
            pltpu.VMEM((2, length, 128), jnp.float32),
            pltpu.VMEM((2, 128, length), jnp.float32),
            *relay_scratch(units),
            pltpu.SemaphoreType.DMA((5,)),
            pltpu.SemaphoreType.DMA((5,)),
            *gather_sems(count, rows, number),
        ],
        compiler_params=pltpu.CompilerParams(
            collective_id=3, has_side_effects=True, vmem_limit_bytes=56 * 2**20
        ),
        name="forward_block",
    )(tokens, target, mask, norm_gain, conv, head, gain, *sources)


def backward_kernel(groups, count, inner, *refs):
    mixed_ref, little_ref, gate_ref, conv_ref, head_ref, gain_ref = refs[:6]
    out_ref, t_ref, u_ref, w_ref, m_ref, e_ref, s_ref, branch_ref = refs[6:14]
    down_ref, up_ref, out_grad = refs[14:17]
    grad_ref, conv_grad, gain_grad, head_grad, down_sum, gate_sum, out_sum = refs[17:24]
    refs = refs[24:]
    do_ref, c_ref, ds_ref, lit_ref, g_ref, grow_ref = refs[:6]
    x_ref, ahead_ref, k_ref, log_ref, less_ref = refs[6:11]
    sending, arriving, relay_send, relay_recv = refs[11:15]
    units = t_ref.shape[0]
    heads = units // 2
    size = t_ref.shape[1]
    mixed_width, vals = mixed_ref.shape[2], branch_ref.shape[2]
    at = Place(groups, count)
    line = Relay(at, False, units, sending, arriving, relay_send, relay_recv)
    further = further_groups(at)
    partners = at.partners() + [(at.group_swap, at.place)] + further + [line.before]
    greet(partners, count // 2 + 3 + len(further))
    works = [
        Work(down_ref, 0, inner, reduce_share(inner), [(down_sum, 0, inner, 0)]),
        Work(up_ref, 0, inner, reduce_share(inner), [(gate_sum, 0, inner, 0)]),
        Work(out_grad, 0, vals, reduce_share(vals), [(out_sum, 0, vals, 0)]),
    ]
    plans = reduce_plans(at, works, refs[15:])
    agenda = Agenda(reduce_steps(plans))
    for step in agenda.take(REDUCE_WINDOW):
        step()
    head_tables(little_ref, head_ref, g_ref, grow_ref)
    grad_ref[:, :PAD, mixed_width:] = jnp.zeros(
        (2, PAD, grad_ref.shape[2] - mixed_width), jnp.bfloat16
    )
    conv_grad[...] = jnp.zeros_like(conv_grad)
    gain_grad[...] = jnp.zeros_like(gain_grad)
    head_grad[...] = jnp.zeros_like(head_grad)
    lit_ref[...] = jnp.zeros_like(lit_ref)
    log_ref[...] = jnp.zeros_like(log_ref)

    def gate_stage(seq, head):
        unit = seq * heads + head
        span = pl.ds(head * DV, DV)
        value = out_ref[unit]
        scale = lax.rsqrt(jnp.mean(value * value, axis=1, keepdims=True) + epsilon)
        normal = value * scale
        active, slope = silu_parts(gate_ref[seq, PAD:, span])
        grad = branch_ref[seq, :, span]
        gain = gain_ref[...]
        through = grad * active
        gain_grad[0:1] += jnp.sum(through * normal, axis=0, keepdims=True)
        gate_span = pl.ds(mixed_width + 128 + head * DV, DV)
        grad_ref[seq, PAD:, gate_span] = (grad * normal * gain * slope).astype(jnp.bfloat16)
        scaled = through * gain
        grad_out = scale * (scaled - normal * jnp.mean(scaled * normal, axis=1, keepdims=True))
        do_ref[unit] = grad_out
        c_ref[unit] = near(e_ref[unit], grad_out, TN)

    for seq in range(2):
        for head in range(heads):
            gate_stage(seq, head)
    agenda.until(BACK_OPEN)

    def pass_on():
        for unit in range(units):
            line.receive(unit, ds_ref)
            line.send(unit, lambda: close(m_ref[unit], ds_ref[unit], TN) + c_ref[unit])

    def score_stage(unit):
        seq, head = unit // heads, unit % heads
        own = Unit(seq, head, heads, mixed_ref, conv_ref)
        unused, gcol, grow = head_columns(seq, head, heads, little_ref, g_ref, grow_ref)
        queries, keys = own.rows(0), own.rows(1)
        decays = decay_table(gcol, grow)
        memory, grad_out = s_ref[unit], do_ref[unit]
        update = u_ref[unit] - near(w_ref[unit], memory)
        x_ref[unit] = update.astype(jnp.bfloat16)
        scores = near(queries, keys, NT) * decays
        ahead_ref[unit] = near(scores, grad_out, TN)
        grad_scores = near(grad_out, update, NT)
        total = grad_scores * scores
        query_part = jnp.exp(gcol) * near(grad_out, memory, NT)
        grad_dot = grad_scores * decays
        own.taps_back(0, query_part + near(grad_dot, keys), grad_ref, conv_grad)
        k_ref[unit] = near(grad_dot, queries, TN)
        lane = lax.broadcasted_iota(jnp.int32, (size, 128), 1)
        log_line = jnp.sum(queries * query_part, axis=1, keepdims=True) + jnp.sum(
            total, axis=1, keepdims=True
        )
        log_ref[seq] += jnp.where(lane == head, log_line, 0.0)
        less_ref[unit] = jnp.broadcast_to(jnp.sum(total, axis=0, keepdims=True), (8, size))

    agenda.around(units, count - 1 - at.place, BACK_RELAY, score_stage, pass_on)

    def grad_stage(seq, head):
        unit = seq * heads + head
        own = Unit(seq, head, heads, mixed_ref, conv_ref)
        beta, gcol, grow = head_columns(seq, head, heads, little_ref, g_ref, grow_ref)
        keys, values = own.rows(1), own.rows(2)
        decays = decay_table(gcol, grow)
        row, col = iotas(size, size)
        strict = row > col
        memory, after = s_ref[unit], ds_ref[unit]
        growth = jnp.exp(gcol)
        last = gcol[size - 1 :, :]
        weights = jnp.exp(last - gcol)
        update = x_ref[unit]
        yield
        keys_dot = jnp.where(strict, near(keys, keys, NT) * decays, 0.0)
        grad_update = ahead_ref[unit] + near(keys * weights, after)
        yield
        grad_wanted = near(t_ref[unit], grad_update, TN)
        yield
        grad_system = -near(grad_wanted, update, NT)
        through = keys_dot * grad_system
        total = beta * through
        yield
        key_read = growth * near(grad_wanted, memory, NT)
        key_part = beta * key_read
        end_part = weights * near(update, after, NT)
        yield
        grad_keys_dot = jnp.where(strict, grad_system * decays, 0.0) * beta
        grad_k = (
            end_part - key_part + k_ref[unit]
            + near(grad_keys_dot, keys) + near(grad_keys_dot, keys, TN)
        )
        yield
        own.taps_back(1, grad_k, grad_ref, conv_grad)
        yield
        own.taps_back(2, beta * grad_wanted, grad_ref, conv_grad)
        yield
        end_line = jnp.sum(keys * end_part, axis=1, keepdims=True)
        grad_beta = (
            jnp.sum(grad_wanted * values, axis=1, keepdims=True)
            - jnp.sum(keys * key_read, axis=1, keepdims=True)
            + jnp.sum(through, axis=1, keepdims=True)
        )
        lane = lax.broadcasted_iota(jnp.int32, (size, 128), 1)
        grad_log = (
            jnp.sum(jnp.where(lane == head, log_ref[seq], 0.0), axis=1, keepdims=True)
            - jnp.sum(keys * key_part, axis=1, keepdims=True)
            - end_line
            + jnp.sum(total, axis=1, keepdims=True)
        )
        grad_last = jnp.sum(end_line) + jnp.sum(
            jnp.exp(last) * jnp.sum(memory * after, axis=1, keepdims=True)
        )
        spot = lax.broadcasted_iota(jnp.int32, (size, 1), 0)
        grad_log = grad_log + jnp.where(spot == size - 1, grad_last, 0.0)
        later = (col >= row).astype(jnp.float32)
        less = jnp.sum(total, axis=0, keepdims=True) + less_ref[unit][0:1]
        less = jnp.broadcast_to(less, (128, size))
        grad_forget = exact(later, jnp.broadcast_to(grad_log, (size, 128))) - exact(later, less, NT)
        rate, bias = head_ref[0:1], head_ref[1:2]
        little = little_ref[own.seq, PAD:, :]
        on_forget = lane == heads + own.head
        grad_soft = jnp.where(on_forget, grad_forget * rate * jax.nn.sigmoid(little + bias), 0.0)
        forget = rate * jax.nn.softplus(little + bias)
        log_total = jnp.sum(jnp.where(on_forget, grad_forget * forget, 0.0), axis=0, keepdims=True)
        head_grad[0:1] += log_total
        head_grad[1:2] += jnp.sum(grad_soft, axis=0, keepdims=True)
        lit_ref[own.seq] += grad_soft + jnp.where(
            lane == own.head, grad_beta * beta * (1.0 - beta), 0.0
        )
        yield

    agenda.loop(2, BACK_GRADS, lambda seq: lockstep([grad_stage(seq, h) for h in range(heads)]))
    grad_ref[:, PAD:, mixed_width : mixed_width + 128] = lit_ref[...].astype(jnp.bfloat16)
    agenda.until(1.0)
    line.finish()


def backward_block(mixed_in, little, gate_pre, conv, head, gain, kept, grad_branch, grad_down, grad_up, grad_out):
    groups, count = lax.axis_size("dp"), lax.axis_size("seq")
    rows, inner = grad_down.shape[2:]
    length = mixed_in.shape[1] - PAD
    units = kept[0].shape[0]
    vals = gate_pre.shape[2]
    total_width = mixed_in.shape[2] + 128 + vals
    joined = jax.ShapeDtypeStruct((rows, 2 * inner), jnp.bfloat16)
    return pl.pallas_call(
        functools.partial(backward_kernel, groups, count, inner),
        out_shape=[
            jax.ShapeDtypeStruct((2, length + PAD, total_width), jnp.bfloat16),
            jax.ShapeDtypeStruct(conv.shape, jnp.float32),
            jax.ShapeDtypeStruct((8, DV), jnp.float32),
            jax.ShapeDtypeStruct((8, 128), jnp.float32),
            joined,
            joined,
            jax.ShapeDtypeStruct((rows, 2 * vals), jnp.bfloat16),
        ],
        in_specs=[ROOM] * 14 + [ANY] * 3,
        out_specs=[ROOM] * 7,
        scratch_shapes=[
            pltpu.VMEM((units, length, DV), jnp.float32),
            pltpu.VMEM((units, DK, DV), jnp.float32),
            pltpu.VMEM((units, DK, DV), jnp.float32),
            pltpu.VMEM((2, length, 128), jnp.float32),
            pltpu.VMEM((2, length, 128), jnp.float32),
            pltpu.VMEM((2, 128, length), jnp.float32),
            pltpu.VMEM((units, length, DV), jnp.bfloat16),
            pltpu.VMEM((units, length, DV), jnp.float32),
            pltpu.VMEM((units, length, DK), jnp.float32),
            pltpu.VMEM((2, length, 128), jnp.float32),
            pltpu.VMEM((units, 8, length), jnp.float32),
            *relay_scratch(units),
            *reduce_scratch(groups, count, rows, [inner, inner, vals]),
        ],
        compiler_params=pltpu.CompilerParams(
            collective_id=5, has_side_effects=True, vmem_limit_bytes=60 * 2**20
        ),
        name="backward_block",
    )(mixed_in, little, gate_pre, conv, head, gain, *kept, grad_branch, grad_down, grad_up, grad_out)


def final_kernel(groups, count, widths, *refs):
    keys, vals, inner = widths
    tokens_ref, gain_ref, first_ref, weight_ref, hidden_ref = refs[:5]
    conv_grad, gain_grad, head_grad, second_grad, loss_ref = refs[5:10]
    up_ref = refs[10]
    token_grad, small_sum, up_sum, in_sum, little_sum = refs[11:16]
    normed, wide_grad, part_ref, weight, given = refs[16:21]
    swap, swap_got, rims, rim_got, small_got, small_hold = refs[21:27]
    weight_sem, swap_send, swap_recv, small_send, small_recv = refs[27:32]
    at = Place(groups, count)
    core = at.group % 2
    further = further_groups(at)
    pair = (at.group_swap, at.place)
    rounds, distance = [], 1
    while distance < groups:
        rounds.append((at.group + distance - 2 * distance * ((at.group // distance) % 2), at.place))
        distance *= 2
    distance = 1
    while distance < count:
        rounds.append((at.group, at.place + distance - 2 * distance * ((at.place // distance) % 2)))
        distance *= 2
    partners = at.partners() + [pair] + further + rounds + list(neighbours(at, 1))
    greet(partners, count // 2 + 4 + len(further) + len(rounds))

    mixed = 2 * keys + vals
    first_width = first_ref.shape[1]
    works = [
        Work(up_ref, inner, inner, reduce_share(inner), [(up_sum, 0, inner, 0)]),
        Work(
            given, 0, first_width, reduce_share(first_width),
            [
                (in_sum, 0, keys, 0),
                (in_sum, 2 * keys, keys, keys),
                (in_sum, 4 * keys, vals, 2 * keys),
                (little_sum, 0, 128, mixed),
                (in_sum, 4 * keys + 2 * vals, vals, mixed + 128),
            ],
        ),
    ]
    plans = reduce_plans(at, works, refs[32:])
    chunks = len(plans) // len(works)
    agenda = Agenda(reduce_steps(plans))
    opening = agenda.steps.index(plans[chunks].begin)
    run_steps(agenda.take(REDUCE_WINDOW))
    fetch = pltpu.make_async_copy(weight_ref, weight, weight_sem)
    fetch.start()

    gain = gain_ref[...]

    def norm_rows(first, number):
        value = tokens_ref[first : first + number].astype(jnp.float32)
        scale = lax.rsqrt(jnp.mean(value * value, axis=1, keepdims=True) + epsilon)
        return scale, value * scale

    height = tokens_ref.shape[0]
    for first in range(0, height, height // 2):
        normed[first : first + height // 2] = (norm_rows(first, height // 2)[1] * gain).astype(jnp.bfloat16)
    half, unused, rows, unused = given.shape
    blocks = [(start, min(640, first_width - start)) for start in range(0, first_width, 640)]
    for index, (start, width) in enumerate(blocks):
        wide_grad[:, :width] = dense(
            normed[...], first_ref[:, start : start + width], ((0,), (0,))
        ).astype(jnp.bfloat16)
        for place in range(2 * half):
            given[place // 2, place % 2, :, start : start + width] = wide_grad[
                place * rows : (place + 1) * rows, :width
            ]
        run_steps(agenda.take(opening * FINAL_BLOCKS * (index + 1) // (100 * len(blocks))))
    fetch.wait()
    model = tokens_ref.shape[1]
    for start in range(0, model, model // 4):
        part_ref[:, start : start + model // 4] = dense(
            first_ref[...], weight[start : start + model // 4], ((1,), (1,))
        )
        run_steps(agenda.take(
            opening * (FINAL_BLOCKS + (100 - FINAL_BLOCKS) * (start + model // 4) // model) // 100
        ))
    length = height // 2 - PAD
    swap[...] = part_ref[length + 2 * PAD :].astype(jnp.bfloat16)
    rims[0] = part_ref[:PAD].astype(jnp.bfloat16)
    rims[1] = part_ref[length + PAD : length + 2 * PAD].astype(jnp.bfloat16)
    own_back, swap_back = neighbours(at, -1)
    swapped = remote(swap, swap_got, swap_send, swap_recv, 0, pair)
    rim_copies = [
        remote(rims.at[0], rim_got.at[0], swap_send, swap_recv, 1, own_back),
        remote(rims.at[1], rim_got.at[1], swap_send, swap_recv, 2, swap_back),
    ]
    swapped.start()

    @pl.when(at.place > 0)
    def _():
        for copy in rim_copies:
            copy.start()

    gain_first = jnp.zeros((1, model), jnp.float32)
    for first in range(0, height, height // 2):
        unit = norm_rows(first, height // 2)[1]
        product = unit * part_ref[first : first + height // 2]
        gain_first = gain_first + jnp.sum(product, axis=0, keepdims=True)
    small_hold[0] = jnp.zeros(small_hold.shape[1:], jnp.float32)
    for start, width, source in ((0, keys, 0), (2 * keys, keys, keys), (4 * keys, vals, 2 * keys)):
        span = pl.ds(tile_start(start + core * width), width)
        small_hold[0, 0:CONV, span] = conv_grad[0:CONV, source : source + width]
    small_hold[0, 4:5, 0:model] = gain_first
    small_hold[0, 4:5, model : 2 * model] = second_grad[...]
    small_hold[0, 4:5, 2 * model : 2 * model + DV] = gain_grad[0:1]
    heads = keys // DK
    for line in range(2):
        found = head_grad[line : line + 1]
        moved = pltpu.roll(head_grad[...], 128 - heads, 1)[line : line + 1]
        small_hold[0, 5:6, 128 * line : 128 * line + 128] = jnp.where(core == 0, moved, found)
    small_hold[0, 5:6, 256:384] = loss_ref[...]

    def add_small(index):
        return remote(
            small_hold.at[index], small_got.at[index], small_send, small_recv, index, rounds[index]
        )

    left = agenda.pieces(len(rounds) + 1, 1.0)
    for index, found in enumerate(left):
        if index > 0:
            add_small(index - 1).wait()
            small_hold[index] = small_hold[index - 1] + small_got[index - 1]
        if index < len(rounds):
            add_small(index).start()
        if index == 1:
            swapped.wait()

            @pl.when(at.place == count - 1)
            def _():
                rim_got[...] = jnp.zeros_like(rim_got)

            @pl.when(at.place < count - 1)
            def _():
                for copy in rim_copies:
                    copy.wait_recv()

            edge = rim_got[0].astype(jnp.float32) + rim_got[1].astype(jnp.float32)
            step = length // 4
            for first in range(0, length, step):
                scale, unit = norm_rows(PAD + first, step)
                grad = part_ref[PAD + first : PAD + first + step] + swap_got[
                    first : first + step
                ].astype(jnp.float32)
                if first + step == length:
                    grad = jnp.concatenate([grad[: step - PAD], grad[step - PAD :] + edge], axis=0)
                scaled = grad * gain
                back = scale * (scaled - unit * jnp.mean(scaled * unit, axis=1, keepdims=True))
                token_grad[first : first + step] = hidden_ref[first : first + step] + back
        run_steps(found)
    small_sum[...] = small_hold[len(rounds)]

    @pl.when(at.place > 0)
    def _():
        for copy in rim_copies:
            copy.wait_send()


FINAL_BLOCKS = 60


def final_block(
    inputs, gain, grad_first, w_first, grad_hidden, grad_conv, grad_gain, grad_head, grad_second,
    loss_row, grad_up, vals,
):
    groups, count = lax.axis_size("dp"), lax.axis_size("seq")
    rows = grad_up.shape[2]
    inner = grad_up.shape[3] // 2
    first_width = grad_first.shape[1]
    keys = (first_width - 128 - 2 * vals) // 2
    height, model = inputs.shape
    length = height // 2 - PAD
    rounds = (groups.bit_length() - 1) + (count.bit_length() - 1)
    small = (8, 4 * keys + 2 * vals)
    kind = jnp.bfloat16

    def joined(width):
        return jax.ShapeDtypeStruct((rows, width), kind)

    return pl.pallas_call(
        functools.partial(final_kernel, groups, count, (keys, vals, inner)),
        out_shape=[
            jax.ShapeDtypeStruct((length, model), jnp.float32),
            jax.ShapeDtypeStruct(small, jnp.float32),
            joined(2 * inner),
            joined(4 * keys + 4 * vals),
            joined(256),
        ],
        in_specs=[ROOM] * 3 + [ANY] + [ROOM] * 6 + [ANY],
        out_specs=[ROOM] * 5,
        scratch_shapes=[
            pltpu.VMEM((height, model), kind),
            pltpu.VMEM((model, 640), kind),
            pltpu.VMEM((height, model), jnp.float32),
            pltpu.VMEM((model, first_width), kind),
            pltpu.VMEM((count // 2, 2, rows, first_width), kind),
            pltpu.VMEM((length, model), kind),
            pltpu.VMEM((length, model), kind),
            pltpu.VMEM((2, PAD, model), kind),
            pltpu.VMEM((2, PAD, model), kind),
            pltpu.VMEM((rounds,) + small, jnp.float32),
            pltpu.VMEM((rounds + 1,) + small, jnp.float32),
            pltpu.SemaphoreType.DMA,
            pltpu.SemaphoreType.DMA((3,)),
            pltpu.SemaphoreType.DMA((3,)),
            pltpu.SemaphoreType.DMA((rounds,)),
            pltpu.SemaphoreType.DMA((rounds,)),
            *reduce_scratch(groups, count, rows, [inner, first_width]),
        ],
        compiler_params=pltpu.CompilerParams(
            collective_id=6, has_side_effects=True, vmem_limit_bytes=60 * 2**20
        ),
        name="final_block",
    )(
        inputs, gain, grad_first, w_first, grad_hidden, grad_conv, grad_gain, grad_head,
        grad_second, loss_row, grad_up,
    )


def third(width, weight):
    return 128 * max(1, round(width * weight / 128))


def norm_parts(field_in):
    scale = lax.rsqrt(jnp.mean(field_in * field_in, axis=-1, keepdims=True) + epsilon)
    return scale, field_in * scale


def norm_back(scale, unit, gain_vec, grad):
    scaled = grad * gain_vec
    return scale * (scaled - unit * jnp.mean(scaled * unit, axis=-1, keepdims=True))


def dense(left, right, dims):
    return lax.dot_general(left, right, (dims, ((), ())), preferred_element_type=jnp.float32)


def swiglu(gate_up):
    hidden_units = gate_up.shape[1] // 2
    return jax.nn.silu(gate_up[:, :hidden_units]) * gate_up[:, hidden_units:]


def on_device(
    tokens,
    target,
    valid,
    in_weight,
    small_weight,
    out_weight,
    ffn_in,
    ffn_out,
    gain_first,
    gain_second,
    gain_out,
    conv_weight,
    decay_log,
    decay_bias,
):
    count = lax.axis_size("seq")
    groups = lax.axis_size("dp")
    core = lax.axis_index("dp") % 2
    rows = in_weight.shape[0]
    length, model = tokens.shape[1], tokens.shape[2]
    both, padded = 2 * length, length + PAD
    heads = HEADS // 2
    keys, vals, inner = KEYS // 2, VALUES // 2, FF // 2
    mixed_width = 2 * keys + vals

    def mine(array, start, width):
        return lax.dynamic_slice_in_dim(array, start + core * width, width, array.ndim - 1)

    def qkv_half(array):
        parts = [mine(array, 0, keys), mine(array, KEYS, keys), mine(array, 2 * KEYS, vals)]
        return jnp.concatenate(parts, axis=1)

    small_half = [mine(small_weight, 0, heads), mine(small_weight, HEADS, heads)]
    spare = jnp.zeros((rows, 128 - 2 * heads), jnp.bfloat16)
    part_gate = mine(in_weight, 2 * KEYS + VALUES, vals)
    part_first = jnp.concatenate([qkv_half(in_weight)] + small_half + [spare, part_gate], axis=1)
    part_out = mine(out_weight, 0, vals)
    part_up = jnp.concatenate([mine(ffn_in, 0, inner), mine(ffn_in, FF, inner)], axis=1)
    part_down = mine(ffn_out, 0, inner)
    first_width = part_first.shape[1]

    mask_own = valid[0].astype(jnp.float32)
    mask_rows = jnp.broadcast_to(mask_own[None, :], (8, length))
    own_conv = jnp.concatenate([qkv_half(conv_weight), jnp.zeros((8 - CONV, mixed_width))], axis=0)
    lanes = ((0, 0), (heads, 128 - 2 * heads))
    head = jnp.concatenate(
        [
            jnp.pad(-jnp.exp(mine(decay_log, 0, heads))[None], lanes),
            jnp.pad(mine(decay_bias, 0, heads)[None], lanes),
            jnp.zeros((6, 128), jnp.float32),
        ],
        axis=0,
    )
    gain_row = gain_out[None]
    parts = [part_first, part_out, part_up, part_down]
    (
        inputs, target_other, mask_other, mixed_in, little, gate_pre, branch, *kept,
        w_first, w_out, w_up, w_down,
    ) = forward_block(
        tokens[0], target[0], mask_rows, gain_first[None], own_conv, head, gain_row,
        parts, [third(v.shape[1], 0.33) for v in parts],
    )
    branch = branch.reshape(both, vals)
    w_first, w_out, w_up, w_down = (
        v.reshape(model, v.shape[2]) for v in (w_first, w_out, w_up, w_down)
    )

    def core_sum(part):
        pairs = [(group, group ^ 1) for group in range(groups)]
        got = lax.ppermute(part.astype(jnp.bfloat16), "dp", pairs)
        return part + jnp.concatenate([got[length:], got[:length]], axis=0).astype(jnp.float32)

    positions = jnp.concatenate([tokens[0], inputs[padded + PAD :]], axis=0).astype(jnp.float32)
    hidden = positions + core_sum(dense(branch, w_out, ((1,), (1,))))
    second_scale, second_unit = norm_parts(hidden)
    second = (second_unit * gain_second).astype(jnp.bfloat16)
    gate_up = dense(second, w_up, ((1,), (0,)))
    active_f, swiglu_pull = jax.vjp(swiglu, gate_up)
    active = active_f.astype(jnp.bfloat16)
    summed = hidden + core_sum(dense(active, w_down, ((1,), (1,))))
    mask = jnp.concatenate([mask_own, mask_other[0]])
    errors = summed - jnp.concatenate([target[0], target_other]).astype(jnp.float32)
    own_errors = errors[:length]
    loss_part = jnp.sum(mask_own * jnp.mean(own_errors * own_errors, axis=-1))

    grad_summed = mask[:, None] * errors
    grad_feed = grad_summed.astype(jnp.bfloat16)
    grad_active = dense(grad_feed, w_down, ((1,), (0,)))
    grad_down = dense(grad_feed, active, ((0,), (0,))).astype(jnp.bfloat16)
    grad_gate_up = swiglu_pull(grad_active)[0].astype(jnp.bfloat16)
    grad_up = dense(second, grad_gate_up, ((0,), (0,))).astype(jnp.bfloat16)
    grad_second = core_sum(dense(grad_gate_up, w_up, ((1,), (1,))))
    grad_gain_second = jnp.sum((grad_second * second_unit)[:length], axis=0)
    grad_hidden = grad_summed + norm_back(second_scale, second_unit, gain_second, grad_second)
    grad_attn = grad_hidden.astype(jnp.bfloat16)
    grad_out = dense(grad_attn, branch, ((0,), (0,))).astype(jnp.bfloat16)
    grad_branch = dense(grad_attn, w_out, ((1,), (0,))).reshape(2, length, vals)

    def by_place(array):
        return array.reshape(count // 2, 2, rows, array.shape[1])

    grad_up = by_place(grad_up)
    grad_first, grad_conv, grad_gain_out, grad_head, sum_down, sum_gate, sum_out = backward_block(
        mixed_in, little, gate_pre, own_conv, head, gain_row, kept, grad_branch,
        by_place(grad_down), grad_up, by_place(grad_out),
    )
    loss_row = jnp.concatenate(
        [loss_part[None], jnp.sum(mask_own)[None], jnp.zeros((126,), jnp.float32)]
    )[None]
    grad_tokens, small_sum, sum_up, sum_in, sum_small = final_block(
        inputs, gain_first[None], grad_first.reshape(2 * padded, first_width), w_first,
        grad_hidden[:length], grad_conv, grad_gain_out, grad_head, grad_gain_second[None],
        loss_row, grad_up, vals,
    )
    valid_count = jnp.maximum(small_sum[5, 257], 1.0)
    loss_value = small_sum[5, 256] / valid_count
    factor = length * groups * count / valid_count
    sum_small = jnp.concatenate(
        [
            sum_small[:, 0:heads],
            sum_small[:, 128 : 128 + heads],
            sum_small[:, heads : 2 * heads],
            sum_small[:, 128 + heads : 128 + 2 * heads],
        ],
        axis=1,
    )

    def scaled(array):
        return array.astype(jnp.float32) * factor

    return (
        summed[:length].astype(jnp.bfloat16)[None],
        loss_value,
        scaled(grad_tokens)[None],
        scaled(sum_in),
        scaled(sum_small),
        scaled(sum_out),
        scaled(jnp.concatenate([sum_gate, sum_up], axis=1)),
        scaled(sum_down),
        scaled(small_sum[4, :model]),
        scaled(small_sum[4, model : 2 * model]),
        scaled(small_sum[4, 2 * model : 2 * model + DV]),
        scaled(small_sum[:CONV]),
        scaled(small_sum[5, :HEADS]),
        scaled(small_sum[5, 128 : 128 + HEADS]),
    )


def solution(mesh):
    placed = (
        P("dp", "seq", None),
        P("dp", "seq", None),
        P("dp", "seq"),
        P("seq", None),
        P("seq", None),
        P("seq", None),
        P("seq", None),
        P("seq", None),
        P(),
        P(),
        P(),
        P(),
        P(),
        P(),
    )
    return jax.shard_map(
        on_device,
        mesh=mesh,
        in_specs=placed,
        out_specs=(
            P("dp", "seq", None),
            P(),
            P("dp", "seq", None),
            P("seq", None),
            P("seq", None),
            P("seq", None),
            P("seq", None),
            P("seq", None),
            P(),
            P(),
            P(),
            P(),
            P(),
            P(),
        ),
        check_vma=False,
    )
```

```python
import functools

import jax
import jax.numpy as jnp
from jax import lax
from jax.experimental import pallas as pl
from jax.experimental.pallas import tpu as pltpu
from jax.sharding import PartitionSpec as P

HEADS = 6
DK = 128
DV = 256
FF = 2816
CONV = 4
BLOCK = 64
KEYS = 768
VALUES = 1536


precise = lax.Precision.HIGHEST
epsilon = 1e-06


MESH = pl.DeviceIdType.MESH
NN = (((1,), (0,)), ((), ()))
NT = (((1,), (1,)), ((), ()))
TN = (((0,), (0,)), ((), ()))


def exact(left, right, dims=NN):
    return lax.dot_general(
        left, right, dims, precision=precise, preferred_element_type=jnp.float32
    )


def near(left, right, dims=NN):
    return lax.dot_general(
        left.astype(jnp.bfloat16),
        right.astype(jnp.bfloat16),
        dims,
        preferred_element_type=jnp.float32,
    )


def close(left, right, dims=NN):
    left_top, right_top = left.astype(jnp.bfloat16), right.astype(jnp.bfloat16)
    left_rest = (left - left_top.astype(jnp.float32)).astype(jnp.bfloat16)
    right_rest = (right - right_top.astype(jnp.float32)).astype(jnp.bfloat16)
    return (
        near(left_rest, right_top, dims) + near(left_top, right_rest, dims)
    ) + near(left_top, right_top, dims)


def iotas(rows, columns):
    return (
        lax.broadcasted_iota(jnp.int32, (rows, columns), 0),
        lax.broadcasted_iota(jnp.int32, (rows, columns), 1),
    )


def decay_table(gcol, grow):
    size = gcol.shape[0]
    row, col = iotas(size, size)
    keep = row >= col
    return jnp.where(keep, jnp.exp(jnp.where(keep, gcol - grow, 0.0)), 0.0)


def tile_start(start):
    return pl.multiple_of(start, 128)


class Place:
    def __init__(self, groups, count):
        self.groups, self.count, self.half = groups, count, count // 2
        self.group, self.place = lax.axis_index("dp"), lax.axis_index("seq")
        self.pair, self.side = self.place // 2, self.place % 2
        self.plane = (self.group // 2) % 2
        self.group_swap = self.group + 1 - 2 * (self.group % 2)
        self.across = self.group + 2 - 4 * self.plane
        self.beside = self.place + 1 - 2 * self.side

    def shard(self, pair, side):
        return 2 * pair + side

    def ahead(self, step):
        return lax.rem(self.pair + step, self.half)

    def behind(self, step):
        return lax.rem(self.pair + self.half - step, self.half)

    def partners(self):
        along = [(self.group, self.shard(self.ahead(step), self.side)) for step in range(1, self.half)]
        return along + [(self.group, self.beside), (self.across, self.place)]


def greet(signalled, awaited):
    barrier = pltpu.get_barrier_semaphore()
    for device in signalled:
        pl.semaphore_signal(barrier, inc=1, device_id=device, device_id_type=MESH)
    pl.semaphore_wait(barrier, awaited)


def remote(source, target, sends, receives, index, device):
    return pltpu.make_async_remote_copy(
        src_ref=source,
        dst_ref=target,
        send_sem=sends.at[index],
        recv_sem=receives.at[index],
        device_id=device,
        device_id_type=MESH,
    )


class Gather:
    def __init__(self, at, source, target, lines, share, sends, receives, local):
        self.at, self.source, self.target, self.lines = at, source, target, lines
        self.sends, self.receives, self.local = sends, receives, local
        width = source.shape[1]
        self.own = pl.ds(tile_start(at.plane * share), width - share)
        self.lent = pl.ds(tile_start(at.plane * (width - share)), share)
        self.borrowed = pl.ds(tile_start((1 - at.plane) * (width - share)), share)
        self.started = {}

    def copy(self, index, shard, columns, device, from_source=False):
        there = self.target.at[shard, self.lines, columns]
        here = self.source.at[self.lines, columns] if from_source else there
        return remote(here, there, self.sends, self.receives, index, device)

    def along(self, step):
        at = self.at
        device = (at.group, at.shard(at.ahead(step), at.side))
        return self.copy(step - 1, at.place, self.own, device, True)

    def beside(self, step):
        at = self.at
        shard = at.shard(at.behind(step), at.side)
        return self.copy(at.half - 1 + step, shard, self.own, (at.group, at.beside), step == 0)

    def across(self, step, side):
        at = self.at
        shard = at.shard(at.behind(step), at.side if side == 0 else 1 - at.side)
        return self.copy(2 * at.half - 1 + 2 * step + side - 1, shard, self.lent, (at.across, at.place))

    def keep(self):
        return pltpu.make_async_copy(
            self.source.at[self.lines], self.target.at[self.at.place, self.lines], self.local
        )

    def launch(self, make, *where):
        make(*where).start()
        self.started[make.__name__, where] = make

    def begin(self):
        self.keep().start()
        for step in range(1, self.at.half):
            self.launch(self.along, step)
        self.launch(self.beside, 0)

    def arrived(self, index, shard, columns):
        self.copy(index, shard, columns, (self.at.group, self.at.place)).wait_recv()

    def pass_along(self, step):
        at = self.at
        self.arrived(step - 1, at.shard(at.behind(step), at.side), self.own)
        self.launch(self.beside, step)
        self.launch(self.across, step, 0)

    def pass_beside(self, step):
        at = self.at
        self.arrived(at.half - 1 + step, at.shard(at.behind(step), 1 - at.side), self.own)
        self.launch(self.across, step, 1)

    def take_across(self):
        at = self.at
        for step in range(at.half):
            for side in range(2):
                if step or side:
                    shard = at.shard(at.behind(step), at.side if side == 0 else 1 - at.side)
                    self.arrived(2 * at.half - 1 + 2 * step + side - 1, shard, self.borrowed)
        self.keep().wait()

    def finish(self):
        for (unused, where), make in self.started.items():
            make(*where).wait_send()

    def stages(self):
        half = self.at.half
        first = [functools.partial(self.pass_along, step) for step in range(1, half)]
        second = [functools.partial(self.pass_beside, step) for step in range(half)]
        return [first, second, [self.take_across]]


def copies_of_gather(count):
    return 2 * count - 2


def lagged(plans, lag):
    depth = max(len(plan) for plan in plans)
    turns = []
    for turn in range(len(plans) + lag * (depth - 1)):
        steps = []
        for index, plan in enumerate(plans):
            stage, rest = divmod(turn - index, lag)
            if rest == 0 and 0 <= stage < len(plan):
                steps = plan[stage] + steps
        turns.append(steps)
    return turns


class Work:
    def __init__(self, given, base, width, share, spots):
        self.given, self.base, self.width, self.share, self.spots = given, base, width, share, spots


class Reduce:
    def __init__(self, at, work, lines, buffers, sems):
        self.at, self.given, self.spots, self.lines = at, work.given, work.spots, lines
        self.sends, self.receives, self.local = sems
        width, share = work.width, work.share
        self.wide = width - share
        wide, narrow, full = pl.ds(0, self.wide), pl.ds(0, share), pl.ds(0, width)
        self.acc = buffers[0].at[:, :, :, wide]
        self.from_across = buffers[1].at[:, :, :, narrow]
        self.from_beside, self.from_along = buffers[2].at[:, :, wide], buffers[3].at[:, :, wide]
        self.part, self.from_plane = buffers[4].at[:, wide], buffers[5].at[:, wide]
        self.total, self.other = buffers[6].at[:, full], buffers[7].at[:, full]
        self.far = buffers[8].at[:, :, full] if at.groups > 4 else None
        self.own = pl.ds(tile_start(at.plane * share), self.wide)
        self.given_own = pl.ds(tile_start(work.base + at.plane * share), self.wide)
        self.given_lent = pl.ds(tile_start(work.base + (1 - at.plane) * self.wide), share)
        self.inner = pl.ds(tile_start(at.plane * (width - 2 * share)), share)
        self.theirs = pl.ds(tile_start((1 - at.plane) * share), self.wide)

    def side(self, mine):
        return self.at.side if mine else 1 - self.at.side

    def across(self, mine):
        at = self.at
        return remote(
            self.given.at[:, self.side(mine), self.lines, self.given_lent], self.from_across.at[mine],
            self.sends, self.receives, mine, (at.across, at.place),
        )

    def load(self, mine):
        return pltpu.make_async_copy(
            self.given.at[:, self.side(mine), self.lines, self.given_own], self.acc.at[mine],
            self.local.at[mine],
        )

    def beside(self):
        at = self.at
        return remote(
            self.acc.at[0], self.from_beside, self.sends, self.receives, 2, (at.group, at.beside)
        )

    def along(self, step):
        at = self.at
        pair = at.ahead(step)
        return remote(
            self.acc.at[1, pair], self.from_along.at[step - 1],
            self.sends, self.receives, 4 + step, (at.group, at.shard(pair, at.side)),
        )

    def plane(self):
        at = self.at
        return remote(
            self.part, self.from_plane, self.sends, self.receives, 3, (at.across, at.place)
        )

    def core(self):
        at = self.at
        return remote(
            self.total, self.other, self.sends, self.receives, 4, (at.group_swap, at.place)
        )

    def further(self, index, distance):
        at = self.at
        group = at.group + distance - 2 * distance * ((at.group // distance) % 2)
        return remote(
            self.total, self.far.at[index], self.sends, self.receives,
            4 + at.half + index, (group, at.place),
        )

    def begin(self):
        for mine in range(2):
            self.load(mine).start()
            self.across(mine).start()

    def add_across(self, mine):
        self.load(mine).wait()
        self.across(mine).wait_recv()
        held = self.acc[mine, :, :, self.inner].astype(jnp.float32)
        got = self.from_across[mine].astype(jnp.float32)
        self.acc[mine, :, :, self.inner] = (held + got).astype(jnp.bfloat16)
        if not mine:
            self.beside().start()

    def add_beside(self):
        self.beside().wait_recv()
        for step in range(1, self.at.half + 1):
            pair = self.at.ahead(step)
            held = self.acc[1, pair].astype(jnp.float32)
            got = self.from_beside[pair].astype(jnp.float32)
            self.acc[1, pair] = (held + got).astype(jnp.bfloat16)
            if step < self.at.half:
                self.along(step).start()

    def add_along(self):
        value = self.acc[1, self.at.pair].astype(jnp.float32)
        for step in range(1, self.at.half):
            self.along(step).wait_recv()
            value = value + self.from_along[step - 1].astype(jnp.float32)
        self.part[...] = value.astype(jnp.bfloat16)
        self.plane().start()

    def add_plane(self):
        self.plane().wait_recv()
        self.total[...] = jnp.zeros_like(self.total)
        self.total[:, self.own] = self.part[...]
        held = self.total[:, self.theirs].astype(jnp.float32)
        got = self.from_plane[...].astype(jnp.float32)
        self.total[:, self.theirs] = (held + got).astype(jnp.bfloat16)
        distance = 4
        while distance < self.at.groups:
            index = distance.bit_length() - 3
            copy = self.further(index, distance)
            copy.start()
            copy.wait()
            got = self.far[index].astype(jnp.float32)
            self.total[...] = (self.total[...].astype(jnp.float32) + got).astype(jnp.bfloat16)
            distance *= 2
        self.core().start()

    def deliver(self):
        self.core().wait_recv()
        core = self.at.group % 2
        for target, start, stride, width, source in self.spots:
            for held, which in ((self.total, core), (self.other, 1 - core)):
                span = pl.ds(tile_start(start + which * stride), width)
                target[self.lines, span] = held[:, source : source + width]

    def finish(self):
        copies = [self.across(0), self.across(1), self.beside(), self.plane(), self.core()]
        copies += [self.along(step) for step in range(1, self.at.half)]
        for copy in copies:
            copy.wait_send()

    def stages(self):
        return [
            [functools.partial(self.add_across, 0)],
            [functools.partial(self.add_across, 1), self.add_beside],
            [self.add_along],
            [self.add_plane],
            [self.deliver],
        ]


ANY = pl.BlockSpec(memory_space=pl.ANY)
ROOM = pl.BlockSpec(memory_space=pltpu.VMEM)
PAD = 16
CHUNKS, WINDOW, GATHER_LAG = 4, 2, 1
REDUCE_CHUNKS, REDUCE_WINDOW, REDUCE_LAG, POOL = 4, 2, 1, 6


def neighbours(at, step):
    place = lax.rem(at.place + at.count + step, at.count)
    return (at.group, place), (at.group_swap, place)


def chunks_of(rows):
    return max(1, min(CHUNKS, rows // 16))


def gather_sems(count, rows, number):
    chunks = chunks_of(rows)
    return [
        pltpu.SemaphoreType.DMA((number * chunks, copies_of_gather(count))),
        pltpu.SemaphoreType.DMA((number * chunks, copies_of_gather(count))),
        pltpu.SemaphoreType.DMA((number * chunks,)),
    ]


def gather_plans(at, sources, targets, shares, sends, receives, local):
    rows = sources[0].shape[0]
    chunks = chunks_of(rows)
    lines = rows // chunks
    return [
        Gather(
            at, sources[i], targets[i], pl.ds(part * lines, lines), shares[i],
            sends.at[i * chunks + part], receives.at[i * chunks + part], local.at[i * chunks + part],
        )
        for i in range(len(sources))
        for part in range(chunks)
    ]


def gather_steps(plans):
    steps = [plan.begin for plan in plans[:WINDOW]]
    for index, turn in enumerate(lagged([plan.stages() for plan in plans], GATHER_LAG)):
        steps += turn
        if index + WINDOW < len(plans):
            steps.append(plans[index + WINDOW].begin)
    return steps + [plan.finish for plan in plans]


def reduce_steps(plans):
    steps = [plan.begin for plan in plans[:REDUCE_WINDOW]]
    for index, turn in enumerate(lagged([plan.stages() for plan in plans], REDUCE_LAG)):
        steps += turn
        later = index + REDUCE_WINDOW
        if later < len(plans):
            if later >= POOL:
                steps.append(plans[later - POOL].finish)
            steps.append(plans[later].begin)
    return steps + [plan.finish for plan in plans[-POOL:]]


def reduce_buffers(groups, count, rows, width, share):
    wide, half = width - share, count // 2
    kind = jnp.bfloat16
    far = (max(1, (groups // 4).bit_length() - 1), rows, width) if groups > 4 else (1, 16, 128)
    return [
        pltpu.VMEM((2, half, rows, wide), kind),
        pltpu.VMEM((2, half, rows, share), kind),
        pltpu.VMEM((half, rows, wide), kind),
        pltpu.VMEM((half - 1, rows, wide), kind),
        pltpu.VMEM((rows, wide), kind),
        pltpu.VMEM((rows, wide), kind),
        pltpu.VMEM((rows, width), kind),
        pltpu.VMEM((rows, width), kind),
        pltpu.VMEM(far, kind),
    ]


def copies_of_reduce(groups, count):
    return count // 2 + 4 + max(1, (groups // 4).bit_length() - 1)


def further_groups(at):
    found, distance = [], 4
    while distance < at.groups:
        found.append((at.group + distance - 2 * distance * ((at.group // distance) % 2), at.place))
        distance *= 2
    return found


def reduce_plans(at, works, scratch):
    rows = works[0].given.shape[2]
    chunks = reduce_chunks(rows)
    lines = rows // chunks
    sends, receives, local = scratch[9 * POOL : 9 * POOL + 3]
    plans = []
    for work in works:
        for part in range(chunks):
            spot = len(plans)
            slot = spot % POOL
            plans.append(
                Reduce(
                    at, work, pl.ds(part * lines, lines), scratch[9 * slot : 9 * slot + 9],
                    (sends.at[spot], receives.at[spot], local.at[spot]),
                )
            )
    return plans


def reduce_chunks(rows):
    return max(1, min(REDUCE_CHUNKS, rows // 16))


def reduce_scratch(groups, count, rows, widths):
    chunks = reduce_chunks(rows)
    width = max(widths)
    scratch = reduce_buffers(groups, count, rows // chunks, width, reduce_share(width)) * POOL
    number, copies = len(widths) * chunks, copies_of_reduce(groups, count)
    return scratch + [
        pltpu.SemaphoreType.DMA((number, copies)),
        pltpu.SemaphoreType.DMA((number, copies)),
        pltpu.SemaphoreType.DMA((number, 2)),
    ]


def reduce_share(width):
    return third(width, 0.28)


class Relay:
    def __init__(self, at, forward, units, sending, arriving, sends, receives):
        self.at, self.units = at, units
        self.sending, self.arriving, self.sends, self.receives = sending, arriving, sends, receives
        last = at.count - 1
        step = 1 if forward else -1
        self.is_first = at.place == (0 if forward else last)
        self.is_last = at.place == (last if forward else 0)
        self.beyond = (at.group, lax.rem(at.place + at.count + step, at.count))
        self.before = (at.group, lax.rem(at.place + at.count - step, at.count))

    def copy(self, unit):
        return remote(
            self.sending.at[unit], self.arriving.at[unit], self.sends, self.receives, unit, self.beyond
        )

    def receive(self, unit, target):
        @pl.when(self.is_first)
        def _():
            target[unit] = jnp.zeros(target.shape[1:], jnp.float32)

        @pl.when(jnp.logical_not(self.is_first))
        def _():
            self.copy(unit).wait_recv()
            target[unit] = self.arriving[unit].astype(jnp.float32)

    def send(self, unit, value):
        @pl.when(jnp.logical_not(self.is_last))
        def _():
            self.sending[unit] = value().astype(jnp.bfloat16)
            self.copy(unit).start()

    def finish(self):
        @pl.when(jnp.logical_not(self.is_last))
        def _():
            for unit in range(self.units):
                self.copy(unit).wait_send()


def relay_scratch(units):
    return [
        pltpu.VMEM((units, DK, DV), jnp.bfloat16),
        pltpu.VMEM((units, DK, DV), jnp.bfloat16),
        pltpu.SemaphoreType.DMA((units,)),
        pltpu.SemaphoreType.DMA((units,)),
    ]


class Agenda:
    def __init__(self, steps):
        self.steps, self.done = steps, 0

    def take(self, upto):
        upto = max(upto, self.done)
        found, self.done = self.steps[self.done : upto], upto
        return found

    def until(self, share):
        for step in self.take(int(len(self.steps) * share)):
            step()

    def pieces(self, number, share):
        found = self.take(int(len(self.steps) * share))
        cuts = [len(found) * i // number for i in range(number + 1)]
        return [found[low:high] for low, high in zip(cuts, cuts[1:])]

    def loop(self, rounds, end, stage):
        pieces = self.pieces(rounds * PAUSES, end)
        taken = []

        def body(index, carry):
            for pause, unused in enumerate(stage(index)):
                taken.append(pause)
                for other in range(rounds):
                    found = pieces[other * PAUSES + pause]
                    if found:
                        pl.when(index == other)(functools.partial(run_steps, found))
            return carry

        lax.fori_loop(0, rounds, body, 0)
        assert len(taken) == PAUSES

    def around(self, rounds, turn, end, stage, main):
        pieces = self.pieces(rounds, end)

        def body(index, carry):
            stage(index)
            for other, found in enumerate(pieces):
                if found:
                    pl.when(index == other)(functools.partial(run_steps, found))
            return carry

        split = jnp.minimum(turn, rounds)
        lax.fori_loop(0, split, body, 0)
        main()
        lax.fori_loop(split, rounds, body, 0)


def run_steps(steps):
    for step in steps:
        step()


PAUSES = 9


def lockstep(stages):
    for unused in zip(*stages):
        yield


def rolled(value, shift):
    shift = shift % value.shape[0]
    return value if shift == 0 else pltpu.roll(value, shift, 0)


def silu_parts(value):
    gate = jax.nn.sigmoid(value)
    return value * gate, gate * (1.0 + value * (1.0 - gate))


def lane_start(start):
    return start if isinstance(start, int) else tile_start(start)


class Unit:
    def __init__(self, seq, head, heads, mixed_ref, conv_ref):
        self.seq, self.head = seq, head
        self.mixed_ref, self.conv_ref = mixed_ref, conv_ref
        keys = heads * DK
        self.columns = [
            (lane_start(self.head * DK), DK),
            (lane_start(keys + self.head * DK), DK),
            (lane_start(2 * keys + self.head * DV), DV),
        ]

    def taps(self, part):
        start, width = self.columns[part]
        span = pl.ds(start, width)
        field = self.mixed_ref[self.seq, :, span].astype(jnp.float32)
        weights = self.conv_ref[:, span]
        shifts = [rolled(field, CONV - 1 - tap)[PAD:] for tap in range(CONV)]
        value = weights[0:1] * shifts[0]
        for tap in range(1, CONV):
            value = value + weights[tap : tap + 1] * shifts[tap]
        return shifts, weights, value

    def rows(self, part):
        value = self.taps(part)[2]
        active = value * jax.nn.sigmoid(value)
        if part == 2:
            return active
        unit = active * lax.rsqrt(jnp.sum(active * active, axis=1, keepdims=True) + epsilon)
        return unit * DK ** (-0.5) if part == 0 else unit

    def taps_back(self, part, grad, grad_ref, conv_grad_ref):
        shifts, weights, value = self.taps(part)
        active, slope = silu_parts(value)
        if part < 2:
            scale = lax.rsqrt(jnp.sum(active * active, axis=1, keepdims=True) + epsilon)
            unit = active * scale
            grad = grad * DK ** (-0.5) if part == 0 else grad
            grad = scale * (grad - unit * jnp.sum(grad * unit, axis=1, keepdims=True))
        grad = grad * slope
        start, width = self.columns[part]
        span = pl.ds(start, width)
        row = lax.broadcasted_iota(jnp.int32, (8, width), 0)
        taps = jnp.zeros((8, width), jnp.float32)
        longer = jnp.concatenate([jnp.zeros((PAD, width), jnp.float32), grad], axis=0)
        total = jnp.zeros(longer.shape, jnp.float32)
        for tap in range(CONV):
            taps = taps + jnp.where(row == tap, jnp.sum(grad * shifts[tap], axis=0, keepdims=True), 0.0)
            total = total + weights[tap : tap + 1] * rolled(longer, tap - (CONV - 1))
        grad_ref[self.seq, :, span] = total.astype(jnp.bfloat16)
        conv_grad_ref[:, span] += taps


def head_tables(little_ref, head_ref, g_ref, grow_ref):
    seqs, size = little_ref.shape[0], g_ref.shape[1]
    row, col = iotas(size, size)
    below = (row >= col).astype(jnp.float32)
    above = (row <= col).astype(jnp.float32)
    for seq in range(seqs):
        forget = head_ref[0:1] * jax.nn.softplus(little_ref[seq, PAD:, :] + head_ref[1:2])
        g_ref[seq] = exact(below, forget)
        grow_ref[seq] = exact(forget, above, TN)


def head_columns(seq, head, heads, little_ref, g_ref, grow_ref):
    size = g_ref.shape[1]
    lane = lax.broadcasted_iota(jnp.int32, (size, 128), 1)
    line = lax.broadcasted_iota(jnp.int32, (128, size), 0)

    def column(table, index):
        return jnp.sum(jnp.where(lane == index, table, 0.0), axis=1, keepdims=True)

    beta = column(jax.nn.sigmoid(little_ref[seq, PAD:, :]), head)
    gcol = column(g_ref[seq], heads + head)
    grow = jnp.sum(jnp.where(line == heads + head, grow_ref[seq], 0.0), axis=0, keepdims=True)
    return beta, gcol, grow


def merged(inverses, systems, width):
    size = systems[0].shape[0]
    row, col = iotas(size, size)
    joined = (row // (2 * width) == col // (2 * width)) & (row // width != col // width)
    inner = [close(jnp.where(joined, system, 0.0), inverse) for system, inverse in zip(systems, inverses)]
    return [inverse - close(inverse, value) for inverse, value in zip(inverses, inner)]


def forward_kernel(groups, count, shares, *refs):
    number = len(shares)
    tokens_ref, target_ref, mask_ref, norm_ref, conv_ref, head_ref, gain_ref = refs[:7]
    sources, refs = refs[7 : 7 + number], refs[7 + number :]
    inputs_ref, target_other, mask_other, mixed_ref, little_ref, gate_ref = refs[:6]
    branch_ref, out_ref, t_ref, u_ref, w_ref, m_ref, e_ref, s_ref = refs[6:14]
    targets, refs = refs[14 : 14 + number], refs[14 + number :]
    normed, b_ref, g_ref, grow_ref, sending, arriving, relay_send, relay_recv = refs[:8]
    swap_send, swap_recv, sends, receives, local = refs[8:]
    units = t_ref.shape[0]
    heads = units // 2
    size = t_ref.shape[1]
    half = size // 2
    at = Place(groups, count)
    line = Relay(at, True, units, sending, arriving, relay_send, relay_recv)
    core = (at.group_swap, at.place)
    greet(at.partners() + [line.before, core] + list(neighbours(at, -1)), count // 2 + 5)
    padded = size + PAD
    swaps = [
        remote(here, there, swap_send, swap_recv, index, core)
        for index, (here, there) in enumerate((
            (tokens_ref, inputs_ref.at[pl.ds(padded + PAD, size)]),
            (target_ref, target_other),
            (mask_ref, mask_other),
        ))
    ]
    tail = tokens_ref.at[pl.ds(size - PAD, PAD)]
    own_next, swap_next = neighbours(at, 1)
    rims = [
        remote(tail, inputs_ref.at[pl.ds(0, PAD)], swap_send, swap_recv, 3, own_next),
        remote(tail, inputs_ref.at[pl.ds(padded, PAD)], swap_send, swap_recv, 4, swap_next),
    ]
    swaps[0].start()

    @pl.when(at.place < count - 1)
    def _():
        for copy in rims:
            copy.start()

    plans = gather_plans(at, sources, targets, shares, sends, receives, local)
    agenda = Agenda(gather_steps(plans))
    run_steps(agenda.take(WINDOW))
    for copy in swaps[1:]:
        copy.start()
    inputs_ref[PAD:padded] = tokens_ref[...]

    @pl.when(at.place == 0)
    def _():
        inputs_ref[:PAD] = jnp.zeros((PAD, inputs_ref.shape[1]), jnp.bfloat16)
        inputs_ref[padded : padded + PAD] = jnp.zeros((PAD, inputs_ref.shape[1]), jnp.bfloat16)

    @pl.when(at.place > 0)
    def _():
        for copy in rims:
            copy.wait_recv()

    swaps[0].wait()
    for seq in range(2):
        value = inputs_ref[seq * padded : (seq + 1) * padded].astype(jnp.float32)
        scale = lax.rsqrt(jnp.mean(value * value, axis=1, keepdims=True) + epsilon)
        normed[seq * padded : (seq + 1) * padded] = (value * scale * norm_ref[...]).astype(jnp.bfloat16)
    first_chunks = len(plans) // number
    run_steps(agenda.take(agenda.steps.index(plans[first_chunks - 1].take_across) + 1))

    weight = targets[0]
    model = normed.shape[1]
    mixed_width = mixed_ref.shape[2]
    cuts = [0, mixed_width // 2, mixed_width, mixed_width + 128, weight.shape[2]]
    for start, end in zip(cuts, cuts[1:]):
        value = dense(normed[...], weight[:, :, start:end].reshape(model, end - start), ((1,), (0,)))
        value = value.reshape(2, padded, end - start)
        if end <= mixed_width:
            mixed_ref[:, :, start:end] = value.astype(jnp.bfloat16)
        elif end == mixed_width + 128:
            little_ref[...] = value
        else:
            gate_ref[...] = value
        agenda.until(agenda.done / len(agenda.steps) + FORWARD_PROJECT / 4)
    head_tables(little_ref, head_ref, g_ref, grow_ref)

    def local_stage(seq, head):
        unit = seq * heads + head
        own = Unit(seq, head, heads, mixed_ref, conv_ref)
        beta, gcol, grow = head_columns(seq, head, heads, little_ref, g_ref, grow_ref)
        decays = decay_table(gcol, grow)
        keys = own.rows(1)
        row, col = iotas(size, size)
        system = jnp.where(row > col, beta * close(keys, keys, NT) * decays, 0.0)
        yield
        systems = [system[:half, :half], system[half:, half:]]
        row, col = iotas(half, half)
        inverses = [
            (row == col).astype(jnp.float32) - jnp.where(row // 2 == col // 2, value, 0.0)
            for value in systems
        ]
        width = 2
        while width < half:
            inverses = merged(inverses, systems, width)
            width *= 2
            yield
        corner = -close(inverses[1], close(system[half:, :half], inverses[0]))
        t_ref[unit, :half, :half] = inverses[0]
        t_ref[unit, :half, half:] = jnp.zeros((half, half), jnp.float32)
        t_ref[unit, half:, :half] = corner
        t_ref[unit, half:, half:] = inverses[1]
        solve = t_ref[unit]
        growth = jnp.exp(gcol)
        last = gcol[size - 1 :, :]
        update = near(solve, beta * own.rows(2))
        back = near(solve, (beta * growth) * keys)
        u_ref[unit] = update
        w_ref[unit] = back
        yield
        weighted = keys * jnp.exp(last - gcol)
        drow, dcol = iotas(DK, DK)
        m_ref[unit] = jnp.where(drow == dcol, jnp.exp(last), 0.0) - near(weighted, back, TN)
        b_ref[unit] = near(weighted, update, TN)
        yield

    agenda.loop(2, FORWARD_LOCAL, lambda seq: lockstep([local_stage(seq, h) for h in range(heads)]))

    def pass_on():
        for unit in range(units):
            line.receive(unit, s_ref)
            line.send(unit, lambda: close(m_ref[unit], s_ref[unit]) + b_ref[unit])

    def score_stage(unit):
        seq, head = unit // heads, unit % heads
        own = Unit(seq, head, heads, mixed_ref, conv_ref)
        unused, gcol, grow = head_columns(seq, head, heads, little_ref, g_ref, grow_ref)
        queries = own.rows(0)
        scores = near(queries, own.rows(1), NT) * decay_table(gcol, grow)
        out_ref[unit] = near(scores, u_ref[unit])
        e_ref[unit] = jnp.exp(gcol) * queries - near(scores, w_ref[unit])

    agenda.around(units, at.place, FORWARD_RELAY, score_stage, pass_on)

    def read_stage(seq, head):
        unit = seq * heads + head
        value = out_ref[unit] + near(e_ref[unit], s_ref[unit])
        out_ref[unit] = value
        span = pl.ds(head * DV, DV)
        scale = lax.rsqrt(jnp.mean(value * value, axis=1, keepdims=True) + epsilon)
        gate = gate_ref[seq, PAD:, span]
        branch = value * scale * gain_ref[...] * (gate * jax.nn.sigmoid(gate))
        branch_ref[seq, :, span] = branch.astype(jnp.bfloat16)

    for seq in range(2):
        for head in range(heads):
            read_stage(seq, head)
            agenda.until(
                FORWARD_RELAY + (FORWARD_READ - FORWARD_RELAY) * (seq * heads + head + 1) / units
            )
    agenda.until(1.0)
    line.finish()
    for copy in swaps[1:]:
        copy.wait()

    @pl.when(at.place < count - 1)
    def _():
        for copy in rims:
            copy.wait_send()


FORWARD_PROJECT, FORWARD_LOCAL, FORWARD_RELAY, FORWARD_READ = 0.04, 0.65, 0.85, 0.92
BACK_OPEN, BACK_RELAY, BACK_GRADS, BACK_BLOCKS, BACK_PART = 0.06, 0.22, 0.42, 0.5, 0.58


def forward_block(tokens, target, mask, norm_gain, conv, head, gain, sources, shares):
    groups, count = lax.axis_size("dp"), lax.axis_size("seq")
    number, rows = len(sources), sources[0].shape[0]
    length, model = tokens.shape
    mixed_width = conv.shape[1]
    heads = mixed_width // (2 * DK + DV)
    units = 2 * heads
    padded = length + PAD

    def table(*shape):
        return jax.ShapeDtypeStruct((units,) + shape, jnp.float32)

    return pl.pallas_call(
        functools.partial(forward_kernel, groups, count, shares),
        out_shape=[
            jax.ShapeDtypeStruct((2 * padded, model), tokens.dtype),
            jax.ShapeDtypeStruct(target.shape, target.dtype),
            jax.ShapeDtypeStruct(mask.shape, mask.dtype),
            jax.ShapeDtypeStruct((2, padded, mixed_width), jnp.bfloat16),
            jax.ShapeDtypeStruct((2, padded, 128), jnp.float32),
            jax.ShapeDtypeStruct((2, padded, heads * DV), jnp.float32),
            jax.ShapeDtypeStruct((2, length, heads * DV), jnp.bfloat16),
            table(length, DV),
            table(length, length),
            table(length, DV),
            table(length, DK),
            table(DK, DK),
            table(length, DK),
            table(DK, DV),
        ]
        + [jax.ShapeDtypeStruct((count,) + v.shape, v.dtype) for v in sources],
        in_specs=[ROOM, ANY, ANY] + [ROOM] * 4 + [ANY] * number,
        out_specs=[ROOM, ANY, ANY] + [ROOM] * 11 + [ROOM] + [ANY] * (number - 1),
        scratch_shapes=[
            pltpu.VMEM((2 * padded, model), jnp.bfloat16),
            pltpu.VMEM((units, DK, DV), jnp.float32),
            pltpu.VMEM((2, length, 128), jnp.float32),
            pltpu.VMEM((2, 128, length), jnp.float32),
            *relay_scratch(units),
            pltpu.SemaphoreType.DMA((5,)),
            pltpu.SemaphoreType.DMA((5,)),
            *gather_sems(count, rows, number),
        ],
        compiler_params=pltpu.CompilerParams(
            collective_id=3, has_side_effects=True, vmem_limit_bytes=56 * 2**20
        ),
        name="forward_block",
    )(tokens, target, mask, norm_gain, conv, head, gain, *sources)


def backward_kernel(groups, count, *refs):
    mixed_ref, little_ref, gate_ref, conv_ref, head_ref, gain_ref = refs[:6]
    out_ref, t_ref, u_ref, w_ref, m_ref, e_ref, s_ref, branch_ref = refs[6:14]
    tokens_ref, norm_ref, hidden_ref, second_grad, loss_ref = refs[14:19]
    weight_ref, down_ref, up_ref, out_grad = refs[19:23]
    token_grad, small_sum, down_sum, gate_sum, up_sum, out_sum, in_sum, little_sum, given = refs[23:32]
    refs = refs[32:]
    do_ref, c_ref, ds_ref, lit_ref, g_ref, grow_ref = refs[:6]
    x_ref, ahead_ref, k_ref, log_ref, less_ref = refs[6:11]
    sending, arriving, relay_send, relay_recv = refs[11:15]
    grad_ref, conv_grad, gain_grad, head_grad = refs[15:19]
    normed, wide_grad, part_ref, weight = refs[19:23]
    swap, swap_got, rims, rim_got, small_got = refs[23:28]
    wide_sem, weight_sem, swap_send, swap_recv, small_send, small_recv = refs[28:34]
    scratch = refs[34:]
    units = t_ref.shape[0]
    heads = units // 2
    size = t_ref.shape[1]
    mixed_width, vals = mixed_ref.shape[2], branch_ref.shape[2]
    at = Place(groups, count)
    line = Relay(at, False, units, sending, arriving, relay_send, relay_recv)
    core = at.group % 2
    further = further_groups(at)
    pair = (at.group_swap, at.place)
    rounds, distance = [], 1
    while distance < groups:
        rounds.append((at.group + distance - 2 * distance * ((at.group // distance) % 2), at.place))
        distance *= 2
    distance = 1
    while distance < count:
        rounds.append((at.group, at.place + distance - 2 * distance * ((at.place // distance) % 2)))
        distance *= 2
    partners = at.partners() + [pair, line.before] + further + rounds + list(neighbours(at, 1))
    greet(partners, count // 2 + 5 + len(further) + len(rounds))
    keys_width, inner = heads * DK, down_ref.shape[3]
    first_width = grad_ref.shape[2]
    cut = 2 * FINAL_COLUMNS
    works = [
        Work(down_ref, 0, inner, reduce_share(inner), [(down_sum, 0, inner, inner, 0)]),
        Work(up_ref, 0, inner, reduce_share(inner), [(gate_sum, 0, inner, inner, 0)]),
        Work(out_grad, 0, vals, reduce_share(vals), [(out_sum, 0, vals, vals, 0)]),
        Work(up_ref, inner, inner, reduce_share(inner), [(up_sum, 0, inner, inner, 0)]),
        Work(
            given, 0, cut, reduce_share(cut),
            [
                (in_sum, 0, keys_width, keys_width, 0),
                (in_sum, 2 * keys_width, keys_width, keys_width, keys_width),
                (in_sum, 4 * keys_width, vals, cut - 2 * keys_width, 2 * keys_width),
            ],
        ),
        Work(
            given, cut, first_width - cut, reduce_share(first_width - cut),
            [
                (in_sum, 2 * keys_width + cut, vals, mixed_width - cut, 0),
                (little_sum, 0, 128, 128, mixed_width - cut),
                (in_sum, 4 * keys_width + 2 * vals, vals, vals, mixed_width + 128 - cut),
            ],
        ),
    ]
    plans = reduce_plans(at, works, scratch)
    chunks = len(plans) // len(works)
    agenda = Agenda(reduce_steps(plans))
    openings = [agenda.steps.index(plans[chunks * 4].begin), agenda.steps.index(plans[chunks * 5].begin)]
    run_steps(agenda.take(REDUCE_WINDOW))
    head_tables(little_ref, head_ref, g_ref, grow_ref)
    grad_ref[:, :PAD, mixed_width:] = jnp.zeros(
        (2, PAD, grad_ref.shape[2] - mixed_width), jnp.bfloat16
    )
    conv_grad[...] = jnp.zeros_like(conv_grad)
    gain_grad[...] = jnp.zeros_like(gain_grad)
    head_grad[...] = jnp.zeros_like(head_grad)
    lit_ref[...] = jnp.zeros_like(lit_ref)
    log_ref[...] = jnp.zeros_like(log_ref)

    def gate_stage(seq, head):
        unit = seq * heads + head
        span = pl.ds(head * DV, DV)
        value = out_ref[unit]
        scale = lax.rsqrt(jnp.mean(value * value, axis=1, keepdims=True) + epsilon)
        normal = value * scale
        active, slope = silu_parts(gate_ref[seq, PAD:, span])
        grad = branch_ref[seq, :, span]
        gain = gain_ref[...]
        through = grad * active
        gain_grad[0:1] += jnp.sum(through * normal, axis=0, keepdims=True)
        gate_span = pl.ds(mixed_width + 128 + head * DV, DV)
        grad_ref[seq, PAD:, gate_span] = (grad * normal * gain * slope).astype(jnp.bfloat16)
        scaled = through * gain
        grad_out = scale * (scaled - normal * jnp.mean(scaled * normal, axis=1, keepdims=True))
        do_ref[unit] = grad_out
        c_ref[unit] = near(e_ref[unit], grad_out, TN)

    for seq in range(2):
        for head in range(heads):
            gate_stage(seq, head)
    agenda.until(BACK_OPEN)

    def pass_on():
        for unit in range(units):
            line.receive(unit, ds_ref)
            line.send(unit, lambda: close(m_ref[unit], ds_ref[unit], TN) + c_ref[unit])

    def score_stage(unit):
        seq, head = unit // heads, unit % heads
        own = Unit(seq, head, heads, mixed_ref, conv_ref)
        unused, gcol, grow = head_columns(seq, head, heads, little_ref, g_ref, grow_ref)
        queries, keys = own.rows(0), own.rows(1)
        decays = decay_table(gcol, grow)
        memory, grad_out = s_ref[unit], do_ref[unit]
        update = u_ref[unit] - near(w_ref[unit], memory)
        x_ref[unit] = update.astype(jnp.bfloat16)
        scores = near(queries, keys, NT) * decays
        ahead_ref[unit] = near(scores, grad_out, TN)
        grad_scores = near(grad_out, update, NT)
        total = grad_scores * scores
        query_part = jnp.exp(gcol) * near(grad_out, memory, NT)
        grad_dot = grad_scores * decays
        own.taps_back(0, query_part + near(grad_dot, keys), grad_ref, conv_grad)
        k_ref[unit] = near(grad_dot, queries, TN)
        lane = lax.broadcasted_iota(jnp.int32, (size, 128), 1)
        log_line = jnp.sum(queries * query_part, axis=1, keepdims=True) + jnp.sum(
            total, axis=1, keepdims=True
        )
        log_ref[seq] += jnp.where(lane == head, log_line, 0.0)
        less_ref[unit] = jnp.broadcast_to(jnp.sum(total, axis=0, keepdims=True), (8, size))

    agenda.around(units, count - 1 - at.place, BACK_RELAY, score_stage, pass_on)

    def grad_stage(seq, head):
        unit = seq * heads + head
        own = Unit(seq, head, heads, mixed_ref, conv_ref)
        beta, gcol, grow = head_columns(seq, head, heads, little_ref, g_ref, grow_ref)
        keys, values = own.rows(1), own.rows(2)
        decays = decay_table(gcol, grow)
        row, col = iotas(size, size)
        strict = row > col
        memory, after = s_ref[unit], ds_ref[unit]
        growth = jnp.exp(gcol)
        last = gcol[size - 1 :, :]
        weights = jnp.exp(last - gcol)
        update = x_ref[unit]
        yield
        keys_dot = jnp.where(strict, near(keys, keys, NT) * decays, 0.0)
        grad_update = ahead_ref[unit] + near(keys * weights, after)
        yield
        grad_wanted = near(t_ref[unit], grad_update, TN)
        yield
        grad_system = -near(grad_wanted, update, NT)
        through = keys_dot * grad_system
        total = beta * through
        yield
        key_read = growth * near(grad_wanted, memory, NT)
        key_part = beta * key_read
        end_part = weights * near(update, after, NT)
        yield
        grad_keys_dot = jnp.where(strict, grad_system * decays, 0.0) * beta
        grad_k = (
            end_part - key_part + k_ref[unit]
            + near(grad_keys_dot, keys) + near(grad_keys_dot, keys, TN)
        )
        yield
        own.taps_back(1, grad_k, grad_ref, conv_grad)
        yield
        own.taps_back(2, beta * grad_wanted, grad_ref, conv_grad)
        yield
        end_line = jnp.sum(keys * end_part, axis=1, keepdims=True)
        grad_beta = (
            jnp.sum(grad_wanted * values, axis=1, keepdims=True)
            - jnp.sum(keys * key_read, axis=1, keepdims=True)
            + jnp.sum(through, axis=1, keepdims=True)
        )
        lane = lax.broadcasted_iota(jnp.int32, (size, 128), 1)
        grad_log = (
            jnp.sum(jnp.where(lane == head, log_ref[seq], 0.0), axis=1, keepdims=True)
            - jnp.sum(keys * key_part, axis=1, keepdims=True)
            - end_line
            + jnp.sum(total, axis=1, keepdims=True)
        )
        grad_last = jnp.sum(end_line) + jnp.sum(
            jnp.exp(last) * jnp.sum(memory * after, axis=1, keepdims=True)
        )
        spot = lax.broadcasted_iota(jnp.int32, (size, 1), 0)
        grad_log = grad_log + jnp.where(spot == size - 1, grad_last, 0.0)
        later = (col >= row).astype(jnp.float32)
        less = jnp.sum(total, axis=0, keepdims=True) + less_ref[unit][0:1]
        less = jnp.broadcast_to(less, (128, size))
        grad_forget = exact(later, jnp.broadcast_to(grad_log, (size, 128))) - exact(later, less, NT)
        rate, bias = head_ref[0:1], head_ref[1:2]
        little = little_ref[own.seq, PAD:, :]
        on_forget = lane == heads + own.head
        grad_soft = jnp.where(on_forget, grad_forget * rate * jax.nn.sigmoid(little + bias), 0.0)
        forget = rate * jax.nn.softplus(little + bias)
        log_total = jnp.sum(jnp.where(on_forget, grad_forget * forget, 0.0), axis=0, keepdims=True)
        head_grad[0:1] += log_total
        head_grad[1:2] += jnp.sum(grad_soft, axis=0, keepdims=True)
        lit_ref[own.seq] += grad_soft + jnp.where(
            lane == own.head, grad_beta * beta * (1.0 - beta), 0.0
        )
        yield

    agenda.loop(2, BACK_GRADS, lambda seq: lockstep([grad_stage(seq, h) for h in range(heads)]))
    grad_ref[:, PAD:, mixed_width : mixed_width + 128] = lit_ref[...].astype(jnp.bfloat16)
    line.finish()

    gain = norm_ref[...]

    def norm_rows(first, number):
        value = tokens_ref[first : first + number].astype(jnp.float32)
        scale = lax.rsqrt(jnp.mean(value * value, axis=1, keepdims=True) + epsilon)
        return scale, value * scale

    height = tokens_ref.shape[0]
    for first in range(0, height, height // 2):
        normed[first : first + height // 2] = (norm_rows(first, height // 2)[1] * gain).astype(jnp.bfloat16)
    model = tokens_ref.shape[1]
    quarter = model // 4

    def fetch(index):
        return pltpu.make_async_copy(
            weight_ref.at[pl.ds(index * quarter, quarter)], weight.at[index % 2], weight_sem.at[index % 2]
        )

    def store(start, width):
        return pltpu.make_async_copy(
            wide_grad.at[:, :, :, pl.ds(0, width)], given.at[:, :, :, pl.ds(start, width)], wide_sem
        )

    padded = height // 2
    fetch(0).start()
    fetch(1).start()
    half, unused, rows, unused = given.shape
    blocks = [
        (start, min(FINAL_COLUMNS, first_width - start))
        for start in range(0, first_width, FINAL_COLUMNS)
    ]
    for index, (start, width) in enumerate(blocks):
        if index > 0:
            store(*blocks[index - 1]).wait()
        for part in range(4):
            value = sum(
                dense(
                    normed[seq * padded : (seq + 1) * padded, part * quarter : (part + 1) * quarter],
                    grad_ref[seq, :, start : start + width],
                    ((0,), (0,)),
                )
                for seq in range(2)
            ).astype(jnp.bfloat16)
            for line in range(quarter // rows):
                place = part * (quarter // rows) + line
                wide_grad[place // 2, place % 2, :, :width] = value[line * rows : (line + 1) * rows]
        store(start, width).start()
        aim = BACK_GRADS + (BACK_BLOCKS - BACK_GRADS) * (index + 1) / len(blocks)
        run_steps(agenda.take(min(int(len(agenda.steps) * aim), openings[0])))
    store(*blocks[-1]).wait()
    for index in range(4):
        fetch(index).wait()
        for seq in range(2):
            part_ref[
                seq * padded : (seq + 1) * padded, index * quarter : (index + 1) * quarter
            ] = dense(grad_ref[seq], weight[index % 2], ((1,), (1,)))
        if index + 2 < 4:
            fetch(index + 2).start()
        agenda.until(BACK_BLOCKS + (BACK_PART - BACK_BLOCKS) * (index + 1) / 4)
    length = height // 2 - PAD
    swap[...] = part_ref[length + 2 * PAD :].astype(jnp.bfloat16)
    rims[0] = part_ref[:PAD].astype(jnp.bfloat16)
    rims[1] = part_ref[length + PAD : length + 2 * PAD].astype(jnp.bfloat16)
    own_back, swap_back = neighbours(at, -1)
    swapped = remote(swap, swap_got, swap_send, swap_recv, 0, pair)
    rim_copies = [
        remote(rims.at[0], rim_got.at[0], swap_send, swap_recv, 1, own_back),
        remote(rims.at[1], rim_got.at[1], swap_send, swap_recv, 2, swap_back),
    ]
    swapped.start()

    @pl.when(at.place > 0)
    def _():
        for copy in rim_copies:
            copy.start()

    gain_first = jnp.zeros((1, model), jnp.float32)
    for first in range(0, height, height // 2):
        unit = norm_rows(first, height // 2)[1]
        product = unit * part_ref[first : first + height // 2]
        gain_first = gain_first + jnp.sum(product, axis=0, keepdims=True)
    small_sum[...] = jnp.zeros_like(small_sum)
    for start, width, source in (
        (0, keys_width, 0),
        (2 * keys_width, keys_width, keys_width),
        (4 * keys_width, vals, 2 * keys_width),
    ):
        span = pl.ds(tile_start(start + core * width), width)
        small_sum[0:CONV, span] = conv_grad[0:CONV, source : source + width]
    small_sum[4:5, 0:model] = gain_first
    small_sum[4:5, model : 2 * model] = second_grad[...]
    small_sum[4:5, 2 * model : 2 * model + DV] = gain_grad[0:1]
    for line in range(2):
        found = head_grad[line : line + 1]
        moved = pltpu.roll(head_grad[...], 128 - heads, 1)[line : line + 1]
        small_sum[5:6, 128 * line : 128 * line + 128] = jnp.where(core == 0, moved, found)
    small_sum[5:6, 256:384] = loss_ref[...]

    def add_small(index):
        return remote(
            small_sum, small_got.at[index], small_send, small_recv, index, rounds[index]
        )

    left = agenda.pieces(len(rounds) + 1, 1.0)
    for index, found in enumerate(left):
        if index > 0:
            add_small(index - 1).wait()
            small_sum[...] += small_got[index - 1]
        if index < len(rounds):
            add_small(index).start()
        if index == 1:
            swapped.wait()

            @pl.when(at.place == count - 1)
            def _():
                rim_got[...] = jnp.zeros_like(rim_got)

            @pl.when(at.place < count - 1)
            def _():
                for copy in rim_copies:
                    copy.wait_recv()

            edge = rim_got[0].astype(jnp.float32) + rim_got[1].astype(jnp.float32)
            step = length // 4
            for first in range(0, length, step):
                scale, unit = norm_rows(PAD + first, step)
                grad = part_ref[PAD + first : PAD + first + step] + swap_got[
                    first : first + step
                ].astype(jnp.float32)
                if first + step == length:
                    grad = jnp.concatenate([grad[: step - PAD], grad[step - PAD :] + edge], axis=0)
                scaled = grad * gain
                back = scale * (scaled - unit * jnp.mean(scaled * unit, axis=1, keepdims=True))
                token_grad[first : first + step] = hidden_ref[first : first + step] + back
        run_steps(found)

    @pl.when(at.place > 0)
    def _():
        for copy in rim_copies:
            copy.wait_send()


FINAL_COLUMNS = 640


def backward_block(
    mixed_in, little, gate_pre, conv, head, gain, kept, grad_branch, inputs, norm_gain, grad_hidden,
    grad_second, loss_row, w_first, grad_down, grad_up, grad_out,
):
    groups, count = lax.axis_size("dp"), lax.axis_size("seq")
    rows, inner = grad_down.shape[2:]
    length = mixed_in.shape[1] - PAD
    units = kept[0].shape[0]
    mixed_width, vals = mixed_in.shape[2], gate_pre.shape[2]
    first_width = mixed_width + 128 + vals
    keys = (mixed_width - vals) // 2
    height, model = inputs.shape
    rounds = (groups.bit_length() - 1) + (count.bit_length() - 1)
    small = (8, 4 * keys + 2 * vals)
    kind = jnp.bfloat16

    def joined(width):
        return jax.ShapeDtypeStruct((rows, width), kind)

    return pl.pallas_call(
        functools.partial(backward_kernel, groups, count),
        out_shape=[
            jax.ShapeDtypeStruct((length, model), jnp.float32),
            jax.ShapeDtypeStruct(small, jnp.float32),
            joined(2 * inner),
            joined(2 * inner),
            joined(2 * inner),
            joined(2 * vals),
            joined(4 * keys + 4 * vals),
            joined(256),
            jax.ShapeDtypeStruct((count // 2, 2, rows, first_width), kind),
        ],
        in_specs=[ROOM] * 19 + [ANY] * 4,
        out_specs=[ROOM] * 8 + [ANY],
        scratch_shapes=[
            pltpu.VMEM((units, length, DV), jnp.float32),
            pltpu.VMEM((units, DK, DV), jnp.float32),
            pltpu.VMEM((units, DK, DV), jnp.float32),
            pltpu.VMEM((2, length, 128), jnp.float32),
            pltpu.VMEM((2, length, 128), jnp.float32),
            pltpu.VMEM((2, 128, length), jnp.float32),
            pltpu.VMEM((units, length, DV), kind),
            pltpu.VMEM((units, length, DV), jnp.float32),
            pltpu.VMEM((units, length, DK), jnp.float32),
            pltpu.VMEM((2, length, 128), jnp.float32),
            pltpu.VMEM((units, 8, length), jnp.float32),
            *relay_scratch(units),
            pltpu.VMEM((2, length + PAD, first_width), kind),
            pltpu.VMEM(conv.shape, jnp.float32),
            pltpu.VMEM((8, DV), jnp.float32),
            pltpu.VMEM((8, 128), jnp.float32),
            pltpu.VMEM((height, model), kind),
            pltpu.VMEM((count // 2, 2, rows, FINAL_COLUMNS), kind),
            pltpu.VMEM((height, model), jnp.float32),
            pltpu.VMEM((2, model // 4, first_width), kind),
            pltpu.VMEM((length, model), kind),
            pltpu.VMEM((length, model), kind),
            pltpu.VMEM((2, PAD, model), kind),
            pltpu.VMEM((2, PAD, model), kind),
            pltpu.VMEM((rounds,) + small, jnp.float32),
            pltpu.SemaphoreType.DMA,
            pltpu.SemaphoreType.DMA((2,)),
            pltpu.SemaphoreType.DMA((3,)),
            pltpu.SemaphoreType.DMA((3,)),
            pltpu.SemaphoreType.DMA((rounds,)),
            pltpu.SemaphoreType.DMA((rounds,)),
            *reduce_scratch(groups, count, rows, [inner] * 4 + [first_width // 2] * 2),
        ],
        compiler_params=pltpu.CompilerParams(
            collective_id=5, has_side_effects=True, vmem_limit_bytes=62 * 2**20
        ),
        name="backward_block",
    )(
        mixed_in, little, gate_pre, conv, head, gain, *kept, grad_branch, inputs, norm_gain,
        grad_hidden, grad_second, loss_row, w_first, grad_down, grad_up, grad_out,
    )


def third(width, weight):
    return 128 * max(1, round(width * weight / 128))


def norm_parts(field_in):
    scale = lax.rsqrt(jnp.mean(field_in * field_in, axis=-1, keepdims=True) + epsilon)
    return scale, field_in * scale


def norm_back(scale, unit, gain_vec, grad):
    scaled = grad * gain_vec
    return scale * (scaled - unit * jnp.mean(scaled * unit, axis=-1, keepdims=True))


def dense(left, right, dims):
    return lax.dot_general(left, right, (dims, ((), ())), preferred_element_type=jnp.float32)


def swiglu(gate_up):
    hidden_units = gate_up.shape[1] // 2
    return jax.nn.silu(gate_up[:, :hidden_units]) * gate_up[:, hidden_units:]


def on_device(
    tokens,
    target,
    valid,
    in_weight,
    small_weight,
    out_weight,
    ffn_in,
    ffn_out,
    gain_first,
    gain_second,
    gain_out,
    conv_weight,
    decay_log,
    decay_bias,
):
    count = lax.axis_size("seq")
    groups = lax.axis_size("dp")
    core = lax.axis_index("dp") % 2
    rows = in_weight.shape[0]
    length, model = tokens.shape[1], tokens.shape[2]
    both, padded = 2 * length, length + PAD
    heads = HEADS // 2
    keys, vals, inner = KEYS // 2, VALUES // 2, FF // 2
    mixed_width = 2 * keys + vals

    def mine(array, start, width):
        return lax.dynamic_slice_in_dim(array, start + core * width, width, array.ndim - 1)

    def qkv_half(array):
        parts = [mine(array, 0, keys), mine(array, KEYS, keys), mine(array, 2 * KEYS, vals)]
        return jnp.concatenate(parts, axis=1)

    small_half = [mine(small_weight, 0, heads), mine(small_weight, HEADS, heads)]
    spare = jnp.zeros((rows, 128 - 2 * heads), jnp.bfloat16)
    part_gate = mine(in_weight, 2 * KEYS + VALUES, vals)
    part_first = jnp.concatenate([qkv_half(in_weight)] + small_half + [spare, part_gate], axis=1)
    part_out = mine(out_weight, 0, vals)
    part_up = jnp.concatenate([mine(ffn_in, 0, inner), mine(ffn_in, FF, inner)], axis=1)
    part_down = mine(ffn_out, 0, inner)
    first_width = part_first.shape[1]

    mask_own = valid[0].astype(jnp.float32)
    mask_rows = jnp.broadcast_to(mask_own[None, :], (8, length))
    own_conv = jnp.concatenate([qkv_half(conv_weight), jnp.zeros((8 - CONV, mixed_width))], axis=0)
    lanes = ((0, 0), (heads, 128 - 2 * heads))
    head = jnp.concatenate(
        [
            jnp.pad(-jnp.exp(mine(decay_log, 0, heads))[None], lanes),
            jnp.pad(mine(decay_bias, 0, heads)[None], lanes),
            jnp.zeros((6, 128), jnp.float32),
        ],
        axis=0,
    )
    gain_row = gain_out[None]
    parts = [part_first, part_out, part_up, part_down]
    (
        inputs, target_other, mask_other, mixed_in, little, gate_pre, branch, *kept,
        w_first, w_out, w_up, w_down,
    ) = forward_block(
        tokens[0], target[0], mask_rows, gain_first[None], own_conv, head, gain_row,
        parts, [third(v.shape[1], 0.33) for v in parts],
    )
    branch = branch.reshape(both, vals)
    w_first, w_out, w_up, w_down = (
        v.reshape(model, v.shape[2]) for v in (w_first, w_out, w_up, w_down)
    )

    def core_sum(part):
        pairs = [(group, group ^ 1) for group in range(groups)]
        got = lax.ppermute(part.astype(jnp.bfloat16), "dp", pairs)
        return part + jnp.concatenate([got[length:], got[:length]], axis=0).astype(jnp.float32)

    positions = jnp.concatenate([tokens[0], inputs[padded + PAD :]], axis=0).astype(jnp.float32)
    hidden = positions + core_sum(dense(branch, w_out, ((1,), (1,))))
    second_scale, second_unit = norm_parts(hidden)
    second = (second_unit * gain_second).astype(jnp.bfloat16)
    gate_up = dense(second, w_up, ((1,), (0,)))
    active_f, swiglu_pull = jax.vjp(swiglu, gate_up)
    active = active_f.astype(jnp.bfloat16)
    summed = hidden + core_sum(dense(active, w_down, ((1,), (1,))))
    mask = jnp.concatenate([mask_own, mask_other[0]])
    errors = summed - jnp.concatenate([target[0], target_other]).astype(jnp.float32)
    own_errors = errors[:length]
    loss_part = jnp.sum(mask_own * jnp.mean(own_errors * own_errors, axis=-1))

    grad_summed = mask[:, None] * errors
    grad_feed = grad_summed.astype(jnp.bfloat16)
    grad_active = dense(grad_feed, w_down, ((1,), (0,)))
    grad_down = dense(grad_feed, active, ((0,), (0,))).astype(jnp.bfloat16)
    grad_gate_up = swiglu_pull(grad_active)[0].astype(jnp.bfloat16)
    grad_up = dense(second, grad_gate_up, ((0,), (0,))).astype(jnp.bfloat16)
    grad_second = core_sum(dense(grad_gate_up, w_up, ((1,), (1,))))
    grad_gain_second = jnp.sum((grad_second * second_unit)[:length], axis=0)
    grad_hidden = grad_summed + norm_back(second_scale, second_unit, gain_second, grad_second)
    grad_attn = grad_hidden.astype(jnp.bfloat16)
    grad_out = dense(grad_attn, branch, ((0,), (0,))).astype(jnp.bfloat16)
    grad_branch = dense(grad_attn, w_out, ((1,), (0,))).reshape(2, length, vals)

    def by_place(array):
        return array.reshape(count // 2, 2, rows, array.shape[1])

    grad_up = by_place(grad_up)
    loss_row = jnp.concatenate(
        [loss_part[None], jnp.sum(mask_own)[None], jnp.zeros((126,), jnp.float32)]
    )[None]
    grad_tokens, small_sum, sum_down, sum_gate, sum_up, sum_out, sum_in, sum_small, unused = backward_block(
        mixed_in, little, gate_pre, own_conv, head, gain_row, kept, grad_branch,
        inputs, gain_first[None], grad_hidden[:length], grad_gain_second[None], loss_row, w_first,
        by_place(grad_down), grad_up, by_place(grad_out),
    )
    valid_count = jnp.maximum(small_sum[5, 257], 1.0)
    loss_value = small_sum[5, 256] / valid_count
    factor = length * groups * count / valid_count
    sum_small = jnp.concatenate(
        [
            sum_small[:, 0:heads],
            sum_small[:, 128 : 128 + heads],
            sum_small[:, heads : 2 * heads],
            sum_small[:, 128 + heads : 128 + 2 * heads],
        ],
        axis=1,
    )

    def scaled(array):
        return array.astype(jnp.float32) * factor

    return (
        summed[:length].astype(jnp.bfloat16)[None],
        loss_value,
        scaled(grad_tokens)[None],
        scaled(sum_in),
        scaled(sum_small),
        scaled(sum_out),
        scaled(jnp.concatenate([sum_gate, sum_up], axis=1)),
        scaled(sum_down),
        scaled(small_sum[4, :model]),
        scaled(small_sum[4, model : 2 * model]),
        scaled(small_sum[4, 2 * model : 2 * model + DV]),
        scaled(small_sum[:CONV]),
        scaled(small_sum[5, :HEADS]),
        scaled(small_sum[5, 128 : 128 + HEADS]),
    )


def solution(mesh):
    placed = (
        P("dp", "seq", None),
        P("dp", "seq", None),
        P("dp", "seq"),
        P("seq", None),
        P("seq", None),
        P("seq", None),
        P("seq", None),
        P("seq", None),
        P(),
        P(),
        P(),
        P(),
        P(),
        P(),
    )
    return jax.shard_map(
        on_device,
        mesh=mesh,
        in_specs=placed,
        out_specs=(
            P("dp", "seq", None),
            P(),
            P("dp", "seq", None),
            P("seq", None),
            P("seq", None),
            P("seq", None),
            P("seq", None),
            P("seq", None),
            P(),
            P(),
            P(),
            P(),
            P(),
            P(),
        ),
        check_vma=False,
    )
```

```python
import functools

import jax
import jax.numpy as jnp
from jax import lax
from jax.experimental import pallas as pl
from jax.experimental.pallas import tpu as pltpu
from jax.sharding import PartitionSpec as P

HEADS = 6
DK = 128
DV = 256
FF = 2816
CONV = 4
BLOCK = 64
KEYS = 768
VALUES = 1536


precise = lax.Precision.HIGHEST
epsilon = 1e-06


MESH = pl.DeviceIdType.MESH
NN = (((1,), (0,)), ((), ()))
NT = (((1,), (1,)), ((), ()))
TN = (((0,), (0,)), ((), ()))


def exact(left, right, dims=NN):
    return lax.dot_general(
        left, right, dims, precision=precise, preferred_element_type=jnp.float32
    )


def near(left, right, dims=NN):
    return lax.dot_general(
        left.astype(jnp.bfloat16),
        right.astype(jnp.bfloat16),
        dims,
        preferred_element_type=jnp.float32,
    )


def close(left, right, dims=NN):
    left_top, right_top = left.astype(jnp.bfloat16), right.astype(jnp.bfloat16)
    left_rest = (left - left_top.astype(jnp.float32)).astype(jnp.bfloat16)
    right_rest = (right - right_top.astype(jnp.float32)).astype(jnp.bfloat16)
    return (
        near(left_rest, right_top, dims) + near(left_top, right_rest, dims)
    ) + near(left_top, right_top, dims)


def iotas(rows, columns):
    return (
        lax.broadcasted_iota(jnp.int32, (rows, columns), 0),
        lax.broadcasted_iota(jnp.int32, (rows, columns), 1),
    )


def decay_table(gcol, grow):
    size = gcol.shape[0]
    row, col = iotas(size, size)
    keep = row >= col
    return jnp.where(keep, jnp.exp(jnp.where(keep, gcol - grow, 0.0)), 0.0)


def tile_start(start):
    return pl.multiple_of(start, 128)


class Place:
    def __init__(self, groups, count):
        self.groups, self.count, self.half = groups, count, count // 2
        self.group, self.place = lax.axis_index("dp"), lax.axis_index("seq")
        self.pair, self.side = self.place // 2, self.place % 2
        self.plane = (self.group // 2) % 2
        self.group_swap = self.group + 1 - 2 * (self.group % 2)
        self.across = self.group + 2 - 4 * self.plane
        self.beside = self.place + 1 - 2 * self.side

    def shard(self, pair, side):
        return 2 * pair + side

    def ahead(self, step):
        return lax.rem(self.pair + step, self.half)

    def behind(self, step):
        return lax.rem(self.pair + self.half - step, self.half)

    def partners(self):
        along = [(self.group, self.shard(self.ahead(step), self.side)) for step in range(1, self.half)]
        return along + [(self.group, self.beside), (self.across, self.place)]


def greet(signalled, awaited):
    barrier = pltpu.get_barrier_semaphore()
    for device in signalled:
        pl.semaphore_signal(barrier, inc=1, device_id=device, device_id_type=MESH)
    pl.semaphore_wait(barrier, awaited)


def remote(source, target, sends, receives, index, device):
    return pltpu.make_async_remote_copy(
        src_ref=source,
        dst_ref=target,
        send_sem=sends.at[index],
        recv_sem=receives.at[index],
        device_id=device,
        device_id_type=MESH,
    )


class Gather:
    def __init__(self, at, source, target, lines, share, sends, receives, local):
        self.at, self.source, self.target, self.lines = at, source, target, lines
        self.sends, self.receives, self.local = sends, receives, local
        width = source.shape[1]
        self.own = pl.ds(tile_start(at.plane * share), width - share)
        self.lent = pl.ds(tile_start(at.plane * (width - share)), share)
        self.borrowed = pl.ds(tile_start((1 - at.plane) * (width - share)), share)
        self.started = {}

    def copy(self, index, shard, columns, device, from_source=False):
        there = self.target.at[shard, self.lines, columns]
        here = self.source.at[self.lines, columns] if from_source else there
        return remote(here, there, self.sends, self.receives, index, device)

    def along(self, step):
        at = self.at
        device = (at.group, at.shard(at.ahead(step), at.side))
        return self.copy(step - 1, at.place, self.own, device, True)

    def beside(self, step):
        at = self.at
        shard = at.shard(at.behind(step), at.side)
        return self.copy(at.half - 1 + step, shard, self.own, (at.group, at.beside), step == 0)

    def across(self, step, side):
        at = self.at
        shard = at.shard(at.behind(step), at.side if side == 0 else 1 - at.side)
        return self.copy(2 * at.half - 1 + 2 * step + side - 1, shard, self.lent, (at.across, at.place))

    def keep(self):
        return pltpu.make_async_copy(
            self.source.at[self.lines], self.target.at[self.at.place, self.lines], self.local
        )

    def launch(self, make, *where):
        make(*where).start()
        self.started[make.__name__, where] = make

    def begin(self):
        self.keep().start()
        for step in range(1, self.at.half):
            self.launch(self.along, step)
        self.launch(self.beside, 0)

    def arrived(self, index, shard, columns):
        self.copy(index, shard, columns, (self.at.group, self.at.place)).wait_recv()

    def pass_along(self, step):
        at = self.at
        self.arrived(step - 1, at.shard(at.behind(step), at.side), self.own)
        self.launch(self.beside, step)
        self.launch(self.across, step, 0)

    def pass_beside(self, step):
        at = self.at
        self.arrived(at.half - 1 + step, at.shard(at.behind(step), 1 - at.side), self.own)
        self.launch(self.across, step, 1)

    def take_across(self):
        at = self.at
        for step in range(at.half):
            for side in range(2):
                if step or side:
                    shard = at.shard(at.behind(step), at.side if side == 0 else 1 - at.side)
                    self.arrived(2 * at.half - 1 + 2 * step + side - 1, shard, self.borrowed)
        self.keep().wait()

    def finish(self):
        for (unused, where), make in self.started.items():
            make(*where).wait_send()

    def stages(self):
        half = self.at.half
        first = [functools.partial(self.pass_along, step) for step in range(1, half)]
        second = [functools.partial(self.pass_beside, step) for step in range(half)]
        return [first, second, [self.take_across]]


def copies_of_gather(count):
    return 2 * count - 2


def lagged(plans, lag):
    depth = max(len(plan) for plan in plans)
    turns = []
    for turn in range(len(plans) + lag * (depth - 1)):
        steps = []
        for index, plan in enumerate(plans):
            stage, rest = divmod(turn - index, lag)
            if rest == 0 and 0 <= stage < len(plan):
                steps = plan[stage] + steps
        turns.append(steps)
    return turns


class Work:
    def __init__(self, given, base, width, share, spots):
        self.given, self.base, self.width, self.share, self.spots = given, base, width, share, spots


class Reduce:
    def __init__(self, at, work, lines, buffers, sems):
        self.at, self.given, self.spots, self.lines = at, work.given, work.spots, lines
        self.sends, self.receives, self.local = sems
        width, share = work.width, work.share
        self.wide = width - share
        wide, narrow, full = pl.ds(0, self.wide), pl.ds(0, share), pl.ds(0, width)
        self.acc = buffers[0].at[:, :, :, wide]
        self.from_across = buffers[1].at[:, :, :, narrow]
        self.from_beside, self.from_along = buffers[2].at[:, :, wide], buffers[3].at[:, :, wide]
        self.part, self.from_plane = buffers[4].at[:, wide], buffers[5].at[:, wide]
        self.total, self.other = buffers[6].at[:, full], buffers[7].at[:, full]
        self.far = buffers[8].at[:, :, full] if at.groups > 4 else None
        self.own = pl.ds(tile_start(at.plane * share), self.wide)
        self.given_own = pl.ds(tile_start(work.base + at.plane * share), self.wide)
        self.given_lent = pl.ds(tile_start(work.base + (1 - at.plane) * self.wide), share)
        self.inner = pl.ds(tile_start(at.plane * (width - 2 * share)), share)
        self.theirs = pl.ds(tile_start((1 - at.plane) * share), self.wide)

    def side(self, mine):
        return self.at.side if mine else 1 - self.at.side

    def across(self, mine):
        at = self.at
        return remote(
            self.given.at[:, self.side(mine), self.lines, self.given_lent], self.from_across.at[mine],
            self.sends, self.receives, mine, (at.across, at.place),
        )

    def load(self, mine):
        return pltpu.make_async_copy(
            self.given.at[:, self.side(mine), self.lines, self.given_own], self.acc.at[mine],
            self.local.at[mine],
        )

    def beside(self):
        at = self.at
        return remote(
            self.acc.at[0], self.from_beside, self.sends, self.receives, 2, (at.group, at.beside)
        )

    def along(self, step):
        at = self.at
        pair = at.ahead(step)
        return remote(
            self.acc.at[1, pair], self.from_along.at[step - 1],
            self.sends, self.receives, 4 + step, (at.group, at.shard(pair, at.side)),
        )

    def plane(self):
        at = self.at
        return remote(
            self.part, self.from_plane, self.sends, self.receives, 3, (at.across, at.place)
        )

    def core(self):
        at = self.at
        return remote(
            self.total, self.other, self.sends, self.receives, 4, (at.group_swap, at.place)
        )

    def further(self, index, distance):
        at = self.at
        group = at.group + distance - 2 * distance * ((at.group // distance) % 2)
        return remote(
            self.total, self.far.at[index], self.sends, self.receives,
            4 + at.half + index, (group, at.place),
        )

    def begin(self):
        for mine in range(2):
            self.load(mine).start()
            self.across(mine).start()

    def add_across(self, mine):
        self.load(mine).wait()
        self.across(mine).wait_recv()
        held = self.acc[mine, :, :, self.inner].astype(jnp.float32)
        got = self.from_across[mine].astype(jnp.float32)
        self.acc[mine, :, :, self.inner] = (held + got).astype(jnp.bfloat16)
        if not mine:
            self.beside().start()

    def add_beside(self):
        self.beside().wait_recv()
        for step in range(1, self.at.half + 1):
            pair = self.at.ahead(step)
            held = self.acc[1, pair].astype(jnp.float32)
            got = self.from_beside[pair].astype(jnp.float32)
            self.acc[1, pair] = (held + got).astype(jnp.bfloat16)
            if step < self.at.half:
                self.along(step).start()

    def add_along(self):
        value = self.acc[1, self.at.pair].astype(jnp.float32)
        for step in range(1, self.at.half):
            self.along(step).wait_recv()
            value = value + self.from_along[step - 1].astype(jnp.float32)
        self.part[...] = value.astype(jnp.bfloat16)
        self.plane().start()

    def add_plane(self):
        self.plane().wait_recv()
        self.total[...] = jnp.zeros_like(self.total)
        self.total[:, self.own] = self.part[...]
        held = self.total[:, self.theirs].astype(jnp.float32)
        got = self.from_plane[...].astype(jnp.float32)
        self.total[:, self.theirs] = (held + got).astype(jnp.bfloat16)
        distance = 4
        while distance < self.at.groups:
            index = distance.bit_length() - 3
            copy = self.further(index, distance)
            copy.start()
            copy.wait()
            got = self.far[index].astype(jnp.float32)
            self.total[...] = (self.total[...].astype(jnp.float32) + got).astype(jnp.bfloat16)
            distance *= 2
        self.core().start()

    def deliver(self):
        self.core().wait_recv()
        core = self.at.group % 2
        for target, start, stride, width, source in self.spots:
            for held, which in ((self.total, core), (self.other, 1 - core)):
                span = pl.ds(tile_start(start + which * stride), width)
                target[self.lines, span] = held[:, source : source + width]

    def finish(self):
        copies = [self.across(0), self.across(1), self.beside(), self.plane(), self.core()]
        copies += [self.along(step) for step in range(1, self.at.half)]
        for copy in copies:
            copy.wait_send()

    def stages(self):
        return [
            [functools.partial(self.add_across, 0)],
            [functools.partial(self.add_across, 1), self.add_beside],
            [self.add_along],
            [self.add_plane],
            [self.deliver],
        ]


ANY = pl.BlockSpec(memory_space=pl.ANY)
ROOM = pl.BlockSpec(memory_space=pltpu.VMEM)
PAD = 16
CHUNKS, WINDOW, GATHER_LAG = 4, 3, 2
REDUCE_CHUNKS, REDUCE_WINDOW, REDUCE_LAG, POOL = 4, 2, 1, 6


def neighbours(at, step):
    place = lax.rem(at.place + at.count + step, at.count)
    return (at.group, place), (at.group_swap, place)


def chunks_of(rows):
    return max(1, min(CHUNKS, rows // 16))


def gather_sems(count, rows, number):
    chunks = chunks_of(rows)
    return [
        pltpu.SemaphoreType.DMA((number * chunks, copies_of_gather(count))),
        pltpu.SemaphoreType.DMA((number * chunks, copies_of_gather(count))),
        pltpu.SemaphoreType.DMA((number * chunks,)),
    ]


def gather_plans(at, sources, targets, shares, sends, receives, local):
    rows = sources[0].shape[0]
    chunks = chunks_of(rows)
    lines = rows // chunks
    return [
        Gather(
            at, sources[i], targets[i], pl.ds(part * lines, lines), shares[i],
            sends.at[i * chunks + part], receives.at[i * chunks + part], local.at[i * chunks + part],
        )
        for i in range(len(sources))
        for part in range(chunks)
    ]


def gather_steps(plans):
    steps = [plan.begin for plan in plans[:WINDOW]]
    for index, turn in enumerate(lagged([plan.stages() for plan in plans], GATHER_LAG)):
        steps += turn
        if index + WINDOW < len(plans):
            steps.append(plans[index + WINDOW].begin)
    return steps + [plan.finish for plan in plans]


def reduce_steps(plans):
    steps = [plan.begin for plan in plans[:REDUCE_WINDOW]]
    for index, turn in enumerate(lagged([plan.stages() for plan in plans], REDUCE_LAG)):
        steps += turn
        later = index + REDUCE_WINDOW
        if later < len(plans):
            if later >= POOL:
                steps.append(plans[later - POOL].finish)
            steps.append(plans[later].begin)
    return steps + [plan.finish for plan in plans[-POOL:]]


def reduce_buffers(groups, count, rows, width, share):
    wide, half = width - share, count // 2
    kind = jnp.bfloat16
    far = (max(1, (groups // 4).bit_length() - 1), rows, width) if groups > 4 else (1, 16, 128)
    return [
        pltpu.VMEM((2, half, rows, wide), kind),
        pltpu.VMEM((2, half, rows, share), kind),
        pltpu.VMEM((half, rows, wide), kind),
        pltpu.VMEM((half - 1, rows, wide), kind),
        pltpu.VMEM((rows, wide), kind),
        pltpu.VMEM((rows, wide), kind),
        pltpu.VMEM((rows, width), kind),
        pltpu.VMEM((rows, width), kind),
        pltpu.VMEM(far, kind),
    ]


def copies_of_reduce(groups, count):
    return count // 2 + 4 + max(1, (groups // 4).bit_length() - 1)


def further_groups(at):
    found, distance = [], 4
    while distance < at.groups:
        found.append((at.group + distance - 2 * distance * ((at.group // distance) % 2), at.place))
        distance *= 2
    return found


def reduce_plans(at, works, scratch):
    rows = works[0].given.shape[2]
    chunks = reduce_chunks(rows)
    lines = rows // chunks
    sends, receives, local = scratch[9 * POOL : 9 * POOL + 3]
    plans = []
    for work in works:
        for part in range(chunks):
            spot = len(plans)
            slot = spot % POOL
            plans.append(
                Reduce(
                    at, work, pl.ds(part * lines, lines), scratch[9 * slot : 9 * slot + 9],
                    (sends.at[spot], receives.at[spot], local.at[spot]),
                )
            )
    return plans


def reduce_chunks(rows):
    return max(1, min(REDUCE_CHUNKS, rows // 16))


def reduce_scratch(groups, count, rows, widths):
    chunks = reduce_chunks(rows)
    width = max(widths)
    scratch = reduce_buffers(groups, count, rows // chunks, width, reduce_share(width)) * POOL
    number, copies = len(widths) * chunks, copies_of_reduce(groups, count)
    return scratch + [
        pltpu.SemaphoreType.DMA((number, copies)),
        pltpu.SemaphoreType.DMA((number, copies)),
        pltpu.SemaphoreType.DMA((number, 2)),
    ]


def reduce_share(width):
    return third(width, 0.28)


class Relay:
    def __init__(self, at, forward, units, sending, arriving, sends, receives):
        self.at, self.units = at, units
        self.sending, self.arriving, self.sends, self.receives = sending, arriving, sends, receives
        last = at.count - 1
        step = 1 if forward else -1
        self.is_first = at.place == (0 if forward else last)
        self.is_last = at.place == (last if forward else 0)
        self.beyond = (at.group, lax.rem(at.place + at.count + step, at.count))
        self.before = (at.group, lax.rem(at.place + at.count - step, at.count))

    def copy(self, unit):
        return remote(
            self.sending.at[unit], self.arriving.at[unit], self.sends, self.receives, unit, self.beyond
        )

    def receive(self, unit, target):
        @pl.when(self.is_first)
        def _():
            target[unit] = jnp.zeros(target.shape[1:], jnp.float32)

        @pl.when(jnp.logical_not(self.is_first))
        def _():
            self.copy(unit).wait_recv()
            target[unit] = self.arriving[unit].astype(jnp.float32)

    def send(self, unit, value):
        @pl.when(jnp.logical_not(self.is_last))
        def _():
            self.sending[unit] = value().astype(jnp.bfloat16)
            self.copy(unit).start()

    def finish(self):
        @pl.when(jnp.logical_not(self.is_last))
        def _():
            for unit in range(self.units):
                self.copy(unit).wait_send()


def relay_scratch(units):
    return [
        pltpu.VMEM((units, DK, DV), jnp.bfloat16),
        pltpu.VMEM((units, DK, DV), jnp.bfloat16),
        pltpu.SemaphoreType.DMA((units,)),
        pltpu.SemaphoreType.DMA((units,)),
    ]


class Agenda:
    def __init__(self, steps):
        self.steps, self.done = steps, 0

    def take(self, upto):
        upto = max(upto, self.done)
        found, self.done = self.steps[self.done : upto], upto
        return found

    def until(self, share):
        for step in self.take(int(len(self.steps) * share)):
            step()

    def pieces(self, number, share):
        found = self.take(int(len(self.steps) * share))
        cuts = [len(found) * i // number for i in range(number + 1)]
        return [found[low:high] for low, high in zip(cuts, cuts[1:])]

    def loop(self, rounds, end, stage):
        pieces = self.pieces(rounds * PAUSES, end)
        taken = []

        def body(index, carry):
            for pause, unused in enumerate(stage(index)):
                taken.append(pause)
                for other in range(rounds):
                    found = pieces[other * PAUSES + pause]
                    if found:
                        pl.when(index == other)(functools.partial(run_steps, found))
            return carry

        lax.fori_loop(0, rounds, body, 0)
        assert len(taken) == PAUSES

    def around(self, rounds, turn, end, stage, main):
        pieces = self.pieces(rounds, end)

        def body(index, carry):
            stage(index)
            for other, found in enumerate(pieces):
                if found:
                    pl.when(index == other)(functools.partial(run_steps, found))
            return carry

        split = jnp.minimum(turn, rounds)
        lax.fori_loop(0, split, body, 0)
        main()
        lax.fori_loop(split, rounds, body, 0)


def run_steps(steps):
    for step in steps:
        step()


PAUSES = 9


def lockstep(stages):
    for unused in zip(*stages):
        yield


def rolled(value, shift):
    shift = shift % value.shape[0]
    return value if shift == 0 else pltpu.roll(value, shift, 0)


def silu_parts(value):
    gate = jax.nn.sigmoid(value)
    return value * gate, gate * (1.0 + value * (1.0 - gate))


def lane_start(start):
    return start if isinstance(start, int) else tile_start(start)


class Unit:
    def __init__(self, seq, head, heads, mixed_ref, conv_ref):
        self.seq, self.head = seq, head
        self.mixed_ref, self.conv_ref = mixed_ref, conv_ref
        keys = heads * DK
        self.columns = [
            (lane_start(self.head * DK), DK),
            (lane_start(keys + self.head * DK), DK),
            (lane_start(2 * keys + self.head * DV), DV),
        ]

    def taps(self, part):
        start, width = self.columns[part]
        span = pl.ds(start, width)
        field = self.mixed_ref[self.seq, :, span].astype(jnp.float32)
        weights = self.conv_ref[:, span]
        shifts = [rolled(field, CONV - 1 - tap)[PAD:] for tap in range(CONV)]
        value = weights[0:1] * shifts[0]
        for tap in range(1, CONV):
            value = value + weights[tap : tap + 1] * shifts[tap]
        return shifts, weights, value

    def rows(self, part):
        value = self.taps(part)[2]
        active = value * jax.nn.sigmoid(value)
        if part == 2:
            return active
        unit = active * lax.rsqrt(jnp.sum(active * active, axis=1, keepdims=True) + epsilon)
        return unit * DK ** (-0.5) if part == 0 else unit

    def taps_back(self, part, grad, grad_ref, conv_grad_ref):
        shifts, weights, value = self.taps(part)
        active, slope = silu_parts(value)
        if part < 2:
            scale = lax.rsqrt(jnp.sum(active * active, axis=1, keepdims=True) + epsilon)
            unit = active * scale
            grad = grad * DK ** (-0.5) if part == 0 else grad
            grad = scale * (grad - unit * jnp.sum(grad * unit, axis=1, keepdims=True))
        grad = grad * slope
        start, width = self.columns[part]
        span = pl.ds(start, width)
        row = lax.broadcasted_iota(jnp.int32, (8, width), 0)
        taps = jnp.zeros((8, width), jnp.float32)
        longer = jnp.concatenate([jnp.zeros((PAD, width), jnp.float32), grad], axis=0)
        total = jnp.zeros(longer.shape, jnp.float32)
        for tap in range(CONV):
            taps = taps + jnp.where(row == tap, jnp.sum(grad * shifts[tap], axis=0, keepdims=True), 0.0)
            total = total + weights[tap : tap + 1] * rolled(longer, tap - (CONV - 1))
        grad_ref[self.seq, :, span] = total.astype(jnp.bfloat16)
        conv_grad_ref[:, span] += taps


def head_tables(little_ref, head_ref, g_ref, grow_ref):
    seqs, size = little_ref.shape[0], g_ref.shape[1]
    row, col = iotas(size, size)
    below = (row >= col).astype(jnp.float32)
    above = (row <= col).astype(jnp.float32)
    for seq in range(seqs):
        forget = head_ref[0:1] * jax.nn.softplus(little_ref[seq, PAD:, :] + head_ref[1:2])
        g_ref[seq] = exact(below, forget)
        grow_ref[seq] = exact(forget, above, TN)


def head_columns(seq, head, heads, little_ref, g_ref, grow_ref):
    size = g_ref.shape[1]
    lane = lax.broadcasted_iota(jnp.int32, (size, 128), 1)
    line = lax.broadcasted_iota(jnp.int32, (128, size), 0)

    def column(table, index):
        return jnp.sum(jnp.where(lane == index, table, 0.0), axis=1, keepdims=True)

    beta = column(jax.nn.sigmoid(little_ref[seq, PAD:, :]), head)
    gcol = column(g_ref[seq], heads + head)
    grow = jnp.sum(jnp.where(line == heads + head, grow_ref[seq], 0.0), axis=0, keepdims=True)
    return beta, gcol, grow


def merged(inverses, systems, width):
    size = systems[0].shape[0]
    row, col = iotas(size, size)
    joined = (row // (2 * width) == col // (2 * width)) & (row // width != col // width)
    inner = [close(jnp.where(joined, system, 0.0), inverse) for system, inverse in zip(systems, inverses)]
    return [inverse - close(inverse, value) for inverse, value in zip(inverses, inner)]


def forward_kernel(groups, count, shares, *refs):
    number = len(shares)
    tokens_ref, target_ref, mask_ref, norm_ref, conv_ref, head_ref, gain_ref, second_gain = refs[:8]
    in_weight, small_part, out_weight, ffn_in, ffn_out = refs[8:13]
    refs = refs[13:]
    inputs_ref, target_other, mask_other, mixed_ref, little_ref, gate_ref = refs[:6]
    branch_ref, out_ref, t_ref, u_ref, w_ref, m_ref, e_ref, s_ref = refs[6:14]
    hidden_ref, second_ref, gate_up_ref, active_ref = refs[14:18]
    targets, refs = refs[18 : 18 + number], refs[18 + number :]
    normed, b_ref, g_ref, grow_ref, sending, arriving, relay_send, relay_recv = refs[:8]
    half_sent, half_got, pack_sem, swap_send, swap_recv = refs[8:13]
    sources, refs = refs[13 : 13 + number], refs[13 + number :]
    sends, receives, local = refs
    units = t_ref.shape[0]
    heads = units // 2
    size = t_ref.shape[1]
    half = size // 2
    at = Place(groups, count)
    line = Relay(at, True, units, sending, arriving, relay_send, relay_recv)
    core = (at.group_swap, at.place)
    heads_width, inner = heads * DK, sources[3].shape[1]
    vals = heads * DV
    spans = [
        (0, in_weight, 0, heads_width, 0),
        (0, in_weight, 2 * heads_width, heads_width, heads_width),
        (0, in_weight, 4 * heads_width, vals, 2 * heads_width),
        (0, in_weight, 4 * heads_width + 2 * vals, vals, 2 * heads_width + vals + 128),
        (1, out_weight, 0, vals, 0),
        (2, ffn_in, 0, inner, 0),
        (2, ffn_in, 2 * inner, inner, inner),
        (3, ffn_out, 0, inner, 0),
    ]
    packs = [[], [], [], []]
    for index, (matrix, weight, start, width, place) in enumerate(spans):
        span = pl.ds(tile_start(start + (at.group % 2) * width), width)
        packs[matrix].append(
            pltpu.make_async_copy(
                weight.at[:, span], sources[matrix].at[:, pl.ds(place, width)], pack_sem.at[index]
            )
        )
    packs[0].append(
        pltpu.make_async_copy(
            small_part, sources[0].at[:, pl.ds(2 * heads_width + vals, 128)], pack_sem.at[len(spans)]
        )
    )
    for pack in packs:
        for copy in pack:
            copy.start()
    greet(at.partners() + [line.before, core] + list(neighbours(at, -1)), count // 2 + 5)
    padded = size + PAD
    swaps = [
        remote(here, there, swap_send, swap_recv, index, core)
        for index, (here, there) in enumerate((
            (tokens_ref, inputs_ref.at[pl.ds(padded + PAD, size)]),
            (target_ref, target_other),
            (mask_ref, mask_other),
        ))
    ]
    tail = tokens_ref.at[pl.ds(size - PAD, PAD)]
    own_next, swap_next = neighbours(at, 1)
    rims = [
        remote(tail, inputs_ref.at[pl.ds(0, PAD)], swap_send, swap_recv, 3, own_next),
        remote(tail, inputs_ref.at[pl.ds(padded, PAD)], swap_send, swap_recv, 4, swap_next),
    ]
    swaps[0].start()

    @pl.when(at.place < count - 1)
    def _():
        for copy in rims:
            copy.start()

    plans = gather_plans(at, sources, targets, shares, sends, receives, local)
    agenda = Agenda(gather_steps(plans))
    for pack in packs:
        for copy in pack:
            copy.wait()
    run_steps(agenda.take(WINDOW))
    for copy in swaps[1:]:
        copy.start()
    inputs_ref[PAD:padded] = tokens_ref[...]

    @pl.when(at.place == 0)
    def _():
        inputs_ref[:PAD] = jnp.zeros((PAD, inputs_ref.shape[1]), jnp.bfloat16)
        inputs_ref[padded : padded + PAD] = jnp.zeros((PAD, inputs_ref.shape[1]), jnp.bfloat16)

    @pl.when(at.place > 0)
    def _():
        for copy in rims:
            copy.wait_recv()

    swaps[0].wait()
    for seq in range(2):
        value = inputs_ref[seq * padded : (seq + 1) * padded].astype(jnp.float32)
        scale = lax.rsqrt(jnp.mean(value * value, axis=1, keepdims=True) + epsilon)
        normed[seq * padded : (seq + 1) * padded] = (value * scale * norm_ref[...]).astype(jnp.bfloat16)
    first_chunks = len(plans) // number
    run_steps(agenda.take(agenda.steps.index(plans[first_chunks - 1].take_across) + 1))

    weight = targets[0]
    model = normed.shape[1]
    mixed_width = mixed_ref.shape[2]
    cuts = [0, mixed_width // 2, mixed_width, mixed_width + 128, weight.shape[2]]
    for start, end in zip(cuts, cuts[1:]):
        value = dense(normed[...], weight[:, :, start:end].reshape(model, end - start), ((1,), (0,)))
        value = value.reshape(2, padded, end - start)
        if end <= mixed_width:
            mixed_ref[:, :, start:end] = value.astype(jnp.bfloat16)
        elif end == mixed_width + 128:
            little_ref[...] = value
        else:
            gate_ref[...] = value
        agenda.until(agenda.done / len(agenda.steps) + FORWARD_PROJECT / 4)
    head_tables(little_ref, head_ref, g_ref, grow_ref)

    def local_stage(seq, head):
        unit = seq * heads + head
        own = Unit(seq, head, heads, mixed_ref, conv_ref)
        beta, gcol, grow = head_columns(seq, head, heads, little_ref, g_ref, grow_ref)
        decays = decay_table(gcol, grow)
        keys = own.rows(1)
        row, col = iotas(size, size)
        system = jnp.where(row > col, beta * close(keys, keys, NT) * decays, 0.0)
        yield
        systems = [system[:half, :half], system[half:, half:]]
        row, col = iotas(half, half)
        inverses = [
            (row == col).astype(jnp.float32) - jnp.where(row // 2 == col // 2, value, 0.0)
            for value in systems
        ]
        width = 2
        while width < half:
            inverses = merged(inverses, systems, width)
            width *= 2
            yield
        corner = -close(inverses[1], close(system[half:, :half], inverses[0]))
        t_ref[unit, :half, :half] = inverses[0]
        t_ref[unit, :half, half:] = jnp.zeros((half, half), jnp.float32)
        t_ref[unit, half:, :half] = corner
        t_ref[unit, half:, half:] = inverses[1]
        solve = t_ref[unit]
        growth = jnp.exp(gcol)
        last = gcol[size - 1 :, :]
        update = near(solve, beta * own.rows(2))
        back = near(solve, (beta * growth) * keys)
        u_ref[unit] = update
        w_ref[unit] = back
        yield
        weighted = keys * jnp.exp(last - gcol)
        drow, dcol = iotas(DK, DK)
        m_ref[unit] = jnp.where(drow == dcol, jnp.exp(last), 0.0) - near(weighted, back, TN)
        b_ref[unit] = near(weighted, update, TN)
        yield

    agenda.loop(2, FORWARD_LOCAL, lambda seq: lockstep([local_stage(seq, h) for h in range(heads)]))

    def pass_on():
        for unit in range(units):
            line.receive(unit, s_ref)
            line.send(unit, lambda: close(m_ref[unit], s_ref[unit]) + b_ref[unit])

    def score_stage(unit):
        seq, head = unit // heads, unit % heads
        own = Unit(seq, head, heads, mixed_ref, conv_ref)
        unused, gcol, grow = head_columns(seq, head, heads, little_ref, g_ref, grow_ref)
        queries = own.rows(0)
        scores = near(queries, own.rows(1), NT) * decay_table(gcol, grow)
        out_ref[unit] = near(scores, u_ref[unit])
        e_ref[unit] = jnp.exp(gcol) * queries - near(scores, w_ref[unit])

    agenda.around(units, at.place, FORWARD_RELAY, score_stage, pass_on)

    def read_stage(seq, head):
        unit = seq * heads + head
        value = out_ref[unit] + near(e_ref[unit], s_ref[unit])
        out_ref[unit] = value
        span = pl.ds(head * DV, DV)
        scale = lax.rsqrt(jnp.mean(value * value, axis=1, keepdims=True) + epsilon)
        gate = gate_ref[seq, PAD:, span]
        branch = value * scale * gain_ref[...] * (gate * jax.nn.sigmoid(gate))
        branch_ref[seq, :, span] = branch.astype(jnp.bfloat16)

    for seq in range(2):
        for head in range(heads):
            read_stage(seq, head)
            agenda.until(
                FORWARD_RELAY + (FORWARD_READ - FORWARD_RELAY) * (seq * heads + head + 1) / units
            )
    run_steps(agenda.take(agenda.steps.index(plans[2 * first_chunks - 1].take_across) + 1))
    part = dense(
        branch_ref[...].reshape(2 * size, vals), targets[1][...].reshape(model, vals), ((1,), (1,))
    )
    hidden_ref[...] = part
    half_sent[...] = part.astype(jnp.bfloat16)
    exchange = remote(half_sent, half_got, swap_send, swap_recv, 5, core)
    exchange.start()
    agenda.until(FORWARD_SENT)
    exchange.wait()
    for seq in range(2):
        rows = pl.ds(seq * size, size)
        value = inputs_ref[seq * padded + PAD : (seq + 1) * padded].astype(jnp.float32)
        got = half_got[(1 - seq) * size : (2 - seq) * size].astype(jnp.float32)
        value = value + hidden_ref[rows] + got
        hidden_ref[rows] = value
        scale = lax.rsqrt(jnp.mean(value * value, axis=1, keepdims=True) + epsilon)
        second_ref[rows] = (value * scale * second_gain[...]).astype(jnp.bfloat16)
    run_steps(agenda.take(agenda.steps.index(plans[3 * first_chunks - 1].take_across) + 1))
    pieces = agenda.pieces(UP_PIECES, FORWARD_UP)
    tiles = inner // 128
    for index in range(UP_PIECES):
        start, end = 128 * (tiles * index // UP_PIECES), 128 * (tiles * (index + 1) // UP_PIECES)
        halves = []
        for base in (0, inner):
            weight = targets[2][:, :, base + start : base + end].reshape(model, end - start)
            value = dense(second_ref[...], weight, ((1,), (0,)))
            gate_up_ref[:, base + start : base + end] = value
            halves.append(value)
        active_ref[:, start:end] = (
            halves[0] * jax.nn.sigmoid(halves[0]) * halves[1]
        ).astype(jnp.bfloat16)
        run_steps(pieces[index])
    agenda.until(1.0)
    line.finish()
    for copy in swaps[1:]:
        copy.wait()

    @pl.when(at.place < count - 1)
    def _():
        for copy in rims:
            copy.wait_send()


FORWARD_PROJECT, FORWARD_LOCAL, FORWARD_RELAY, FORWARD_READ = 0.04, 0.58, 0.74, 0.78
FORWARD_SENT, FORWARD_UP, UP_PIECES = 0.84, 0.96, 4
BACK_OPEN, BACK_RELAY, BACK_GRADS, BACK_BLOCKS, BACK_PART = 0.06, 0.22, 0.42, 0.5, 0.58


def forward_block(
    tokens, target, mask, norm_gain, conv, head, gain, second_gain,
    in_weight, small_part, out_weight, ffn_in, ffn_out,
):
    groups, count = lax.axis_size("dp"), lax.axis_size("seq")
    rows = in_weight.shape[0]
    inner, vals = ffn_out.shape[1] // 2, out_weight.shape[1] // 2
    widths = [conv.shape[1] + 128 + vals, vals, 2 * inner, inner]
    number = len(widths)
    shares = [third(width, 0.33) for width in widths]
    length, model = tokens.shape
    mixed_width = conv.shape[1]
    heads = mixed_width // (2 * DK + DV)
    units = 2 * heads
    padded = length + PAD

    def table(*shape):
        return jax.ShapeDtypeStruct((units,) + shape, jnp.float32)

    return pl.pallas_call(
        functools.partial(forward_kernel, groups, count, shares),
        out_shape=[
            jax.ShapeDtypeStruct((2 * padded, model), tokens.dtype),
            jax.ShapeDtypeStruct(target.shape, target.dtype),
            jax.ShapeDtypeStruct(mask.shape, mask.dtype),
            jax.ShapeDtypeStruct((2, padded, mixed_width), jnp.bfloat16),
            jax.ShapeDtypeStruct((2, padded, 128), jnp.float32),
            jax.ShapeDtypeStruct((2, padded, heads * DV), jnp.float32),
            jax.ShapeDtypeStruct((2, length, heads * DV), jnp.bfloat16),
            table(length, DV),
            table(length, length),
            table(length, DV),
            table(length, DK),
            table(DK, DK),
            table(length, DK),
            table(DK, DV),
            jax.ShapeDtypeStruct((2 * length, model), jnp.float32),
            jax.ShapeDtypeStruct((2 * length, model), jnp.bfloat16),
            jax.ShapeDtypeStruct((2 * length, 2 * inner), jnp.float32),
            jax.ShapeDtypeStruct((2 * length, inner), jnp.bfloat16),
        ]
        + [jax.ShapeDtypeStruct((count, rows, width), jnp.bfloat16) for width in widths],
        in_specs=[ROOM, ANY, ANY] + [ROOM] * 5 + [ANY] * 5,
        out_specs=[ROOM, ANY, ANY] + [ROOM] * 15 + [ROOM] * 3 + [ANY],
        scratch_shapes=[
            pltpu.VMEM((2 * padded, model), jnp.bfloat16),
            pltpu.VMEM((units, DK, DV), jnp.float32),
            pltpu.VMEM((2, length, 128), jnp.float32),
            pltpu.VMEM((2, 128, length), jnp.float32),
            *relay_scratch(units),
            pltpu.VMEM((2 * length, model), jnp.bfloat16),
            pltpu.VMEM((2 * length, model), jnp.bfloat16),
            pltpu.SemaphoreType.DMA((9,)),
            pltpu.SemaphoreType.DMA((6,)),
            pltpu.SemaphoreType.DMA((6,)),
            *[pltpu.VMEM((rows, width), jnp.bfloat16) for width in widths],
            *gather_sems(count, rows, number),
        ],
        compiler_params=pltpu.CompilerParams(
            collective_id=3, has_side_effects=True, vmem_limit_bytes=56 * 2**20
        ),
        name="forward_block",
    )(
        tokens, target, mask, norm_gain, conv, head, gain, second_gain,
        in_weight, small_part, out_weight, ffn_in, ffn_out,
    )


def backward_kernel(groups, count, *refs):
    mixed_ref, little_ref, gate_ref, conv_ref, head_ref, gain_ref = refs[:6]
    out_ref, t_ref, u_ref, w_ref, m_ref, e_ref, s_ref, branch_ref = refs[6:14]
    tokens_ref, norm_ref, hidden_ref, second_grad, loss_ref = refs[14:19]
    weight_ref, down_ref, up_ref, out_grad = refs[19:23]
    token_grad, small_sum, down_sum, gate_sum, up_sum, out_sum, in_sum, little_sum, given = refs[23:32]
    refs = refs[32:]
    do_ref, c_ref, ds_ref, lit_ref, g_ref, grow_ref = refs[:6]
    x_ref, ahead_ref, k_ref, log_ref, less_ref = refs[6:11]
    sending, arriving, relay_send, relay_recv = refs[11:15]
    grad_ref, conv_grad, gain_grad, head_grad = refs[15:19]
    normed, wide_grad, part_ref, weight = refs[19:23]
    swap, swap_got, rims, rim_got, small_got = refs[23:28]
    wide_sem, weight_sem, swap_send, swap_recv, small_send, small_recv = refs[28:34]
    scratch = refs[34:]
    units = t_ref.shape[0]
    heads = units // 2
    size = t_ref.shape[1]
    mixed_width, vals = mixed_ref.shape[2], branch_ref.shape[2]
    at = Place(groups, count)
    line = Relay(at, False, units, sending, arriving, relay_send, relay_recv)
    core = at.group % 2
    further = further_groups(at)
    pair = (at.group_swap, at.place)
    rounds, distance = [], 1
    while distance < groups:
        rounds.append((at.group + distance - 2 * distance * ((at.group // distance) % 2), at.place))
        distance *= 2
    distance = 1
    while distance < count:
        rounds.append((at.group, at.place + distance - 2 * distance * ((at.place // distance) % 2)))
        distance *= 2
    partners = at.partners() + [pair, line.before] + further + rounds + list(neighbours(at, 1))
    greet(partners, count // 2 + 5 + len(further) + len(rounds))
    keys_width, inner = heads * DK, down_ref.shape[3]
    first_width = grad_ref.shape[2]
    cut = 2 * FINAL_COLUMNS
    works = [
        Work(down_ref, 0, inner, reduce_share(inner), [(down_sum, 0, inner, inner, 0)]),
        Work(up_ref, 0, inner, reduce_share(inner), [(gate_sum, 0, inner, inner, 0)]),
        Work(out_grad, 0, vals, reduce_share(vals), [(out_sum, 0, vals, vals, 0)]),
        Work(up_ref, inner, inner, reduce_share(inner), [(up_sum, 0, inner, inner, 0)]),
        Work(
            given, 0, cut, reduce_share(cut),
            [
                (in_sum, 0, keys_width, keys_width, 0),
                (in_sum, 2 * keys_width, keys_width, keys_width, keys_width),
                (in_sum, 4 * keys_width, vals, cut - 2 * keys_width, 2 * keys_width),
            ],
        ),
        Work(
            given, cut, first_width - cut, reduce_share(first_width - cut),
            [
                (in_sum, 2 * keys_width + cut, vals, mixed_width - cut, 0),
                (little_sum, 0, 128, 128, mixed_width - cut),
                (in_sum, 4 * keys_width + 2 * vals, vals, vals, mixed_width + 128 - cut),
            ],
        ),
    ]
    plans = reduce_plans(at, works, scratch)
    chunks = len(plans) // len(works)
    agenda = Agenda(reduce_steps(plans))
    openings = [agenda.steps.index(plans[chunks * 4].begin), agenda.steps.index(plans[chunks * 5].begin)]
    run_steps(agenda.take(REDUCE_WINDOW))
    head_tables(little_ref, head_ref, g_ref, grow_ref)
    grad_ref[:, :PAD, mixed_width:] = jnp.zeros(
        (2, PAD, grad_ref.shape[2] - mixed_width), jnp.bfloat16
    )
    conv_grad[...] = jnp.zeros_like(conv_grad)
    gain_grad[...] = jnp.zeros_like(gain_grad)
    head_grad[...] = jnp.zeros_like(head_grad)
    lit_ref[...] = jnp.zeros_like(lit_ref)
    log_ref[...] = jnp.zeros_like(log_ref)

    def gate_stage(seq, head):
        unit = seq * heads + head
        span = pl.ds(head * DV, DV)
        value = out_ref[unit]
        scale = lax.rsqrt(jnp.mean(value * value, axis=1, keepdims=True) + epsilon)
        normal = value * scale
        active, slope = silu_parts(gate_ref[seq, PAD:, span])
        grad = branch_ref[seq, :, span]
        gain = gain_ref[...]
        through = grad * active
        gain_grad[0:1] += jnp.sum(through * normal, axis=0, keepdims=True)
        gate_span = pl.ds(mixed_width + 128 + head * DV, DV)
        grad_ref[seq, PAD:, gate_span] = (grad * normal * gain * slope).astype(jnp.bfloat16)
        scaled = through * gain
        grad_out = scale * (scaled - normal * jnp.mean(scaled * normal, axis=1, keepdims=True))
        do_ref[unit] = grad_out
        c_ref[unit] = near(e_ref[unit], grad_out, TN)

    for seq in range(2):
        for head in range(heads):
            gate_stage(seq, head)
    agenda.until(BACK_OPEN)

    def pass_on():
        for unit in range(units):
            line.receive(unit, ds_ref)
            line.send(unit, lambda: close(m_ref[unit], ds_ref[unit], TN) + c_ref[unit])

    def score_stage(unit):
        seq, head = unit // heads, unit % heads
        own = Unit(seq, head, heads, mixed_ref, conv_ref)
        unused, gcol, grow = head_columns(seq, head, heads, little_ref, g_ref, grow_ref)
        queries, keys = own.rows(0), own.rows(1)
        decays = decay_table(gcol, grow)
        memory, grad_out = s_ref[unit], do_ref[unit]
        update = u_ref[unit] - near(w_ref[unit], memory)
        x_ref[unit] = update.astype(jnp.bfloat16)
        scores = near(queries, keys, NT) * decays
        ahead_ref[unit] = near(scores, grad_out, TN)
        grad_scores = near(grad_out, update, NT)
        total = grad_scores * scores
        query_part = jnp.exp(gcol) * near(grad_out, memory, NT)
        grad_dot = grad_scores * decays
        own.taps_back(0, query_part + near(grad_dot, keys), grad_ref, conv_grad)
        k_ref[unit] = near(grad_dot, queries, TN)
        lane = lax.broadcasted_iota(jnp.int32, (size, 128), 1)
        log_line = jnp.sum(queries * query_part, axis=1, keepdims=True) + jnp.sum(
            total, axis=1, keepdims=True
        )
        log_ref[seq] += jnp.where(lane == head, log_line, 0.0)
        less_ref[unit] = jnp.broadcast_to(jnp.sum(total, axis=0, keepdims=True), (8, size))

    agenda.around(units, count - 1 - at.place, BACK_RELAY, score_stage, pass_on)

    def grad_stage(seq, head):
        unit = seq * heads + head
        own = Unit(seq, head, heads, mixed_ref, conv_ref)
        beta, gcol, grow = head_columns(seq, head, heads, little_ref, g_ref, grow_ref)
        keys, values = own.rows(1), own.rows(2)
        decays = decay_table(gcol, grow)
        row, col = iotas(size, size)
        strict = row > col
        memory, after = s_ref[unit], ds_ref[unit]
        growth = jnp.exp(gcol)
        last = gcol[size - 1 :, :]
        weights = jnp.exp(last - gcol)
        update = x_ref[unit]
        yield
        keys_dot = jnp.where(strict, near(keys, keys, NT) * decays, 0.0)
        grad_update = ahead_ref[unit] + near(keys * weights, after)
        yield
        grad_wanted = near(t_ref[unit], grad_update, TN)
        yield
        grad_system = -near(grad_wanted, update, NT)
        through = keys_dot * grad_system
        total = beta * through
        yield
        key_read = growth * near(grad_wanted, memory, NT)
        key_part = beta * key_read
        end_part = weights * near(update, after, NT)
        yield
        grad_keys_dot = jnp.where(strict, grad_system * decays, 0.0) * beta
        grad_k = (
            end_part - key_part + k_ref[unit]
            + near(grad_keys_dot, keys) + near(grad_keys_dot, keys, TN)
        )
        yield
        own.taps_back(1, grad_k, grad_ref, conv_grad)
        yield
        own.taps_back(2, beta * grad_wanted, grad_ref, conv_grad)
        yield
        end_line = jnp.sum(keys * end_part, axis=1, keepdims=True)
        grad_beta = (
            jnp.sum(grad_wanted * values, axis=1, keepdims=True)
            - jnp.sum(keys * key_read, axis=1, keepdims=True)
            + jnp.sum(through, axis=1, keepdims=True)
        )
        lane = lax.broadcasted_iota(jnp.int32, (size, 128), 1)
        grad_log = (
            jnp.sum(jnp.where(lane == head, log_ref[seq], 0.0), axis=1, keepdims=True)
            - jnp.sum(keys * key_part, axis=1, keepdims=True)
            - end_line
            + jnp.sum(total, axis=1, keepdims=True)
        )
        grad_last = jnp.sum(end_line) + jnp.sum(
            jnp.exp(last) * jnp.sum(memory * after, axis=1, keepdims=True)
        )
        spot = lax.broadcasted_iota(jnp.int32, (size, 1), 0)
        grad_log = grad_log + jnp.where(spot == size - 1, grad_last, 0.0)
        later = (col >= row).astype(jnp.float32)
        less = jnp.sum(total, axis=0, keepdims=True) + less_ref[unit][0:1]
        less = jnp.broadcast_to(less, (128, size))
        grad_forget = exact(later, jnp.broadcast_to(grad_log, (size, 128))) - exact(later, less, NT)
        rate, bias = head_ref[0:1], head_ref[1:2]
        little = little_ref[own.seq, PAD:, :]
        on_forget = lane == heads + own.head
        grad_soft = jnp.where(on_forget, grad_forget * rate * jax.nn.sigmoid(little + bias), 0.0)
        forget = rate * jax.nn.softplus(little + bias)
        log_total = jnp.sum(jnp.where(on_forget, grad_forget * forget, 0.0), axis=0, keepdims=True)
        head_grad[0:1] += log_total
        head_grad[1:2] += jnp.sum(grad_soft, axis=0, keepdims=True)
        lit_ref[own.seq] += grad_soft + jnp.where(
            lane == own.head, grad_beta * beta * (1.0 - beta), 0.0
        )
        yield

    agenda.loop(2, BACK_GRADS, lambda seq: lockstep([grad_stage(seq, h) for h in range(heads)]))
    grad_ref[:, PAD:, mixed_width : mixed_width + 128] = lit_ref[...].astype(jnp.bfloat16)
    line.finish()

    gain = norm_ref[...]

    def norm_rows(first, number):
        value = tokens_ref[first : first + number].astype(jnp.float32)
        scale = lax.rsqrt(jnp.mean(value * value, axis=1, keepdims=True) + epsilon)
        return scale, value * scale

    height = tokens_ref.shape[0]
    for first in range(0, height, height // 2):
        normed[first : first + height // 2] = (norm_rows(first, height // 2)[1] * gain).astype(jnp.bfloat16)
    model = tokens_ref.shape[1]
    quarter = model // 4

    def fetch(index):
        return pltpu.make_async_copy(
            weight_ref.at[pl.ds(index * quarter, quarter)], weight.at[index % 2], weight_sem.at[index % 2]
        )

    def store(start, width):
        return pltpu.make_async_copy(
            wide_grad.at[:, :, :, pl.ds(0, width)], given.at[:, :, :, pl.ds(start, width)], wide_sem
        )

    padded = height // 2
    fetch(0).start()
    fetch(1).start()
    half, unused, rows, unused = given.shape
    blocks = [
        (start, min(FINAL_COLUMNS, first_width - start))
        for start in range(0, first_width, FINAL_COLUMNS)
    ]
    for index, (start, width) in enumerate(blocks):
        if index > 0:
            store(*blocks[index - 1]).wait()
        for part in range(4):
            value = sum(
                dense(
                    normed[seq * padded : (seq + 1) * padded, part * quarter : (part + 1) * quarter],
                    grad_ref[seq, :, start : start + width],
                    ((0,), (0,)),
                )
                for seq in range(2)
            ).astype(jnp.bfloat16)
            for line in range(quarter // rows):
                place = part * (quarter // rows) + line
                wide_grad[place // 2, place % 2, :, :width] = value[line * rows : (line + 1) * rows]
        store(start, width).start()
        aim = BACK_GRADS + (BACK_BLOCKS - BACK_GRADS) * (index + 1) / len(blocks)
        run_steps(agenda.take(min(int(len(agenda.steps) * aim), openings[0])))
    store(*blocks[-1]).wait()
    for index in range(4):
        fetch(index).wait()
        for seq in range(2):
            part_ref[
                seq * padded : (seq + 1) * padded, index * quarter : (index + 1) * quarter
            ] = dense(grad_ref[seq], weight[index % 2], ((1,), (1,)))
        if index + 2 < 4:
            fetch(index + 2).start()
        agenda.until(BACK_BLOCKS + (BACK_PART - BACK_BLOCKS) * (index + 1) / 4)
    length = height // 2 - PAD
    swap[...] = part_ref[length + 2 * PAD :].astype(jnp.bfloat16)
    rims[0] = part_ref[:PAD].astype(jnp.bfloat16)
    rims[1] = part_ref[length + PAD : length + 2 * PAD].astype(jnp.bfloat16)
    own_back, swap_back = neighbours(at, -1)
    swapped = remote(swap, swap_got, swap_send, swap_recv, 0, pair)
    rim_copies = [
        remote(rims.at[0], rim_got.at[0], swap_send, swap_recv, 1, own_back),
        remote(rims.at[1], rim_got.at[1], swap_send, swap_recv, 2, swap_back),
    ]
    swapped.start()

    @pl.when(at.place > 0)
    def _():
        for copy in rim_copies:
            copy.start()

    gain_first = jnp.zeros((1, model), jnp.float32)
    for first in range(0, height, height // 2):
        unit = norm_rows(first, height // 2)[1]
        product = unit * part_ref[first : first + height // 2]
        gain_first = gain_first + jnp.sum(product, axis=0, keepdims=True)
    small_sum[...] = jnp.zeros_like(small_sum)
    for start, width, source in (
        (0, keys_width, 0),
        (2 * keys_width, keys_width, keys_width),
        (4 * keys_width, vals, 2 * keys_width),
    ):
        span = pl.ds(tile_start(start + core * width), width)
        small_sum[0:CONV, span] = conv_grad[0:CONV, source : source + width]
    small_sum[4:5, 0:model] = gain_first
    small_sum[4:5, model : 2 * model] = second_grad[...]
    small_sum[4:5, 2 * model : 2 * model + DV] = gain_grad[0:1]
    for line in range(2):
        found = head_grad[line : line + 1]
        moved = pltpu.roll(head_grad[...], 128 - heads, 1)[line : line + 1]
        small_sum[5:6, 128 * line : 128 * line + 128] = jnp.where(core == 0, moved, found)
    small_sum[5:6, 256:384] = loss_ref[...]

    def add_small(index):
        return remote(
            small_sum, small_got.at[index], small_send, small_recv, index, rounds[index]
        )

    left = agenda.pieces(len(rounds) + 1, 1.0)
    for index, found in enumerate(left):
        if index > 0:
            add_small(index - 1).wait()
            small_sum[...] += small_got[index - 1]
        if index < len(rounds):
            add_small(index).start()
        if index == 1:
            swapped.wait()

            @pl.when(at.place == count - 1)
            def _():
                rim_got[...] = jnp.zeros_like(rim_got)

            @pl.when(at.place < count - 1)
            def _():
                for copy in rim_copies:
                    copy.wait_recv()

            edge = rim_got[0].astype(jnp.float32) + rim_got[1].astype(jnp.float32)
            step = length // 4
            for first in range(0, length, step):
                scale, unit = norm_rows(PAD + first, step)
                grad = part_ref[PAD + first : PAD + first + step] + swap_got[
                    first : first + step
                ].astype(jnp.float32)
                if first + step == length:
                    grad = jnp.concatenate([grad[: step - PAD], grad[step - PAD :] + edge], axis=0)
                scaled = grad * gain
                back = scale * (scaled - unit * jnp.mean(scaled * unit, axis=1, keepdims=True))
                token_grad[first : first + step] = hidden_ref[first : first + step] + back
        run_steps(found)

    @pl.when(at.place > 0)
    def _():
        for copy in rim_copies:
            copy.wait_send()


FINAL_COLUMNS = 640


def backward_block(
    mixed_in, little, gate_pre, conv, head, gain, kept, grad_branch, inputs, norm_gain, grad_hidden,
    grad_second, loss_row, w_first, grad_down, grad_up, grad_out,
):
    groups, count = lax.axis_size("dp"), lax.axis_size("seq")
    rows, inner = grad_down.shape[2:]
    length = mixed_in.shape[1] - PAD
    units = kept[0].shape[0]
    mixed_width, vals = mixed_in.shape[2], gate_pre.shape[2]
    first_width = mixed_width + 128 + vals
    keys = (mixed_width - vals) // 2
    height, model = inputs.shape
    rounds = (groups.bit_length() - 1) + (count.bit_length() - 1)
    small = (8, 4 * keys + 2 * vals)
    kind = jnp.bfloat16

    def joined(width):
        return jax.ShapeDtypeStruct((rows, width), kind)

    return pl.pallas_call(
        functools.partial(backward_kernel, groups, count),
        out_shape=[
            jax.ShapeDtypeStruct((length, model), jnp.float32),
            jax.ShapeDtypeStruct(small, jnp.float32),
            joined(2 * inner),
            joined(2 * inner),
            joined(2 * inner),
            joined(2 * vals),
            joined(4 * keys + 4 * vals),
            joined(256),
            jax.ShapeDtypeStruct((count // 2, 2, rows, first_width), kind),
        ],
        in_specs=[ROOM] * 19 + [ANY] * 4,
        out_specs=[ROOM] * 8 + [ANY],
        scratch_shapes=[
            pltpu.VMEM((units, length, DV), jnp.float32),
            pltpu.VMEM((units, DK, DV), jnp.float32),
            pltpu.VMEM((units, DK, DV), jnp.float32),
            pltpu.VMEM((2, length, 128), jnp.float32),
            pltpu.VMEM((2, length, 128), jnp.float32),
            pltpu.VMEM((2, 128, length), jnp.float32),
            pltpu.VMEM((units, length, DV), kind),
            pltpu.VMEM((units, length, DV), jnp.float32),
            pltpu.VMEM((units, length, DK), jnp.float32),
            pltpu.VMEM((2, length, 128), jnp.float32),
            pltpu.VMEM((units, 8, length), jnp.float32),
            *relay_scratch(units),
            pltpu.VMEM((2, length + PAD, first_width), kind),
            pltpu.VMEM(conv.shape, jnp.float32),
            pltpu.VMEM((8, DV), jnp.float32),
            pltpu.VMEM((8, 128), jnp.float32),
            pltpu.VMEM((height, model), kind),
            pltpu.VMEM((count // 2, 2, rows, FINAL_COLUMNS), kind),
            pltpu.VMEM((height, model), jnp.float32),
            pltpu.VMEM((2, model // 4, first_width), kind),
            pltpu.VMEM((length, model), kind),
            pltpu.VMEM((length, model), kind),
            pltpu.VMEM((2, PAD, model), kind),
            pltpu.VMEM((2, PAD, model), kind),
            pltpu.VMEM((rounds,) + small, jnp.float32),
            pltpu.SemaphoreType.DMA,
            pltpu.SemaphoreType.DMA((2,)),
            pltpu.SemaphoreType.DMA((3,)),
            pltpu.SemaphoreType.DMA((3,)),
            pltpu.SemaphoreType.DMA((rounds,)),
            pltpu.SemaphoreType.DMA((rounds,)),
            *reduce_scratch(groups, count, rows, [inner] * 4 + [first_width // 2] * 2),
        ],
        compiler_params=pltpu.CompilerParams(
            collective_id=5, has_side_effects=True, vmem_limit_bytes=62 * 2**20
        ),
        name="backward_block",
    )(
        mixed_in, little, gate_pre, conv, head, gain, *kept, grad_branch, inputs, norm_gain,
        grad_hidden, grad_second, loss_row, w_first, grad_down, grad_up, grad_out,
    )


def third(width, weight):
    return 128 * max(1, round(width * weight / 128))


def norm_parts(field_in):
    scale = lax.rsqrt(jnp.mean(field_in * field_in, axis=-1, keepdims=True) + epsilon)
    return scale, field_in * scale


def norm_back(scale, unit, gain_vec, grad):
    scaled = grad * gain_vec
    return scale * (scaled - unit * jnp.mean(scaled * unit, axis=-1, keepdims=True))


def dense(left, right, dims):
    return lax.dot_general(left, right, (dims, ((), ())), preferred_element_type=jnp.float32)


def swiglu(gate_up):
    hidden_units = gate_up.shape[1] // 2
    return jax.nn.silu(gate_up[:, :hidden_units]) * gate_up[:, hidden_units:]


def on_device(
    tokens,
    target,
    valid,
    in_weight,
    small_weight,
    out_weight,
    ffn_in,
    ffn_out,
    gain_first,
    gain_second,
    gain_out,
    conv_weight,
    decay_log,
    decay_bias,
):
    count = lax.axis_size("seq")
    groups = lax.axis_size("dp")
    core = lax.axis_index("dp") % 2
    rows = in_weight.shape[0]
    length, model = tokens.shape[1], tokens.shape[2]
    both, padded = 2 * length, length + PAD
    heads = HEADS // 2
    keys, vals, inner = KEYS // 2, VALUES // 2, FF // 2
    mixed_width = 2 * keys + vals

    def mine(array, start, width):
        return lax.dynamic_slice_in_dim(array, start + core * width, width, array.ndim - 1)

    def qkv_half(array):
        parts = [mine(array, 0, keys), mine(array, KEYS, keys), mine(array, 2 * KEYS, vals)]
        return jnp.concatenate(parts, axis=1)

    small_half = [mine(small_weight, 0, heads), mine(small_weight, HEADS, heads)]
    spare = jnp.zeros((rows, 128 - 2 * heads), jnp.bfloat16)
    small_part = jnp.concatenate(small_half + [spare], axis=1)
    first_width = mixed_width + 128 + vals

    mask_own = valid[0].astype(jnp.float32)
    mask_rows = jnp.broadcast_to(mask_own[None, :], (8, length))
    own_conv = jnp.concatenate([qkv_half(conv_weight), jnp.zeros((8 - CONV, mixed_width))], axis=0)
    lanes = ((0, 0), (heads, 128 - 2 * heads))
    head = jnp.concatenate(
        [
            jnp.pad(-jnp.exp(mine(decay_log, 0, heads))[None], lanes),
            jnp.pad(mine(decay_bias, 0, heads)[None], lanes),
            jnp.zeros((6, 128), jnp.float32),
        ],
        axis=0,
    )
    gain_row = gain_out[None]
    (
        inputs, target_other, mask_other, mixed_in, little, gate_pre, branch, *kept,
        hidden, second, gate_up, active, w_first, w_out, w_up, w_down,
    ) = forward_block(
        tokens[0], target[0], mask_rows, gain_first[None], own_conv, head, gain_row,
        gain_second[None], in_weight, small_part, out_weight, ffn_in, ffn_out,
    )
    branch = branch.reshape(both, vals)
    w_first, w_out, w_up, w_down = (
        v.reshape(model, v.shape[2]) for v in (w_first, w_out, w_up, w_down)
    )

    def core_sum(part):
        pairs = [(group, group ^ 1) for group in range(groups)]
        got = lax.ppermute(part.astype(jnp.bfloat16), "dp", pairs)
        return part + jnp.concatenate([got[length:], got[:length]], axis=0).astype(jnp.float32)

    second_scale, second_unit = norm_parts(hidden)
    swiglu_pull = jax.vjp(swiglu, gate_up)[1]
    summed = hidden + core_sum(dense(active, w_down, ((1,), (1,))))
    mask = jnp.concatenate([mask_own, mask_other[0]])
    errors = summed - jnp.concatenate([target[0], target_other]).astype(jnp.float32)
    own_errors = errors[:length]
    loss_part = jnp.sum(mask_own * jnp.mean(own_errors * own_errors, axis=-1))

    grad_summed = mask[:, None] * errors
    grad_feed = grad_summed.astype(jnp.bfloat16)
    grad_active = dense(grad_feed, w_down, ((1,), (0,)))
    grad_down = dense(grad_feed, active, ((0,), (0,))).astype(jnp.bfloat16)
    grad_gate_up = swiglu_pull(grad_active)[0].astype(jnp.bfloat16)
    grad_up = dense(second, grad_gate_up, ((0,), (0,))).astype(jnp.bfloat16)
    grad_second = core_sum(dense(grad_gate_up, w_up, ((1,), (1,))))
    grad_gain_second = jnp.sum((grad_second * second_unit)[:length], axis=0)
    grad_hidden = grad_summed + norm_back(second_scale, second_unit, gain_second, grad_second)
    grad_attn = grad_hidden.astype(jnp.bfloat16)
    grad_out = dense(grad_attn, branch, ((0,), (0,))).astype(jnp.bfloat16)
    grad_branch = dense(grad_attn, w_out, ((1,), (0,))).reshape(2, length, vals)

    def by_place(array):
        return array.reshape(count // 2, 2, rows, array.shape[1])

    grad_up = by_place(grad_up)
    loss_row = jnp.concatenate(
        [loss_part[None], jnp.sum(mask_own)[None], jnp.zeros((126,), jnp.float32)]
    )[None]
    grad_tokens, small_sum, sum_down, sum_gate, sum_up, sum_out, sum_in, sum_small, unused = backward_block(
        mixed_in, little, gate_pre, own_conv, head, gain_row, kept, grad_branch,
        inputs, gain_first[None], grad_hidden[:length], grad_gain_second[None], loss_row, w_first,
        by_place(grad_down), grad_up, by_place(grad_out),
    )
    valid_count = jnp.maximum(small_sum[5, 257], 1.0)
    loss_value = small_sum[5, 256] / valid_count
    factor = length * groups * count / valid_count
    sum_small = jnp.concatenate(
        [
            sum_small[:, 0:heads],
            sum_small[:, 128 : 128 + heads],
            sum_small[:, heads : 2 * heads],
            sum_small[:, 128 + heads : 128 + 2 * heads],
        ],
        axis=1,
    )

    def scaled(array):
        return array.astype(jnp.float32) * factor

    return (
        summed[:length].astype(jnp.bfloat16)[None],
        loss_value,
        scaled(grad_tokens)[None],
        scaled(sum_in),
        scaled(sum_small),
        scaled(sum_out),
        scaled(jnp.concatenate([sum_gate, sum_up], axis=1)),
        scaled(sum_down),
        scaled(small_sum[4, :model]),
        scaled(small_sum[4, model : 2 * model]),
        scaled(small_sum[4, 2 * model : 2 * model + DV]),
        scaled(small_sum[:CONV]),
        scaled(small_sum[5, :HEADS]),
        scaled(small_sum[5, 128 : 128 + HEADS]),
    )


def solution(mesh):
    placed = (
        P("dp", "seq", None),
        P("dp", "seq", None),
        P("dp", "seq"),
        P("seq", None),
        P("seq", None),
        P("seq", None),
        P("seq", None),
        P("seq", None),
        P(),
        P(),
        P(),
        P(),
        P(),
        P(),
    )
    return jax.shard_map(
        on_device,
        mesh=mesh,
        in_specs=placed,
        out_specs=(
            P("dp", "seq", None),
            P(),
            P("dp", "seq", None),
            P("seq", None),
            P("seq", None),
            P("seq", None),
            P("seq", None),
            P("seq", None),
            P(),
            P(),
            P(),
            P(),
            P(),
            P(),
        ),
        check_vma=False,
    )
```

```python
import functools

import jax
import jax.numpy as jnp
from jax import lax
from jax.experimental import pallas as pl
from jax.experimental.pallas import tpu as pltpu
from jax.sharding import PartitionSpec as P

HEADS = 6
DK = 128
DV = 256
FF = 2816
CONV = 4
BLOCK = 64
KEYS = 768
VALUES = 1536


precise = lax.Precision.HIGHEST
epsilon = 1e-06


MESH = pl.DeviceIdType.MESH
NN = (((1,), (0,)), ((), ()))
NT = (((1,), (1,)), ((), ()))
TN = (((0,), (0,)), ((), ()))


def exact(left, right, dims=NN):
    return lax.dot_general(
        left, right, dims, precision=precise, preferred_element_type=jnp.float32
    )


def near(left, right, dims=NN):
    return lax.dot_general(
        left.astype(jnp.bfloat16),
        right.astype(jnp.bfloat16),
        dims,
        preferred_element_type=jnp.float32,
    )


def close(left, right, dims=NN):
    left_top, right_top = left.astype(jnp.bfloat16), right.astype(jnp.bfloat16)
    left_rest = (left - left_top.astype(jnp.float32)).astype(jnp.bfloat16)
    right_rest = (right - right_top.astype(jnp.float32)).astype(jnp.bfloat16)
    return (
        near(left_rest, right_top, dims) + near(left_top, right_rest, dims)
    ) + near(left_top, right_top, dims)


def iotas(rows, columns):
    return (
        lax.broadcasted_iota(jnp.int32, (rows, columns), 0),
        lax.broadcasted_iota(jnp.int32, (rows, columns), 1),
    )


def decay_table(gcol, grow):
    size = gcol.shape[0]
    row, col = iotas(size, size)
    keep = row >= col
    return jnp.where(keep, jnp.exp(jnp.where(keep, gcol - grow, 0.0)), 0.0)


def tile_start(start):
    return pl.multiple_of(start, 128)


class Place:
    def __init__(self, groups, count):
        self.groups, self.count, self.half = groups, count, count // 2
        self.group, self.place = lax.axis_index("dp"), lax.axis_index("seq")
        self.pair, self.side = self.place // 2, self.place % 2
        self.plane = (self.group // 2) % 2
        self.group_swap = self.group + 1 - 2 * (self.group % 2)
        self.across = self.group + 2 - 4 * self.plane
        self.beside = self.place + 1 - 2 * self.side

    def shard(self, pair, side):
        return 2 * pair + side

    def ahead(self, step):
        return lax.rem(self.pair + step, self.half)

    def behind(self, step):
        return lax.rem(self.pair + self.half - step, self.half)

    def partners(self):
        along = [(self.group, self.shard(self.ahead(step), self.side)) for step in range(1, self.half)]
        return along + [(self.group, self.beside), (self.across, self.place)]


def greet(signalled, awaited):
    barrier = pltpu.get_barrier_semaphore()
    for device in signalled:
        pl.semaphore_signal(barrier, inc=1, device_id=device, device_id_type=MESH)
    pl.semaphore_wait(barrier, awaited)


def remote(source, target, sends, receives, index, device):
    return pltpu.make_async_remote_copy(
        src_ref=source,
        dst_ref=target,
        send_sem=sends.at[index],
        recv_sem=receives.at[index],
        device_id=device,
        device_id_type=MESH,
    )


class Gather:
    def __init__(self, at, source, target, lines, share, sends, receives, local):
        self.at, self.source, self.target, self.lines = at, source, target, lines
        self.sends, self.receives, self.local = sends, receives, local
        width = source.shape[1]
        self.own = pl.ds(tile_start(at.plane * share), width - share)
        self.lent = pl.ds(tile_start(at.plane * (width - share)), share)
        self.borrowed = pl.ds(tile_start((1 - at.plane) * (width - share)), share)
        self.started = {}

    def copy(self, index, shard, columns, device, from_source=False):
        there = self.target.at[shard, self.lines, columns]
        here = self.source.at[self.lines, columns] if from_source else there
        return remote(here, there, self.sends, self.receives, index, device)

    def along(self, step):
        at = self.at
        device = (at.group, at.shard(at.ahead(step), at.side))
        return self.copy(step - 1, at.place, self.own, device, True)

    def beside(self, step):
        at = self.at
        shard = at.shard(at.behind(step), at.side)
        return self.copy(at.half - 1 + step, shard, self.own, (at.group, at.beside), step == 0)

    def across(self, step, side):
        at = self.at
        shard = at.shard(at.behind(step), at.side if side == 0 else 1 - at.side)
        return self.copy(2 * at.half - 1 + 2 * step + side - 1, shard, self.lent, (at.across, at.place))

    def keep(self):
        return pltpu.make_async_copy(
            self.source.at[self.lines], self.target.at[self.at.place, self.lines], self.local
        )

    def launch(self, make, *where):
        make(*where).start()
        self.started[make.__name__, where] = make

    def begin(self):
        self.keep().start()
        for step in range(1, self.at.half):
            self.launch(self.along, step)
        self.launch(self.beside, 0)

    def arrived(self, index, shard, columns):
        self.copy(index, shard, columns, (self.at.group, self.at.place)).wait_recv()

    def pass_along(self, step):
        at = self.at
        self.arrived(step - 1, at.shard(at.behind(step), at.side), self.own)
        self.launch(self.beside, step)
        self.launch(self.across, step, 0)

    def pass_beside(self, step):
        at = self.at
        self.arrived(at.half - 1 + step, at.shard(at.behind(step), 1 - at.side), self.own)
        self.launch(self.across, step, 1)

    def take_across(self):
        at = self.at
        for step in range(at.half):
            for side in range(2):
                if step or side:
                    shard = at.shard(at.behind(step), at.side if side == 0 else 1 - at.side)
                    self.arrived(2 * at.half - 1 + 2 * step + side - 1, shard, self.borrowed)
        self.keep().wait()

    def finish(self):
        for (unused, where), make in self.started.items():
            make(*where).wait_send()

    def stages(self):
        half = self.at.half
        first = [functools.partial(self.pass_along, step) for step in range(1, half)]
        second = [functools.partial(self.pass_beside, step) for step in range(half)]
        return [first, second, [self.take_across]]


def copies_of_gather(count):
    return 2 * count - 2


def lagged(plans, lag):
    depth = max(len(plan) for plan in plans)
    turns = []
    for turn in range(len(plans) + lag * (depth - 1)):
        steps = []
        for index, plan in enumerate(plans):
            stage, rest = divmod(turn - index, lag)
            if rest == 0 and 0 <= stage < len(plan):
                steps = plan[stage] + steps
        turns.append(steps)
    return turns


class Work:
    def __init__(self, given, base, width, share, spots):
        self.given, self.base, self.width, self.share, self.spots = given, base, width, share, spots


class Reduce:
    def __init__(self, at, work, lines, buffers, sems):
        self.at, self.given, self.spots, self.lines = at, work.given, work.spots, lines
        self.sends, self.receives, self.local = sems
        width, share = work.width, work.share
        self.wide = width - share
        wide, narrow, full = pl.ds(0, self.wide), pl.ds(0, share), pl.ds(0, width)
        self.acc = buffers[0].at[:, :, :, wide]
        self.from_across = buffers[1].at[:, :, :, narrow]
        self.from_beside, self.from_along = buffers[2].at[:, :, wide], buffers[3].at[:, :, wide]
        self.part, self.from_plane = buffers[4].at[:, wide], buffers[5].at[:, wide]
        self.total, self.other = buffers[6].at[:, full], buffers[7].at[:, full]
        self.far = buffers[8].at[:, :, full] if at.groups > 4 else None
        self.own = pl.ds(tile_start(at.plane * share), self.wide)
        self.given_own = pl.ds(tile_start(work.base + at.plane * share), self.wide)
        self.given_lent = pl.ds(tile_start(work.base + (1 - at.plane) * self.wide), share)
        self.inner = pl.ds(tile_start(at.plane * (width - 2 * share)), share)
        self.theirs = pl.ds(tile_start((1 - at.plane) * share), self.wide)

    def side(self, mine):
        return self.at.side if mine else 1 - self.at.side

    def across(self, mine):
        at = self.at
        return remote(
            self.given.at[:, self.side(mine), self.lines, self.given_lent], self.from_across.at[mine],
            self.sends, self.receives, mine, (at.across, at.place),
        )

    def load(self, mine):
        return pltpu.make_async_copy(
            self.given.at[:, self.side(mine), self.lines, self.given_own], self.acc.at[mine],
            self.local.at[mine],
        )

    def beside(self):
        at = self.at
        return remote(
            self.acc.at[0], self.from_beside, self.sends, self.receives, 2, (at.group, at.beside)
        )

    def along(self, step):
        at = self.at
        pair = at.ahead(step)
        return remote(
            self.acc.at[1, pair], self.from_along.at[step - 1],
            self.sends, self.receives, 4 + step, (at.group, at.shard(pair, at.side)),
        )

    def plane(self):
        at = self.at
        return remote(
            self.part, self.from_plane, self.sends, self.receives, 3, (at.across, at.place)
        )

    def core(self):
        at = self.at
        return remote(
            self.total, self.other, self.sends, self.receives, 4, (at.group_swap, at.place)
        )

    def further(self, index, distance):
        at = self.at
        group = at.group + distance - 2 * distance * ((at.group // distance) % 2)
        return remote(
            self.total, self.far.at[index], self.sends, self.receives,
            4 + at.half + index, (group, at.place),
        )

    def begin(self):
        for mine in range(2):
            self.load(mine).start()
            self.across(mine).start()

    def add_across(self, mine):
        self.load(mine).wait()
        self.across(mine).wait_recv()
        held = self.acc[mine, :, :, self.inner].astype(jnp.float32)
        got = self.from_across[mine].astype(jnp.float32)
        self.acc[mine, :, :, self.inner] = (held + got).astype(jnp.bfloat16)
        if not mine:
            self.beside().start()

    def add_beside(self):
        self.beside().wait_recv()
        for step in range(1, self.at.half + 1):
            pair = self.at.ahead(step)
            held = self.acc[1, pair].astype(jnp.float32)
            got = self.from_beside[pair].astype(jnp.float32)
            self.acc[1, pair] = (held + got).astype(jnp.bfloat16)
            if step < self.at.half:
                self.along(step).start()

    def add_along(self):
        value = self.acc[1, self.at.pair].astype(jnp.float32)
        for step in range(1, self.at.half):
            self.along(step).wait_recv()
            value = value + self.from_along[step - 1].astype(jnp.float32)
        self.part[...] = value.astype(jnp.bfloat16)
        self.plane().start()

    def add_plane(self):
        self.plane().wait_recv()
        self.total[...] = jnp.zeros_like(self.total)
        self.total[:, self.own] = self.part[...]
        held = self.total[:, self.theirs].astype(jnp.float32)
        got = self.from_plane[...].astype(jnp.float32)
        self.total[:, self.theirs] = (held + got).astype(jnp.bfloat16)
        distance = 4
        while distance < self.at.groups:
            index = distance.bit_length() - 3
            copy = self.further(index, distance)
            copy.start()
            copy.wait()
            got = self.far[index].astype(jnp.float32)
            self.total[...] = (self.total[...].astype(jnp.float32) + got).astype(jnp.bfloat16)
            distance *= 2
        self.core().start()

    def deliver(self):
        self.core().wait_recv()
        core = self.at.group % 2
        for target, start, stride, width, source in self.spots:
            for held, which in ((self.total, core), (self.other, 1 - core)):
                span = pl.ds(tile_start(start + which * stride), width)
                target[self.lines, span] = held[:, source : source + width]

    def finish(self):
        copies = [self.across(0), self.across(1), self.beside(), self.plane(), self.core()]
        copies += [self.along(step) for step in range(1, self.at.half)]
        for copy in copies:
            copy.wait_send()

    def stages(self):
        return [
            [functools.partial(self.add_across, 0)],
            [functools.partial(self.add_across, 1), self.add_beside],
            [self.add_along],
            [self.add_plane],
            [self.deliver],
        ]


ANY = pl.BlockSpec(memory_space=pl.ANY)
ROOM = pl.BlockSpec(memory_space=pltpu.VMEM)
PAD = 16
CHUNKS, WINDOW, GATHER_LAG = 4, 3, 2
REDUCE_CHUNKS, REDUCE_WINDOW, REDUCE_LAG, POOL = 4, 2, 1, 6


def neighbours(at, step):
    place = lax.rem(at.place + at.count + step, at.count)
    return (at.group, place), (at.group_swap, place)


def chunks_of(rows):
    return max(1, min(CHUNKS, rows // 16))


def gather_sems(count, rows, number):
    chunks = chunks_of(rows)
    return [
        pltpu.SemaphoreType.DMA((number * chunks, copies_of_gather(count))),
        pltpu.SemaphoreType.DMA((number * chunks, copies_of_gather(count))),
        pltpu.SemaphoreType.DMA((number * chunks,)),
    ]


def gather_plans(at, sources, targets, shares, sends, receives, local):
    rows = sources[0].shape[0]
    chunks = chunks_of(rows)
    lines = rows // chunks
    return [
        Gather(
            at, sources[i], targets[i], pl.ds(part * lines, lines), shares[i],
            sends.at[i * chunks + part], receives.at[i * chunks + part], local.at[i * chunks + part],
        )
        for i in range(len(sources))
        for part in range(chunks)
    ]


def gather_steps(plans):
    steps = [plan.begin for plan in plans[:WINDOW]]
    for index, turn in enumerate(lagged([plan.stages() for plan in plans], GATHER_LAG)):
        steps += turn
        if index + WINDOW < len(plans):
            steps.append(plans[index + WINDOW].begin)
    return steps + [plan.finish for plan in plans]


def reduce_steps(plans):
    steps = [plan.begin for plan in plans[:REDUCE_WINDOW]]
    for index, turn in enumerate(lagged([plan.stages() for plan in plans], REDUCE_LAG)):
        steps += turn
        later = index + REDUCE_WINDOW
        if later < len(plans):
            if later >= POOL:
                steps.append(plans[later - POOL].finish)
            steps.append(plans[later].begin)
    return steps + [plan.finish for plan in plans[-POOL:]]


def reduce_buffers(groups, count, rows, width, share):
    wide, half = width - share, count // 2
    kind = jnp.bfloat16
    far = (max(1, (groups // 4).bit_length() - 1), rows, width) if groups > 4 else (1, 16, 128)
    return [
        pltpu.VMEM((2, half, rows, wide), kind),
        pltpu.VMEM((2, half, rows, share), kind),
        pltpu.VMEM((half, rows, wide), kind),
        pltpu.VMEM((half - 1, rows, wide), kind),
        pltpu.VMEM((rows, wide), kind),
        pltpu.VMEM((rows, wide), kind),
        pltpu.VMEM((rows, width), kind),
        pltpu.VMEM((rows, width), kind),
        pltpu.VMEM(far, kind),
    ]


def copies_of_reduce(groups, count):
    return count // 2 + 4 + max(1, (groups // 4).bit_length() - 1)


def further_groups(at):
    found, distance = [], 4
    while distance < at.groups:
        found.append((at.group + distance - 2 * distance * ((at.group // distance) % 2), at.place))
        distance *= 2
    return found


def reduce_plans(at, works, scratch):
    rows = works[0].given.shape[2]
    chunks = reduce_chunks(rows)
    lines = rows // chunks
    sends, receives, local = scratch[9 * POOL : 9 * POOL + 3]
    plans = []
    for work in works:
        for part in range(chunks):
            spot = len(plans)
            slot = spot % POOL
            plans.append(
                Reduce(
                    at, work, pl.ds(part * lines, lines), scratch[9 * slot : 9 * slot + 9],
                    (sends.at[spot], receives.at[spot], local.at[spot]),
                )
            )
    return plans


def reduce_chunks(rows):
    return max(1, min(REDUCE_CHUNKS, rows // 16))


def reduce_scratch(groups, count, rows, widths):
    chunks = reduce_chunks(rows)
    width = max(widths)
    scratch = reduce_buffers(groups, count, rows // chunks, width, reduce_share(width)) * POOL
    number, copies = len(widths) * chunks, copies_of_reduce(groups, count)
    return scratch + [
        pltpu.SemaphoreType.DMA((number, copies)),
        pltpu.SemaphoreType.DMA((number, copies)),
        pltpu.SemaphoreType.DMA((number, 2)),
    ]


def reduce_share(width):
    return third(width, 0.28)


class Relay:
    def __init__(self, at, forward, units, sending, arriving, sends, receives):
        self.at, self.units = at, units
        self.sending, self.arriving, self.sends, self.receives = sending, arriving, sends, receives
        last = at.count - 1
        step = 1 if forward else -1
        self.is_first = at.place == (0 if forward else last)
        self.is_last = at.place == (last if forward else 0)
        self.beyond = (at.group, lax.rem(at.place + at.count + step, at.count))
        self.before = (at.group, lax.rem(at.place + at.count - step, at.count))

    def copy(self, unit):
        return remote(
            self.sending.at[unit], self.arriving.at[unit], self.sends, self.receives, unit, self.beyond
        )

    def receive(self, unit, target):
        @pl.when(self.is_first)
        def _():
            target[unit] = jnp.zeros(target.shape[1:], jnp.float32)

        @pl.when(jnp.logical_not(self.is_first))
        def _():
            self.copy(unit).wait_recv()
            target[unit] = self.arriving[unit].astype(jnp.float32)

    def send(self, unit, value):
        @pl.when(jnp.logical_not(self.is_last))
        def _():
            self.sending[unit] = value().astype(jnp.bfloat16)
            self.copy(unit).start()

    def finish(self):
        @pl.when(jnp.logical_not(self.is_last))
        def _():
            for unit in range(self.units):
                self.copy(unit).wait_send()


def relay_scratch(units):
    return [
        pltpu.VMEM((units, DK, DV), jnp.bfloat16),
        pltpu.VMEM((units, DK, DV), jnp.bfloat16),
        pltpu.SemaphoreType.DMA((units,)),
        pltpu.SemaphoreType.DMA((units,)),
    ]


class Agenda:
    def __init__(self, steps):
        self.steps, self.done = steps, 0

    def take(self, upto):
        upto = max(upto, self.done)
        found, self.done = self.steps[self.done : upto], upto
        return found

    def until(self, share):
        for step in self.take(int(len(self.steps) * share)):
            step()

    def pieces(self, number, share):
        found = self.take(int(len(self.steps) * share))
        cuts = [len(found) * i // number for i in range(number + 1)]
        return [found[low:high] for low, high in zip(cuts, cuts[1:])]

    def loop(self, rounds, end, stage):
        pieces = self.pieces(rounds * PAUSES, end)
        taken = []

        def body(index, carry):
            for pause, unused in enumerate(stage(index)):
                taken.append(pause)
                for other in range(rounds):
                    found = pieces[other * PAUSES + pause]
                    if found:
                        pl.when(index == other)(functools.partial(run_steps, found))
            return carry

        lax.fori_loop(0, rounds, body, 0)
        assert len(taken) == PAUSES

    def around(self, rounds, turn, end, stage, main):
        pieces = self.pieces(rounds, end)

        def body(index, carry):
            stage(index)
            for other, found in enumerate(pieces):
                if found:
                    pl.when(index == other)(functools.partial(run_steps, found))
            return carry

        split = jnp.minimum(turn, rounds)
        lax.fori_loop(0, split, body, 0)
        main()
        lax.fori_loop(split, rounds, body, 0)


def run_steps(steps):
    for step in steps:
        step()


PAUSES = 9


def lockstep(stages):
    for unused in zip(*stages):
        yield


def rolled(value, shift):
    shift = shift % value.shape[0]
    return value if shift == 0 else pltpu.roll(value, shift, 0)


def silu_parts(value):
    gate = jax.nn.sigmoid(value)
    return value * gate, gate * (1.0 + value * (1.0 - gate))


def lane_start(start):
    return start if isinstance(start, int) else tile_start(start)


class Unit:
    def __init__(self, seq, head, heads, mixed_ref, conv_ref):
        self.seq, self.head = seq, head
        self.mixed_ref, self.conv_ref = mixed_ref, conv_ref
        keys = heads * DK
        self.columns = [
            (lane_start(self.head * DK), DK),
            (lane_start(keys + self.head * DK), DK),
            (lane_start(2 * keys + self.head * DV), DV),
        ]

    def taps(self, part):
        start, width = self.columns[part]
        span = pl.ds(start, width)
        field = self.mixed_ref[self.seq, :, span].astype(jnp.float32)
        weights = self.conv_ref[:, span]
        shifts = [rolled(field, CONV - 1 - tap)[PAD:] for tap in range(CONV)]
        value = weights[0:1] * shifts[0]
        for tap in range(1, CONV):
            value = value + weights[tap : tap + 1] * shifts[tap]
        return shifts, weights, value

    def rows(self, part):
        value = self.taps(part)[2]
        active = value * jax.nn.sigmoid(value)
        if part == 2:
            return active
        unit = active * lax.rsqrt(jnp.sum(active * active, axis=1, keepdims=True) + epsilon)
        return unit * DK ** (-0.5) if part == 0 else unit

    def taps_back(self, part, grad, grad_ref, conv_grad_ref):
        shifts, weights, value = self.taps(part)
        active, slope = silu_parts(value)
        if part < 2:
            scale = lax.rsqrt(jnp.sum(active * active, axis=1, keepdims=True) + epsilon)
            unit = active * scale
            grad = grad * DK ** (-0.5) if part == 0 else grad
            grad = scale * (grad - unit * jnp.sum(grad * unit, axis=1, keepdims=True))
        grad = grad * slope
        start, width = self.columns[part]
        span = pl.ds(start, width)
        row = lax.broadcasted_iota(jnp.int32, (8, width), 0)
        taps = jnp.zeros((8, width), jnp.float32)
        longer = jnp.concatenate([jnp.zeros((PAD, width), jnp.float32), grad], axis=0)
        total = jnp.zeros(longer.shape, jnp.float32)
        for tap in range(CONV):
            taps = taps + jnp.where(row == tap, jnp.sum(grad * shifts[tap], axis=0, keepdims=True), 0.0)
            total = total + weights[tap : tap + 1] * rolled(longer, tap - (CONV - 1))
        grad_ref[self.seq, :, span] = total.astype(jnp.bfloat16)
        conv_grad_ref[:, span] += taps


def head_tables(little_ref, head_ref, g_ref, grow_ref):
    seqs, size = little_ref.shape[0], g_ref.shape[1]
    row, col = iotas(size, size)
    below = (row >= col).astype(jnp.float32)
    above = (row <= col).astype(jnp.float32)
    for seq in range(seqs):
        forget = head_ref[0:1] * jax.nn.softplus(little_ref[seq, PAD:, :] + head_ref[1:2])
        g_ref[seq] = exact(below, forget)
        grow_ref[seq] = exact(forget, above, TN)


def head_columns(seq, head, heads, little_ref, g_ref, grow_ref):
    size = g_ref.shape[1]
    lane = lax.broadcasted_iota(jnp.int32, (size, 128), 1)
    line = lax.broadcasted_iota(jnp.int32, (128, size), 0)

    def column(table, index):
        return jnp.sum(jnp.where(lane == index, table, 0.0), axis=1, keepdims=True)

    beta = column(jax.nn.sigmoid(little_ref[seq, PAD:, :]), head)
    gcol = column(g_ref[seq], heads + head)
    grow = jnp.sum(jnp.where(line == heads + head, grow_ref[seq], 0.0), axis=0, keepdims=True)
    return beta, gcol, grow


def merged(inverses, systems, width):
    size = systems[0].shape[0]
    row, col = iotas(size, size)
    joined = (row // (2 * width) == col // (2 * width)) & (row // width != col // width)
    inner = [close(jnp.where(joined, system, 0.0), inverse) for system, inverse in zip(systems, inverses)]
    return [inverse - close(inverse, value) for inverse, value in zip(inverses, inner)]


def forward_kernel(groups, count, shares, *refs):
    number = len(shares)
    tokens_ref, target_ref, mask_ref, norm_ref, conv_ref, head_ref, gain_ref, second_gain = refs[:8]
    in_weight, small_part, out_weight, ffn_in, ffn_out = refs[8:13]
    refs = refs[13:]
    inputs_ref, target_other, mask_other, mixed_ref, little_ref, gate_ref = refs[:6]
    branch_ref, out_ref, t_ref, u_ref, w_ref, m_ref, e_ref, s_ref = refs[6:14]
    hidden_ref, second_ref, gate_up_ref, active_ref = refs[14:18]
    targets, refs = refs[18 : 18 + number], refs[18 + number :]
    normed, b_ref, g_ref, grow_ref, sending, arriving, relay_send, relay_recv = refs[:8]
    half_sent, half_got, pack_sem, swap_send, swap_recv = refs[8:13]
    sources, refs = refs[13 : 13 + number], refs[13 + number :]
    sends, receives, local = refs
    units = t_ref.shape[0]
    heads = units // 2
    size = t_ref.shape[1]
    half = size // 2
    at = Place(groups, count)
    line = Relay(at, True, units, sending, arriving, relay_send, relay_recv)
    core = (at.group_swap, at.place)
    heads_width, inner = heads * DK, sources[3].shape[1]
    vals = heads * DV
    spans = [
        (0, in_weight, 0, heads_width, 0),
        (0, in_weight, 2 * heads_width, heads_width, heads_width),
        (0, in_weight, 4 * heads_width, vals, 2 * heads_width),
        (0, in_weight, 4 * heads_width + 2 * vals, vals, 2 * heads_width + vals + 128),
        (1, out_weight, 0, vals, 0),
        (2, ffn_in, 0, inner, 0),
        (2, ffn_in, 2 * inner, inner, inner),
        (3, ffn_out, 0, inner, 0),
    ]
    packs = [[], [], [], []]
    for index, (matrix, weight, start, width, place) in enumerate(spans):
        span = pl.ds(tile_start(start + (at.group % 2) * width), width)
        packs[matrix].append(
            pltpu.make_async_copy(
                weight.at[:, span], sources[matrix].at[:, pl.ds(place, width)], pack_sem.at[index]
            )
        )
    packs[0].append(
        pltpu.make_async_copy(
            small_part, sources[0].at[:, pl.ds(2 * heads_width + vals, 128)], pack_sem.at[len(spans)]
        )
    )
    for pack in packs:
        for copy in pack:
            copy.start()
    greet(at.partners() + [line.before, core] + list(neighbours(at, -1)), count // 2 + 5)
    padded = size + PAD
    swaps = [
        remote(here, there, swap_send, swap_recv, index, core)
        for index, (here, there) in enumerate((
            (tokens_ref, inputs_ref.at[pl.ds(padded + PAD, size)]),
            (target_ref, target_other),
            (mask_ref, mask_other),
        ))
    ]
    tail = tokens_ref.at[pl.ds(size - PAD, PAD)]
    own_next, swap_next = neighbours(at, 1)
    rims = [
        remote(tail, inputs_ref.at[pl.ds(0, PAD)], swap_send, swap_recv, 3, own_next),
        remote(tail, inputs_ref.at[pl.ds(padded, PAD)], swap_send, swap_recv, 4, swap_next),
    ]
    swaps[0].start()

    @pl.when(at.place < count - 1)
    def _():
        for copy in rims:
            copy.start()

    plans = gather_plans(at, sources, targets, shares, sends, receives, local)
    agenda = Agenda(gather_steps(plans))
    for pack in packs:
        for copy in pack:
            copy.wait()
    run_steps(agenda.take(WINDOW))
    for copy in swaps[1:]:
        copy.start()
    inputs_ref[PAD:padded] = tokens_ref[...]

    @pl.when(at.place == 0)
    def _():
        inputs_ref[:PAD] = jnp.zeros((PAD, inputs_ref.shape[1]), jnp.bfloat16)
        inputs_ref[padded : padded + PAD] = jnp.zeros((PAD, inputs_ref.shape[1]), jnp.bfloat16)

    @pl.when(at.place > 0)
    def _():
        for copy in rims:
            copy.wait_recv()

    swaps[0].wait()
    for seq in range(2):
        value = inputs_ref[seq * padded : (seq + 1) * padded].astype(jnp.float32)
        scale = lax.rsqrt(jnp.mean(value * value, axis=1, keepdims=True) + epsilon)
        normed[seq * padded : (seq + 1) * padded] = (value * scale * norm_ref[...]).astype(jnp.bfloat16)
    first_chunks = len(plans) // number
    run_steps(agenda.take(agenda.steps.index(plans[first_chunks - 1].take_across) + 1))

    weight = targets[0]
    model = normed.shape[1]
    mixed_width = mixed_ref.shape[2]
    cuts = [0, mixed_width // 2, mixed_width, mixed_width + 128, weight.shape[2]]
    for start, end in zip(cuts, cuts[1:]):
        value = dense(normed[...], weight[:, :, start:end].reshape(model, end - start), ((1,), (0,)))
        value = value.reshape(2, padded, end - start)
        if end <= mixed_width:
            mixed_ref[:, :, start:end] = value.astype(jnp.bfloat16)
        elif end == mixed_width + 128:
            little_ref[...] = value
        else:
            gate_ref[...] = value
        agenda.until(agenda.done / len(agenda.steps) + FORWARD_PROJECT / 4)
    head_tables(little_ref, head_ref, g_ref, grow_ref)

    def local_stage(seq, head):
        unit = seq * heads + head
        own = Unit(seq, head, heads, mixed_ref, conv_ref)
        beta, gcol, grow = head_columns(seq, head, heads, little_ref, g_ref, grow_ref)
        decays = decay_table(gcol, grow)
        keys = own.rows(1)
        row, col = iotas(size, size)
        system = jnp.where(row > col, beta * close(keys, keys, NT) * decays, 0.0)
        yield
        systems = [system[:half, :half], system[half:, half:]]
        row, col = iotas(half, half)
        inverses = [
            (row == col).astype(jnp.float32) - jnp.where(row // 2 == col // 2, value, 0.0)
            for value in systems
        ]
        width = 2
        while width < half:
            inverses = merged(inverses, systems, width)
            width *= 2
            yield
        corner = -close(inverses[1], close(system[half:, :half], inverses[0]))
        t_ref[unit, :half, :half] = inverses[0]
        t_ref[unit, :half, half:] = jnp.zeros((half, half), jnp.float32)
        t_ref[unit, half:, :half] = corner
        t_ref[unit, half:, half:] = inverses[1]
        solve = t_ref[unit]
        growth = jnp.exp(gcol)
        last = gcol[size - 1 :, :]
        update = near(solve, beta * own.rows(2))
        back = near(solve, (beta * growth) * keys)
        u_ref[unit] = update
        w_ref[unit] = back
        yield
        weighted = keys * jnp.exp(last - gcol)
        drow, dcol = iotas(DK, DK)
        m_ref[unit] = jnp.where(drow == dcol, jnp.exp(last), 0.0) - near(weighted, back, TN)
        b_ref[unit] = near(weighted, update, TN)
        yield

    agenda.loop(2, FORWARD_LOCAL, lambda seq: lockstep([local_stage(seq, h) for h in range(heads)]))

    def pass_on():
        for unit in range(units):
            line.receive(unit, s_ref)
            line.send(unit, lambda: close(m_ref[unit], s_ref[unit]) + b_ref[unit])

    def score_stage(unit):
        seq, head = unit // heads, unit % heads
        own = Unit(seq, head, heads, mixed_ref, conv_ref)
        unused, gcol, grow = head_columns(seq, head, heads, little_ref, g_ref, grow_ref)
        queries = own.rows(0)
        scores = near(queries, own.rows(1), NT) * decay_table(gcol, grow)
        out_ref[unit] = near(scores, u_ref[unit])
        e_ref[unit] = jnp.exp(gcol) * queries - near(scores, w_ref[unit])

    agenda.around(units, at.place, FORWARD_RELAY, score_stage, pass_on)

    def read_stage(seq, head):
        unit = seq * heads + head
        value = out_ref[unit] + near(e_ref[unit], s_ref[unit])
        out_ref[unit] = value
        span = pl.ds(head * DV, DV)
        scale = lax.rsqrt(jnp.mean(value * value, axis=1, keepdims=True) + epsilon)
        gate = gate_ref[seq, PAD:, span]
        branch = value * scale * gain_ref[...] * (gate * jax.nn.sigmoid(gate))
        branch_ref[seq, :, span] = branch.astype(jnp.bfloat16)

    for seq in range(2):
        for head in range(heads):
            read_stage(seq, head)
            agenda.until(
                FORWARD_RELAY + (FORWARD_READ - FORWARD_RELAY) * (seq * heads + head + 1) / units
            )
    run_steps(agenda.take(agenda.steps.index(plans[2 * first_chunks - 1].take_across) + 1))
    part = dense(
        branch_ref[...].reshape(2 * size, vals), targets[1][...].reshape(model, vals), ((1,), (1,))
    )
    hidden_ref[...] = part
    half_sent[...] = part.astype(jnp.bfloat16)
    exchange = remote(half_sent, half_got, swap_send, swap_recv, 5, core)
    exchange.start()
    agenda.until(FORWARD_SENT)
    exchange.wait()
    for seq in range(2):
        rows = pl.ds(seq * size, size)
        value = inputs_ref[seq * padded + PAD : (seq + 1) * padded].astype(jnp.float32)
        got = half_got[(1 - seq) * size : (2 - seq) * size].astype(jnp.float32)
        value = value + hidden_ref[rows] + got
        hidden_ref[rows] = value
        scale = lax.rsqrt(jnp.mean(value * value, axis=1, keepdims=True) + epsilon)
        second_ref[rows] = (value * scale * second_gain[...]).astype(jnp.bfloat16)
    run_steps(agenda.take(agenda.steps.index(plans[3 * first_chunks - 1].take_across) + 1))
    pieces = agenda.pieces(UP_PIECES, FORWARD_UP)
    tiles = inner // 128
    for index in range(UP_PIECES):
        start, end = 128 * (tiles * index // UP_PIECES), 128 * (tiles * (index + 1) // UP_PIECES)
        halves = []
        for base in (0, inner):
            weight = targets[2][:, :, base + start : base + end].reshape(model, end - start)
            value = dense(second_ref[...], weight, ((1,), (0,)))
            gate_up_ref[:, base + start : base + end] = value
            halves.append(value)
        active_ref[:, start:end] = (
            halves[0] * jax.nn.sigmoid(halves[0]) * halves[1]
        ).astype(jnp.bfloat16)
        run_steps(pieces[index])
    agenda.until(1.0)
    line.finish()
    for copy in swaps[1:]:
        copy.wait()

    @pl.when(at.place < count - 1)
    def _():
        for copy in rims:
            copy.wait_send()


FORWARD_PROJECT, FORWARD_LOCAL, FORWARD_RELAY, FORWARD_READ = 0.04, 0.58, 0.74, 0.78
FORWARD_SENT, FORWARD_UP, UP_PIECES = 0.84, 0.96, 4
BACK_OPEN, BACK_RELAY, BACK_GRADS, BACK_BLOCKS, BACK_PART = 0.06, 0.22, 0.42, 0.5, 0.58


def forward_block(
    tokens, target, mask, norm_gain, conv, head, gain, second_gain,
    in_weight, small_part, out_weight, ffn_in, ffn_out,
):
    groups, count = lax.axis_size("dp"), lax.axis_size("seq")
    rows = in_weight.shape[0]
    inner, vals = ffn_out.shape[1] // 2, out_weight.shape[1] // 2
    widths = [conv.shape[1] + 128 + vals, vals, 2 * inner, inner]
    number = len(widths)
    shares = [third(width, 0.365) for width in widths]
    length, model = tokens.shape
    mixed_width = conv.shape[1]
    heads = mixed_width // (2 * DK + DV)
    units = 2 * heads
    padded = length + PAD

    def table(*shape):
        return jax.ShapeDtypeStruct((units,) + shape, jnp.float32)

    return pl.pallas_call(
        functools.partial(forward_kernel, groups, count, shares),
        out_shape=[
            jax.ShapeDtypeStruct((2 * padded, model), tokens.dtype),
            jax.ShapeDtypeStruct(target.shape, target.dtype),
            jax.ShapeDtypeStruct(mask.shape, mask.dtype),
            jax.ShapeDtypeStruct((2, padded, mixed_width), jnp.bfloat16),
            jax.ShapeDtypeStruct((2, padded, 128), jnp.float32),
            jax.ShapeDtypeStruct((2, padded, heads * DV), jnp.float32),
            jax.ShapeDtypeStruct((2, length, heads * DV), jnp.bfloat16),
            table(length, DV),
            table(length, length),
            table(length, DV),
            table(length, DK),
            table(DK, DK),
            table(length, DK),
            table(DK, DV),
            jax.ShapeDtypeStruct((2 * length, model), jnp.float32),
            jax.ShapeDtypeStruct((2 * length, model), jnp.bfloat16),
            jax.ShapeDtypeStruct((2 * length, 2 * inner), jnp.float32),
            jax.ShapeDtypeStruct((2 * length, inner), jnp.bfloat16),
        ]
        + [jax.ShapeDtypeStruct((count, rows, width), jnp.bfloat16) for width in widths],
        in_specs=[ROOM, ANY, ANY] + [ROOM] * 5 + [ANY] * 5,
        out_specs=[ROOM, ANY, ANY] + [ROOM] * 15 + [ROOM] * 3 + [ANY],
        scratch_shapes=[
            pltpu.VMEM((2 * padded, model), jnp.bfloat16),
            pltpu.VMEM((units, DK, DV), jnp.float32),
            pltpu.VMEM((2, length, 128), jnp.float32),
            pltpu.VMEM((2, 128, length), jnp.float32),
            *relay_scratch(units),
            pltpu.VMEM((2 * length, model), jnp.bfloat16),
            pltpu.VMEM((2 * length, model), jnp.bfloat16),
            pltpu.SemaphoreType.DMA((9,)),
            pltpu.SemaphoreType.DMA((6,)),
            pltpu.SemaphoreType.DMA((6,)),
            *[pltpu.VMEM((rows, width), jnp.bfloat16) for width in widths],
            *gather_sems(count, rows, number),
        ],
        compiler_params=pltpu.CompilerParams(
            collective_id=3, has_side_effects=True, vmem_limit_bytes=56 * 2**20
        ),
        name="forward_block",
    )(
        tokens, target, mask, norm_gain, conv, head, gain, second_gain,
        in_weight, small_part, out_weight, ffn_in, ffn_out,
    )


def backward_kernel(groups, count, *refs):
    mixed_ref, little_ref, gate_ref, conv_ref, head_ref, gain_ref = refs[:6]
    out_ref, t_ref, u_ref, w_ref, m_ref, e_ref, s_ref, branch_ref = refs[6:14]
    tokens_ref, norm_ref, hidden_ref, second_grad, loss_ref = refs[14:19]
    weight_ref, down_ref, up_ref, out_grad = refs[19:23]
    token_grad, small_sum, down_sum, gate_sum, up_sum, out_sum, in_sum, little_sum, given = refs[23:32]
    refs = refs[32:]
    do_ref, c_ref, ds_ref, lit_ref, g_ref, grow_ref = refs[:6]
    x_ref, ahead_ref, k_ref, log_ref, less_ref = refs[6:11]
    sending, arriving, relay_send, relay_recv = refs[11:15]
    grad_ref, conv_grad, gain_grad, head_grad = refs[15:19]
    normed, wide_grad, part_ref, weight = refs[19:23]
    swap, swap_got, rims, rim_got, small_got = refs[23:28]
    wide_sem, weight_sem, swap_send, swap_recv, small_send, small_recv = refs[28:34]
    scratch = refs[34:]
    units = t_ref.shape[0]
    heads = units // 2
    size = t_ref.shape[1]
    mixed_width, vals = mixed_ref.shape[2], branch_ref.shape[2]
    at = Place(groups, count)
    line = Relay(at, False, units, sending, arriving, relay_send, relay_recv)
    core = at.group % 2
    further = further_groups(at)
    pair = (at.group_swap, at.place)
    rounds, distance = [], 1
    while distance < groups:
        rounds.append((at.group + distance - 2 * distance * ((at.group // distance) % 2), at.place))
        distance *= 2
    distance = 1
    while distance < count:
        rounds.append((at.group, at.place + distance - 2 * distance * ((at.place // distance) % 2)))
        distance *= 2
    partners = at.partners() + [pair, line.before] + further + rounds + list(neighbours(at, 1))
    greet(partners, count // 2 + 5 + len(further) + len(rounds))
    keys_width, inner = heads * DK, down_ref.shape[3]
    first_width = grad_ref.shape[2]
    cut = 2 * FINAL_COLUMNS
    works = [
        Work(out_grad, 0, vals, reduce_share(vals), [(out_sum, 0, vals, vals, 0)]),
        Work(down_ref, 0, inner, reduce_share(inner), [(down_sum, 0, inner, inner, 0)]),
        Work(up_ref, 0, inner, reduce_share(inner), [(gate_sum, 0, inner, inner, 0)]),
        Work(up_ref, inner, inner, reduce_share(inner), [(up_sum, 0, inner, inner, 0)]),
        Work(
            given, 0, cut, reduce_share(cut),
            [
                (in_sum, 0, keys_width, keys_width, 0),
                (in_sum, 2 * keys_width, keys_width, keys_width, keys_width),
                (in_sum, 4 * keys_width, vals, cut - 2 * keys_width, 2 * keys_width),
            ],
        ),
        Work(
            given, cut, first_width - cut, reduce_share(first_width - cut),
            [
                (in_sum, 2 * keys_width + cut, vals, mixed_width - cut, 0),
                (little_sum, 0, 128, 128, mixed_width - cut),
                (in_sum, 4 * keys_width + 2 * vals, vals, vals, mixed_width + 128 - cut),
            ],
        ),
    ]
    plans = reduce_plans(at, works, scratch)
    chunks = len(plans) // len(works)
    agenda = Agenda(reduce_steps(plans))
    openings = [agenda.steps.index(plans[chunks * 4].begin), agenda.steps.index(plans[chunks * 5].begin)]
    run_steps(agenda.take(REDUCE_WINDOW))
    head_tables(little_ref, head_ref, g_ref, grow_ref)
    grad_ref[:, :PAD, mixed_width:] = jnp.zeros(
        (2, PAD, grad_ref.shape[2] - mixed_width), jnp.bfloat16
    )
    conv_grad[...] = jnp.zeros_like(conv_grad)
    gain_grad[...] = jnp.zeros_like(gain_grad)
    head_grad[...] = jnp.zeros_like(head_grad)
    lit_ref[...] = jnp.zeros_like(lit_ref)
    log_ref[...] = jnp.zeros_like(log_ref)

    def gate_stage(seq, head):
        unit = seq * heads + head
        span = pl.ds(head * DV, DV)
        value = out_ref[unit]
        scale = lax.rsqrt(jnp.mean(value * value, axis=1, keepdims=True) + epsilon)
        normal = value * scale
        active, slope = silu_parts(gate_ref[seq, PAD:, span])
        grad = branch_ref[seq, :, span]
        gain = gain_ref[...]
        through = grad * active
        gain_grad[0:1] += jnp.sum(through * normal, axis=0, keepdims=True)
        gate_span = pl.ds(mixed_width + 128 + head * DV, DV)
        grad_ref[seq, PAD:, gate_span] = (grad * normal * gain * slope).astype(jnp.bfloat16)
        scaled = through * gain
        grad_out = scale * (scaled - normal * jnp.mean(scaled * normal, axis=1, keepdims=True))
        do_ref[unit] = grad_out
        c_ref[unit] = near(e_ref[unit], grad_out, TN)

    for seq in range(2):
        for head in range(heads):
            gate_stage(seq, head)
    agenda.until(BACK_OPEN)

    def pass_on():
        for unit in range(units):
            line.receive(unit, ds_ref)
            line.send(unit, lambda: close(m_ref[unit], ds_ref[unit], TN) + c_ref[unit])

    def score_stage(unit):
        seq, head = unit // heads, unit % heads
        own = Unit(seq, head, heads, mixed_ref, conv_ref)
        unused, gcol, grow = head_columns(seq, head, heads, little_ref, g_ref, grow_ref)
        queries, keys = own.rows(0), own.rows(1)
        decays = decay_table(gcol, grow)
        memory, grad_out = s_ref[unit], do_ref[unit]
        update = u_ref[unit] - near(w_ref[unit], memory)
        x_ref[unit] = update.astype(jnp.bfloat16)
        scores = near(queries, keys, NT) * decays
        ahead_ref[unit] = near(scores, grad_out, TN)
        grad_scores = near(grad_out, update, NT)
        total = grad_scores * scores
        query_part = jnp.exp(gcol) * near(grad_out, memory, NT)
        grad_dot = grad_scores * decays
        own.taps_back(0, query_part + near(grad_dot, keys), grad_ref, conv_grad)
        k_ref[unit] = near(grad_dot, queries, TN)
        lane = lax.broadcasted_iota(jnp.int32, (size, 128), 1)
        log_line = jnp.sum(queries * query_part, axis=1, keepdims=True) + jnp.sum(
            total, axis=1, keepdims=True
        )
        log_ref[seq] += jnp.where(lane == head, log_line, 0.0)
        less_ref[unit] = jnp.broadcast_to(jnp.sum(total, axis=0, keepdims=True), (8, size))

    agenda.around(units, count - 1 - at.place, BACK_RELAY, score_stage, pass_on)

    def grad_stage(seq, head):
        unit = seq * heads + head
        own = Unit(seq, head, heads, mixed_ref, conv_ref)
        beta, gcol, grow = head_columns(seq, head, heads, little_ref, g_ref, grow_ref)
        keys, values = own.rows(1), own.rows(2)
        decays = decay_table(gcol, grow)
        row, col = iotas(size, size)
        strict = row > col
        memory, after = s_ref[unit], ds_ref[unit]
        growth = jnp.exp(gcol)
        last = gcol[size - 1 :, :]
        weights = jnp.exp(last - gcol)
        update = x_ref[unit]
        yield
        keys_dot = jnp.where(strict, near(keys, keys, NT) * decays, 0.0)
        grad_update = ahead_ref[unit] + near(keys * weights, after)
        yield
        grad_wanted = near(t_ref[unit], grad_update, TN)
        yield
        grad_system = -near(grad_wanted, update, NT)
        through = keys_dot * grad_system
        total = beta * through
        yield
        key_read = growth * near(grad_wanted, memory, NT)
        key_part = beta * key_read
        end_part = weights * near(update, after, NT)
        yield
        grad_keys_dot = jnp.where(strict, grad_system * decays, 0.0) * beta
        grad_k = (
            end_part - key_part + k_ref[unit]
            + near(grad_keys_dot, keys) + near(grad_keys_dot, keys, TN)
        )
        yield
        own.taps_back(1, grad_k, grad_ref, conv_grad)
        yield
        own.taps_back(2, beta * grad_wanted, grad_ref, conv_grad)
        yield
        end_line = jnp.sum(keys * end_part, axis=1, keepdims=True)
        grad_beta = (
            jnp.sum(grad_wanted * values, axis=1, keepdims=True)
            - jnp.sum(keys * key_read, axis=1, keepdims=True)
            + jnp.sum(through, axis=1, keepdims=True)
        )
        lane = lax.broadcasted_iota(jnp.int32, (size, 128), 1)
        grad_log = (
            jnp.sum(jnp.where(lane == head, log_ref[seq], 0.0), axis=1, keepdims=True)
            - jnp.sum(keys * key_part, axis=1, keepdims=True)
            - end_line
            + jnp.sum(total, axis=1, keepdims=True)
        )
        grad_last = jnp.sum(end_line) + jnp.sum(
            jnp.exp(last) * jnp.sum(memory * after, axis=1, keepdims=True)
        )
        spot = lax.broadcasted_iota(jnp.int32, (size, 1), 0)
        grad_log = grad_log + jnp.where(spot == size - 1, grad_last, 0.0)
        later = (col >= row).astype(jnp.float32)
        less = jnp.sum(total, axis=0, keepdims=True) + less_ref[unit][0:1]
        less = jnp.broadcast_to(less, (128, size))
        grad_forget = exact(later, jnp.broadcast_to(grad_log, (size, 128))) - exact(later, less, NT)
        rate, bias = head_ref[0:1], head_ref[1:2]
        little = little_ref[own.seq, PAD:, :]
        on_forget = lane == heads + own.head
        grad_soft = jnp.where(on_forget, grad_forget * rate * jax.nn.sigmoid(little + bias), 0.0)
        forget = rate * jax.nn.softplus(little + bias)
        log_total = jnp.sum(jnp.where(on_forget, grad_forget * forget, 0.0), axis=0, keepdims=True)
        head_grad[0:1] += log_total
        head_grad[1:2] += jnp.sum(grad_soft, axis=0, keepdims=True)
        lit_ref[own.seq] += grad_soft + jnp.where(
            lane == own.head, grad_beta * beta * (1.0 - beta), 0.0
        )
        yield

    agenda.loop(2, BACK_GRADS, lambda seq: lockstep([grad_stage(seq, h) for h in range(heads)]))
    grad_ref[:, PAD:, mixed_width : mixed_width + 128] = lit_ref[...].astype(jnp.bfloat16)
    line.finish()

    gain = norm_ref[...]

    def norm_rows(first, number):
        value = tokens_ref[first : first + number].astype(jnp.float32)
        scale = lax.rsqrt(jnp.mean(value * value, axis=1, keepdims=True) + epsilon)
        return scale, value * scale

    height = tokens_ref.shape[0]
    for first in range(0, height, height // 2):
        normed[first : first + height // 2] = (norm_rows(first, height // 2)[1] * gain).astype(jnp.bfloat16)
    model = tokens_ref.shape[1]
    quarter = model // 4

    def fetch(index):
        return pltpu.make_async_copy(
            weight_ref.at[pl.ds(index * quarter, quarter)], weight.at[index % 2], weight_sem.at[index % 2]
        )

    def store(start, width):
        return pltpu.make_async_copy(
            wide_grad.at[:, :, :, pl.ds(0, width)], given.at[:, :, :, pl.ds(start, width)], wide_sem
        )

    padded = height // 2
    fetch(0).start()
    fetch(1).start()
    half, unused, rows, unused = given.shape
    blocks = [
        (start, min(FINAL_COLUMNS, first_width - start))
        for start in range(0, first_width, FINAL_COLUMNS)
    ]
    for index, (start, width) in enumerate(blocks):
        if index > 0:
            store(*blocks[index - 1]).wait()
        for part in range(4):
            value = sum(
                dense(
                    normed[seq * padded : (seq + 1) * padded, part * quarter : (part + 1) * quarter],
                    grad_ref[seq, :, start : start + width],
                    ((0,), (0,)),
                )
                for seq in range(2)
            ).astype(jnp.bfloat16)
            for line in range(quarter // rows):
                place = part * (quarter // rows) + line
                wide_grad[place // 2, place % 2, :, :width] = value[line * rows : (line + 1) * rows]
        store(start, width).start()
        aim = BACK_GRADS + (BACK_BLOCKS - BACK_GRADS) * (index + 1) / len(blocks)
        run_steps(agenda.take(min(int(len(agenda.steps) * aim), openings[0])))
    store(*blocks[-1]).wait()
    for index in range(4):
        fetch(index).wait()
        for seq in range(2):
            part_ref[
                seq * padded : (seq + 1) * padded, index * quarter : (index + 1) * quarter
            ] = dense(grad_ref[seq], weight[index % 2], ((1,), (1,)))
        if index + 2 < 4:
            fetch(index + 2).start()
        agenda.until(BACK_BLOCKS + (BACK_PART - BACK_BLOCKS) * (index + 1) / 4)
    length = height // 2 - PAD
    swap[...] = part_ref[length + 2 * PAD :].astype(jnp.bfloat16)
    rims[0] = part_ref[:PAD].astype(jnp.bfloat16)
    rims[1] = part_ref[length + PAD : length + 2 * PAD].astype(jnp.bfloat16)
    own_back, swap_back = neighbours(at, -1)
    swapped = remote(swap, swap_got, swap_send, swap_recv, 0, pair)
    rim_copies = [
        remote(rims.at[0], rim_got.at[0], swap_send, swap_recv, 1, own_back),
        remote(rims.at[1], rim_got.at[1], swap_send, swap_recv, 2, swap_back),
    ]
    swapped.start()

    @pl.when(at.place > 0)
    def _():
        for copy in rim_copies:
            copy.start()

    gain_first = jnp.zeros((1, model), jnp.float32)
    for first in range(0, height, height // 2):
        unit = norm_rows(first, height // 2)[1]
        product = unit * part_ref[first : first + height // 2]
        gain_first = gain_first + jnp.sum(product, axis=0, keepdims=True)
    small_sum[...] = jnp.zeros_like(small_sum)
    for start, width, source in (
        (0, keys_width, 0),
        (2 * keys_width, keys_width, keys_width),
        (4 * keys_width, vals, 2 * keys_width),
    ):
        span = pl.ds(tile_start(start + core * width), width)
        small_sum[0:CONV, span] = conv_grad[0:CONV, source : source + width]
    small_sum[4:5, 0:model] = gain_first
    small_sum[4:5, model : 2 * model] = second_grad[...]
    small_sum[4:5, 2 * model : 2 * model + DV] = gain_grad[0:1]
    for line in range(2):
        found = head_grad[line : line + 1]
        moved = pltpu.roll(head_grad[...], 128 - heads, 1)[line : line + 1]
        small_sum[5:6, 128 * line : 128 * line + 128] = jnp.where(core == 0, moved, found)
    small_sum[5:6, 256:384] = loss_ref[...]

    def add_small(index):
        return remote(
            small_sum, small_got.at[index], small_send, small_recv, index, rounds[index]
        )

    left = agenda.pieces(len(rounds) + 1, 1.0)
    for index, found in enumerate(left):
        if index > 0:
            add_small(index - 1).wait()
            small_sum[...] += small_got[index - 1]
        if index < len(rounds):
            add_small(index).start()
        if index == 1:
            swapped.wait()

            @pl.when(at.place == count - 1)
            def _():
                rim_got[...] = jnp.zeros_like(rim_got)

            @pl.when(at.place < count - 1)
            def _():
                for copy in rim_copies:
                    copy.wait_recv()

            edge = rim_got[0].astype(jnp.float32) + rim_got[1].astype(jnp.float32)
            step = length // 4
            for first in range(0, length, step):
                scale, unit = norm_rows(PAD + first, step)
                grad = part_ref[PAD + first : PAD + first + step] + swap_got[
                    first : first + step
                ].astype(jnp.float32)
                if first + step == length:
                    grad = jnp.concatenate([grad[: step - PAD], grad[step - PAD :] + edge], axis=0)
                scaled = grad * gain
                back = scale * (scaled - unit * jnp.mean(scaled * unit, axis=1, keepdims=True))
                token_grad[first : first + step] = hidden_ref[first : first + step] + back
        run_steps(found)

    @pl.when(at.place > 0)
    def _():
        for copy in rim_copies:
            copy.wait_send()


FINAL_COLUMNS = 640


def backward_block(
    mixed_in, little, gate_pre, conv, head, gain, kept, grad_branch, inputs, norm_gain, grad_hidden,
    grad_second, loss_row, w_first, grad_down, grad_up, grad_out,
):
    groups, count = lax.axis_size("dp"), lax.axis_size("seq")
    rows, inner = grad_down.shape[2:]
    length = mixed_in.shape[1] - PAD
    units = kept[0].shape[0]
    mixed_width, vals = mixed_in.shape[2], gate_pre.shape[2]
    first_width = mixed_width + 128 + vals
    keys = (mixed_width - vals) // 2
    height, model = inputs.shape
    rounds = (groups.bit_length() - 1) + (count.bit_length() - 1)
    small = (8, 4 * keys + 2 * vals)
    kind = jnp.bfloat16

    def joined(width):
        return jax.ShapeDtypeStruct((rows, width), kind)

    return pl.pallas_call(
        functools.partial(backward_kernel, groups, count),
        out_shape=[
            jax.ShapeDtypeStruct((length, model), jnp.float32),
            jax.ShapeDtypeStruct(small, jnp.float32),
            joined(2 * inner),
            joined(2 * inner),
            joined(2 * inner),
            joined(2 * vals),
            joined(4 * keys + 4 * vals),
            joined(256),
            jax.ShapeDtypeStruct((count // 2, 2, rows, first_width), kind),
        ],
        in_specs=[ROOM] * 19 + [ANY] * 4,
        out_specs=[ROOM] * 8 + [ANY],
        scratch_shapes=[
            pltpu.VMEM((units, length, DV), jnp.float32),
            pltpu.VMEM((units, DK, DV), jnp.float32),
            pltpu.VMEM((units, DK, DV), jnp.float32),
            pltpu.VMEM((2, length, 128), jnp.float32),
            pltpu.VMEM((2, length, 128), jnp.float32),
            pltpu.VMEM((2, 128, length), jnp.float32),
            pltpu.VMEM((units, length, DV), kind),
            pltpu.VMEM((units, length, DV), jnp.float32),
            pltpu.VMEM((units, length, DK), jnp.float32),
            pltpu.VMEM((2, length, 128), jnp.float32),
            pltpu.VMEM((units, 8, length), jnp.float32),
            *relay_scratch(units),
            pltpu.VMEM((2, length + PAD, first_width), kind),
            pltpu.VMEM(conv.shape, jnp.float32),
            pltpu.VMEM((8, DV), jnp.float32),
            pltpu.VMEM((8, 128), jnp.float32),
            pltpu.VMEM((height, model), kind),
            pltpu.VMEM((count // 2, 2, rows, FINAL_COLUMNS), kind),
            pltpu.VMEM((height, model), jnp.float32),
            pltpu.VMEM((2, model // 4, first_width), kind),
            pltpu.VMEM((length, model), kind),
            pltpu.VMEM((length, model), kind),
            pltpu.VMEM((2, PAD, model), kind),
            pltpu.VMEM((2, PAD, model), kind),
            pltpu.VMEM((rounds,) + small, jnp.float32),
            pltpu.SemaphoreType.DMA,
            pltpu.SemaphoreType.DMA((2,)),
            pltpu.SemaphoreType.DMA((3,)),
            pltpu.SemaphoreType.DMA((3,)),
            pltpu.SemaphoreType.DMA((rounds,)),
            pltpu.SemaphoreType.DMA((rounds,)),
            *reduce_scratch(groups, count, rows, [inner] * 4 + [first_width // 2] * 2),
        ],
        compiler_params=pltpu.CompilerParams(
            collective_id=5, has_side_effects=True, vmem_limit_bytes=62 * 2**20
        ),
        name="backward_block",
    )(
        mixed_in, little, gate_pre, conv, head, gain, *kept, grad_branch, inputs, norm_gain,
        grad_hidden, grad_second, loss_row, w_first, grad_down, grad_up, grad_out,
    )


def third(width, weight):
    return 128 * max(1, round(width * weight / 128))


def norm_parts(field_in):
    scale = lax.rsqrt(jnp.mean(field_in * field_in, axis=-1, keepdims=True) + epsilon)
    return scale, field_in * scale


def norm_back(scale, unit, gain_vec, grad):
    scaled = grad * gain_vec
    return scale * (scaled - unit * jnp.mean(scaled * unit, axis=-1, keepdims=True))


def dense(left, right, dims):
    return lax.dot_general(left, right, (dims, ((), ())), preferred_element_type=jnp.float32)


def swiglu(gate_up):
    hidden_units = gate_up.shape[1] // 2
    return jax.nn.silu(gate_up[:, :hidden_units]) * gate_up[:, hidden_units:]


def on_device(
    tokens,
    target,
    valid,
    in_weight,
    small_weight,
    out_weight,
    ffn_in,
    ffn_out,
    gain_first,
    gain_second,
    gain_out,
    conv_weight,
    decay_log,
    decay_bias,
):
    count = lax.axis_size("seq")
    groups = lax.axis_size("dp")
    core = lax.axis_index("dp") % 2
    rows = in_weight.shape[0]
    length, model = tokens.shape[1], tokens.shape[2]
    both, padded = 2 * length, length + PAD
    heads = HEADS // 2
    keys, vals, inner = KEYS // 2, VALUES // 2, FF // 2
    mixed_width = 2 * keys + vals

    def mine(array, start, width):
        return lax.dynamic_slice_in_dim(array, start + core * width, width, array.ndim - 1)

    def qkv_half(array):
        parts = [mine(array, 0, keys), mine(array, KEYS, keys), mine(array, 2 * KEYS, vals)]
        return jnp.concatenate(parts, axis=1)

    small_half = [mine(small_weight, 0, heads), mine(small_weight, HEADS, heads)]
    spare = jnp.zeros((rows, 128 - 2 * heads), jnp.bfloat16)
    small_part = jnp.concatenate(small_half + [spare], axis=1)
    first_width = mixed_width + 128 + vals

    mask_own = valid[0].astype(jnp.float32)
    mask_rows = jnp.broadcast_to(mask_own[None, :], (8, length))
    own_conv = jnp.concatenate([qkv_half(conv_weight), jnp.zeros((8 - CONV, mixed_width))], axis=0)
    lanes = ((0, 0), (heads, 128 - 2 * heads))
    head = jnp.concatenate(
        [
            jnp.pad(-jnp.exp(mine(decay_log, 0, heads))[None], lanes),
            jnp.pad(mine(decay_bias, 0, heads)[None], lanes),
            jnp.zeros((6, 128), jnp.float32),
        ],
        axis=0,
    )
    gain_row = gain_out[None]
    (
        inputs, target_other, mask_other, mixed_in, little, gate_pre, branch, *kept,
        hidden, second, gate_up, active, w_first, w_out, w_up, w_down,
    ) = forward_block(
        tokens[0], target[0], mask_rows, gain_first[None], own_conv, head, gain_row,
        gain_second[None], in_weight, small_part, out_weight, ffn_in, ffn_out,
    )
    branch = branch.reshape(both, vals)
    w_first, w_out, w_up, w_down = (
        v.reshape(model, v.shape[2]) for v in (w_first, w_out, w_up, w_down)
    )

    def core_sum(part):
        pairs = [(group, group ^ 1) for group in range(groups)]
        got = lax.ppermute(part.astype(jnp.bfloat16), "dp", pairs)
        return part + jnp.concatenate([got[length:], got[:length]], axis=0).astype(jnp.float32)

    second_scale, second_unit = norm_parts(hidden)
    swiglu_pull = jax.vjp(swiglu, gate_up)[1]
    summed = hidden + core_sum(dense(active, w_down, ((1,), (1,))))
    mask = jnp.concatenate([mask_own, mask_other[0]])
    errors = summed - jnp.concatenate([target[0], target_other]).astype(jnp.float32)
    own_errors = errors[:length]
    loss_part = jnp.sum(mask_own * jnp.mean(own_errors * own_errors, axis=-1))

    grad_summed = mask[:, None] * errors
    grad_feed = grad_summed.astype(jnp.bfloat16)
    grad_active = dense(grad_feed, w_down, ((1,), (0,)))
    grad_down = dense(grad_feed, active, ((0,), (0,))).astype(jnp.bfloat16)
    grad_gate_up = swiglu_pull(grad_active)[0].astype(jnp.bfloat16)
    grad_up = dense(second, grad_gate_up, ((0,), (0,))).astype(jnp.bfloat16)
    grad_second = core_sum(dense(grad_gate_up, w_up, ((1,), (1,))))
    grad_gain_second = jnp.sum((grad_second * second_unit)[:length], axis=0)
    grad_hidden = grad_summed + norm_back(second_scale, second_unit, gain_second, grad_second)
    grad_attn = grad_hidden.astype(jnp.bfloat16)
    grad_out = dense(grad_attn, branch, ((0,), (0,))).astype(jnp.bfloat16)
    grad_branch = dense(grad_attn, w_out, ((1,), (0,))).reshape(2, length, vals)

    def by_place(array):
        return array.reshape(count // 2, 2, rows, array.shape[1])

    grad_up = by_place(grad_up)
    loss_row = jnp.concatenate(
        [loss_part[None], jnp.sum(mask_own)[None], jnp.zeros((126,), jnp.float32)]
    )[None]
    grad_tokens, small_sum, sum_down, sum_gate, sum_up, sum_out, sum_in, sum_small, unused = backward_block(
        mixed_in, little, gate_pre, own_conv, head, gain_row, kept, grad_branch,
        inputs, gain_first[None], grad_hidden[:length], grad_gain_second[None], loss_row, w_first,
        by_place(grad_down), grad_up, by_place(grad_out),
    )
    valid_count = jnp.maximum(small_sum[5, 257], 1.0)
    loss_value = small_sum[5, 256] / valid_count
    factor = length * groups * count / valid_count
    sum_small = jnp.concatenate(
        [
            sum_small[:, 0:heads],
            sum_small[:, 128 : 128 + heads],
            sum_small[:, heads : 2 * heads],
            sum_small[:, 128 + heads : 128 + 2 * heads],
        ],
        axis=1,
    )

    def scaled(array):
        return array.astype(jnp.float32) * factor

    return (
        summed[:length].astype(jnp.bfloat16)[None],
        loss_value,
        scaled(grad_tokens)[None],
        scaled(sum_in),
        scaled(sum_small),
        scaled(sum_out),
        scaled(jnp.concatenate([sum_gate, sum_up], axis=1)),
        scaled(sum_down),
        scaled(small_sum[4, :model]),
        scaled(small_sum[4, model : 2 * model]),
        scaled(small_sum[4, 2 * model : 2 * model + DV]),
        scaled(small_sum[:CONV]),
        scaled(small_sum[5, :HEADS]),
        scaled(small_sum[5, 128 : 128 + HEADS]),
    )


def solution(mesh):
    placed = (
        P("dp", "seq", None),
        P("dp", "seq", None),
        P("dp", "seq"),
        P("seq", None),
        P("seq", None),
        P("seq", None),
        P("seq", None),
        P("seq", None),
        P(),
        P(),
        P(),
        P(),
        P(),
        P(),
    )
    return jax.shard_map(
        on_device,
        mesh=mesh,
        in_specs=placed,
        out_specs=(
            P("dp", "seq", None),
            P(),
            P("dp", "seq", None),
            P("seq", None),
            P("seq", None),
            P("seq", None),
            P("seq", None),
            P("seq", None),
            P(),
            P(),
            P(),
            P(),
            P(),
            P(),
        ),
        check_vma=False,
    )
```
